256 devices in a mesh: gx: 8 (over z), gy: 4 (over x), gz: 8 (over y, core).
Axes of the slice: x: 4, y: 4, z: 8, core: 2. Of those that a mesh axis runs over, the one named last changes fastest.
Arguments:
- vectors: float32 [2, 3, 32, 32, 64, 128], P(None, None, 'gx', 'gy', 'gz'), may hold values from -6 to 6
- links: float32 [3, 2, 3, 3, 32, 32, 64], P(None, None, None, None, 'gx', 'gy', 'gz'), may hold values from -1 to 1, as said below
Outputs:
- basis: float32 [2, 3, 32, 32, 64, 128], P(None, None, 'gx', 'gy', 'gz')
- ritz: float32 [2, 128, 128], replicated
The draws below stay inside these ranges and needn't reach their ends.
Inputs may be any that keep to these rules, and one draw needn't show every extreme that they name: `links`: each link is a special unitary 3 x 3 complex matrix.
All inputs are finite; a program needn't handle non-finite values.
Results may differ from the reference program's by a relative error of at most 0.0003.
Values sent between devices are 32-bit elements; how exact they have to be, the bound alone decides.
A program may use at most 128 MiB of HBM per device.

```python
import jax
import jax.numpy as jnp
from jax import lax

NV = 128
NS_STEPS = 10
NX = 32
NY = 32
NZ = 64


def draw_links(key, part):
    key = jax.random.fold_in(key, 7)
    shape = (3, 2, 2, 3, NX, NY, NZ)
    raw = jax.random.normal(key, shape, jnp.float32)
    first = raw[:, 0]
    second = raw[:, 1]
    first = first / jnp.sqrt(jnp.sum(first * first, axis=(1, 2), keepdims=True))
    proj_re = jnp.sum(first[:, 0] * second[:, 0] + first[:, 1] * second[:, 1], axis=1, keepdims=True)
    proj_im = jnp.sum(first[:, 0] * second[:, 1] - first[:, 1] * second[:, 0], axis=1, keepdims=True)
    sec_re = second[:, 0] - (proj_re * first[:, 0] - proj_im * first[:, 1])
    sec_im = second[:, 1] - (proj_re * first[:, 1] + proj_im * first[:, 0])
    second = jnp.stack([sec_re, sec_im], 1)
    second = second / jnp.sqrt(jnp.sum(second * second, axis=(1, 2), keepdims=True))
    third_re = []
    third_im = []
    for k in range(3):
        i = (k + 1) % 3
        j = (k + 2) % 3
        re_part = first[:, 0, i] * second[:, 0, j] - first[:, 1, i] * second[:, 1, j] - (first[:, 0, j] * second[:, 0, i] - first[:, 1, j] * second[:, 1, i])
        im_part = first[:, 0, i] * second[:, 1, j] + first[:, 1, i] * second[:, 0, j] - (first[:, 0, j] * second[:, 1, i] + first[:, 1, j] * second[:, 0, i])
        third_re.append(re_part)
        third_im.append(-im_part)
    third = jnp.stack([jnp.stack(third_re, 1), jnp.stack(third_im, 1)], 1)
    return jnp.stack([first, second, third], 2).astype(jnp.float32)


def steps_of(own_key, shape, cuts, least, high):
    def one(position, parts):
        heights = jax.random.uniform(jax.random.fold_in(jax.random.fold_in(own_key, 6), position), (parts,), jnp.float32, least / len(cuts), high / len(cuts))
        return jnp.repeat(jnp.exp(heights), shape[position] // parts).reshape((-1,) + (1,) * (len(shape) - position - 1))

    loudness = one(*cuts[0])
    for cut in cuts[1:]:
        loudness = loudness * one(*cut)
    return loudness


def bell_draw(own_key, extent, spread, bound, split=(), kind=jnp.bfloat16):
    entries = jax.random.normal(own_key, extent, jnp.float32) * spread
    if len(split) > 0:
        entries = steps_of(own_key, extent, split, -0.22, 0.18) * entries
    return jnp.clip(entries, min=-bound, max=bound).astype(kind)


def setup_inputs(seed: int = 0) -> dict:
    keys = jax.random.split(jax.random.key(seed), 3)
    vectors = bell_draw(keys[0], (2, 3, NX, NY, NZ, NV), 1.0, 6.0, ((2, 8), (3, 4), (4, 8)), jnp.float32)
    links = draw_links(jax.random.fold_in(keys[2], 71), 0)
    return dict(vectors=vectors, links=links)


filter_low = 1.0
filter_high = 12.0

def colour_mul(link, field, dagger):
    link_re = link[0]
    link_im = link[1]
    if dagger:
        link_re = jnp.swapaxes(link_re, 0, 1)
        link_im = -jnp.swapaxes(link_im, 0, 1)
    out_re = 0.0
    out_im = 0.0
    for col in range(3):
        part_re = link_re[:, col][..., None]
        part_im = link_im[:, col][..., None]
        out_re = out_re + part_re * field[0, col] - part_im * field[1, col]
        out_im = out_im + part_re * field[1, col] + part_im * field[0, col]
    return jnp.stack([out_re, out_im])

def laplace(field, links):
    total = 6.0 * field
    for mu in range(3):
        ahead = jnp.roll(field, -1, 2 + mu)
        behind = jnp.roll(field, 1, 2 + mu)
        back_link = jnp.roll(links[mu], 1, 3 + mu)
        total = total - (colour_mul(links[mu], ahead, False) + colour_mul(back_link, behind, True))
    return total

def mapped(field, links):
    return (2.0 * laplace(field, links) - (filter_high + filter_low) * field) / (filter_high - filter_low)

def hdot(left, right):
    return lax.dot_general(left, right, (((0,), (0,)), ((), ())), precision=lax.Precision.HIGHEST, preferred_element_type=jnp.float32)

def gram_parts(first, second):
    width = first.shape[-1]
    a_re = first[0].reshape(-1, width)
    a_im = first[1].reshape(-1, width)
    b_re = second[0].reshape(-1, width)
    b_im = second[1].reshape(-1, width)
    return (hdot(a_re, b_re) + hdot(a_im, b_im), hdot(a_re, b_im) - hdot(a_im, b_re))

def inverse_root(gram_re, gram_im):
    width = gram_re.shape[0]
    whole = jnp.concatenate([jnp.concatenate([gram_re, -gram_im], 1), jnp.concatenate([gram_im, gram_re], 1)], 0)
    scale = jnp.sqrt(jnp.sum(whole * whole))
    iterate = whole / scale
    eye = jnp.eye(2 * width, dtype=jnp.float32)
    result = eye
    for step in range(NS_STEPS):
        factor = 1.5 * eye - 0.5 * jnp.dot(result, iterate, precision=lax.Precision.HIGHEST)
        iterate = jnp.dot(iterate, factor, precision=lax.Precision.HIGHEST)
        result = jnp.dot(factor, result, precision=lax.Precision.HIGHEST)
    result = result / jnp.sqrt(scale)
    return (result[:width, :width], result[width:, :width])

def combine(field, root_re, root_im):
    width = field.shape[-1]
    f_re = field[0].reshape(-1, width)
    f_im = field[1].reshape(-1, width)
    high = lax.Precision.HIGHEST
    out_re = jnp.dot(f_re, root_re, precision=high) - jnp.dot(f_im, root_im, precision=high)
    out_im = jnp.dot(f_re, root_im, precision=high) + jnp.dot(f_im, root_re, precision=high)
    return jnp.stack([out_re.reshape(field.shape[1:]), out_im.reshape(field.shape[1:])])

def reference(vectors, links):
    sites_all = float(NX * NY * NZ)
    previous = vectors
    current = mapped(vectors, links)
    for step in range(3):
        following = 2.0 * mapped(current, links) - previous
        previous = current
        current = following
    gram_re, gram_im = gram_parts(current, current)
    root_re, root_im = inverse_root(gram_re / sites_all, gram_im / sites_all)
    basis = combine(current, root_re, root_im)
    ritz_re, ritz_im = gram_parts(basis, laplace(basis, links))
    return (basis, jnp.stack([ritz_re, ritz_im]) / sites_all)
```

```python
import jax
import jax.numpy as jnp
from jax import lax
from jax.experimental import pallas as pl
from jax.experimental.pallas import tpu as pltpu
from jax.sharding import PartitionSpec as P

NS_STEPS = 10


filter_low = 1.0
filter_high = 12.0


def extended(cells, sides, width):
    for axis, dim in sides:
        count = lax.axis_size(axis)
        head = lax.slice_in_dim(cells, 0, width, axis=dim)
        tail = lax.slice_in_dim(cells, cells.shape[dim] - width, cells.shape[dim], axis=dim)
        cells = jnp.concatenate(
            [
                lax.ppermute(tail, axis, [(i, (i + 1) % count) for i in range(count)]),
                cells,
                lax.ppermute(head, axis, [((i + 1) % count, i) for i in range(count)]),
            ],
            axis=dim,
        )
    return cells


def shifted(value, axis, steps):
    count = lax.axis_size(axis)
    pairs = [(source, (source + steps) % count) for source in range(count)]
    return lax.ppermute(value, axis, pairs)


def colour_mul(link, field, dagger):
    link_re = link[0]
    link_im = link[1]
    if dagger:
        link_re = jnp.swapaxes(link_re, 0, 1)
        link_im = -jnp.swapaxes(link_im, 0, 1)
    out_re = 0.0
    out_im = 0.0
    for col in range(3):
        part_re = link_re[:, col][..., None]
        part_im = link_im[:, col][..., None]
        out_re = out_re + part_re * field[0, col] - part_im * field[1, col]
        out_im = out_im + part_re * field[1, col] + part_im * field[0, col]
    return jnp.stack([out_re, out_im])


def crop(field, depth):
    return field[
        :,
        :,
        depth : field.shape[2] - depth,
        depth : field.shape[3] - depth,
        depth : field.shape[4] - depth,
    ]


def laplace_padded(field, link_wide):
    extent = (link_wide.shape[4] - 4, link_wide.shape[5] - 4, link_wide.shape[6] - 4)
    outer = (field.shape[2] - extent[0]) // 2 - 1
    sizes = (extent[0] + 2 * outer, extent[1] + 2 * outer, extent[2] + 2 * outer)

    def field_part(offset):
        lo = [1 + offset[d] for d in range(3)]
        return field[
            :, :, lo[0] : lo[0] + sizes[0], lo[1] : lo[1] + sizes[1], lo[2] : lo[2] + sizes[2]
        ]

    def link_part(mu, offset):
        lo = [2 - outer + offset[d] for d in range(3)]
        return link_wide[mu][
            :, :, :, lo[0] : lo[0] + sizes[0], lo[1] : lo[1] + sizes[1], lo[2] : lo[2] + sizes[2]
        ]

    total = 6.0 * field_part((0, 0, 0))
    for mu in range(3):
        ahead = tuple((1 if d == mu else 0 for d in range(3)))
        behind = tuple((-1 if d == mu else 0 for d in range(3)))
        total = total - (
            colour_mul(link_part(mu, (0, 0, 0)), field_part(ahead), False)
            + colour_mul(link_part(mu, behind), field_part(behind), True)
        )
    return total


def mapped_padded(field, link_wide):
    return (
        2.0 * laplace_padded(field, link_wide) - (filter_high + filter_low) * crop(field, 1)
    ) / (filter_high - filter_low)


def laplace_whole(field, link_wide):
    padded = extended(field, (("gx", 2), ("gy", 3), ("gz", 4)), 1)
    return laplace_padded(padded, link_wide)


def hdot(left, right):
    return lax.dot_general(
        left,
        right,
        (((0,), (0,)), ((), ())),
        precision=lax.Precision.HIGHEST,
        preferred_element_type=jnp.float32,
    )


def gram_parts(first, second):
    width = first.shape[-1]
    a_re = first[0].reshape(-1, width)
    a_im = first[1].reshape(-1, width)
    b_re = second[0].reshape(-1, width)
    b_im = second[1].reshape(-1, width)
    return (hdot(a_re, b_re) + hdot(a_im, b_im), hdot(a_re, b_im) - hdot(a_im, b_re))


def inverse_root(gram_re, gram_im):
    width = gram_re.shape[0]
    whole = jnp.concatenate(
        [jnp.concatenate([gram_re, -gram_im], 1), jnp.concatenate([gram_im, gram_re], 1)], 0
    )
    scale = jnp.sqrt(jnp.sum(whole * whole))
    iterate = whole / scale
    eye = jnp.eye(2 * width, dtype=jnp.float32)
    result = eye
    for step in range(NS_STEPS):
        factor = 1.5 * eye - 0.5 * jnp.dot(result, iterate, precision=lax.Precision.HIGHEST)
        iterate = jnp.dot(iterate, factor, precision=lax.Precision.HIGHEST)
        result = jnp.dot(factor, result, precision=lax.Precision.HIGHEST)
    result = result / jnp.sqrt(scale)
    return (result[:width, :width], result[width:, :width])


def combine(field, root_re, root_im):
    width = field.shape[-1]
    f_re = field[0].reshape(-1, width)
    f_im = field[1].reshape(-1, width)
    high = lax.Precision.HIGHEST
    out_re = jnp.dot(f_re, root_re, precision=high) - jnp.dot(f_im, root_im, precision=high)
    out_im = jnp.dot(f_re, root_im, precision=high) + jnp.dot(f_im, root_re, precision=high)
    return jnp.stack([out_re.reshape(field.shape[1:]), out_im.reshape(field.shape[1:])])


def upper_face(link_one, mu):
    count = link_one.shape[3 + mu]
    return lax.slice_in_dim(link_one, count - 1, count, axis=3 + mu)


def widen_links(link_one, face, mu):
    joined = jnp.concatenate([face, link_one], 3 + mu)
    others = [(0, 0)] * 3 + [(0, 0) if d == mu else (2, 2) for d in range(3)]
    joined = jnp.pad(joined, others)
    along = [(0, 0)] * 3 + [(1, 2) if d == mu else (0, 0) for d in range(3)]
    return jnp.pad(joined, along)


MESH = pl.DeviceIdType.MESH


def places():
    gx = lax.axis_index("gx")
    gy = lax.axis_index("gy")
    gz = lax.axis_index("gz")
    return gx, gy, gz // 2, gz % 2


def plane_mate(step):
    gx, gy, row, core = places()
    other_y = (gy + step // 4) % 4
    other_row = (row + step % 4) % 4
    return (gx, other_y, other_row * 2 + core), other_y * 4 + other_row


def line_mate(step):
    gx, gy, row, core = places()
    other_x = (gx + step // 2) % 8
    other_core = (core + step % 2) % 2
    return (other_x, gy, row * 2 + other_core)


def reduce_kernel(part_ref, out_ref, first, second, sems):
    gx, gy, row, core = places()
    mine = gy * 4 + row
    line = gx * 2 + core
    barrier = pltpu.get_barrier_semaphore()

    def greet(step, carry):
        device, _ = plane_mate(step)
        pl.semaphore_signal(barrier, inc=1, device_id=device, device_id_type=MESH)
        pl.semaphore_signal(barrier, inc=1, device_id=line_mate(step), device_id_type=MESH)
        return carry

    lax.fori_loop(1, 16, greet, 0)
    pl.semaphore_wait(barrier, 30)

    def scatter(step):
        device, index = plane_mate(step)
        return pltpu.make_async_remote_copy(
            src_ref=part_ref.at[index],
            dst_ref=first.at[step],
            send_sem=sems.at[0, step],
            recv_sem=sems.at[1, step],
            device_id=device,
            device_id_type=MESH,
        )

    def across(step):
        return pltpu.make_async_remote_copy(
            src_ref=second.at[line],
            dst_ref=second.at[line],
            send_sem=sems.at[2, step],
            recv_sem=sems.at[3, step],
            device_id=line_mate(step),
            device_id_type=MESH,
        )

    def gather(step):
        device, _ = plane_mate(step)
        return pltpu.make_async_remote_copy(
            src_ref=out_ref.at[mine],
            dst_ref=out_ref.at[mine],
            send_sem=sems.at[4, step],
            recv_sem=sems.at[5, step],
            device_id=device,
            device_id_type=MESH,
        )

    def start_all(make):
        def body(step, carry):
            make(step).start()
            return carry

        lax.fori_loop(1, 16, body, 0)

    def wait_all(make):
        def body(step, carry):
            make(step).wait()
            return carry

        lax.fori_loop(1, 16, body, 0)

    start_all(scatter)
    first[0] = part_ref[mine]
    wait_all(scatter)
    total = first[0]
    for step in range(1, 16):
        total = total + first[step]
    second[line] = total
    start_all(across)
    wait_all(across)
    total = second[0]
    for step in range(1, 16):
        total = total + second[step]
    out_ref[mine] = total
    start_all(gather)
    wait_all(gather)


def reduced(parts):
    return pl.pallas_call(
        reduce_kernel,
        out_shape=jax.ShapeDtypeStruct(parts.shape, jnp.float32),
        in_specs=[pl.BlockSpec(memory_space=pltpu.VMEM)],
        out_specs=pl.BlockSpec(memory_space=pltpu.VMEM),
        scratch_shapes=[
            pltpu.VMEM(parts.shape, jnp.float32),
            pltpu.VMEM(parts.shape, jnp.float32),
            pltpu.SemaphoreType.DMA((6, 16)),
        ],
        compiler_params=pltpu.CompilerParams(collective_id=0, has_side_effects=True),
    )(parts)


def lower_mask(order, strict):
    row = lax.broadcasted_iota(jnp.int32, (order, order), 0)
    column = lax.broadcasted_iota(jnp.int32, (order, order), 1)
    return row > column if strict else row >= column


def packed(re_part, im_part):
    return jnp.where(lower_mask(re_part.shape[0], False), re_part, im_part)


def unpacked(both):
    zero = jnp.zeros_like(both)
    low = jnp.where(lower_mask(both.shape[0], False), both, zero)
    strict = jnp.where(lower_mask(both.shape[0], True), both, zero)
    high = both - low
    return low + strict.T, high - high.T


def shards(vectors, links):
    sites_all = float(
        vectors.shape[2]
        * lax.axis_size("gx")
        * vectors.shape[3]
        * lax.axis_size("gy")
        * vectors.shape[4]
        * lax.axis_size("gz")
    )
    face_x = shifted(upper_face(links[0], 0), "gx", 1)
    face_y = shifted(upper_face(links[1], 1), "gy", 1)
    face_z = shifted(upper_face(links[2], 2), "gz", 1)
    link_wide = jnp.stack(
        [
            widen_links(links[0], face_x, 0),
            widen_links(links[1], face_y, 1),
            widen_links(links[2], face_z, 2),
        ]
    )

    def one_pass(field):
        padded = extended(field, (("gx", 2), ("gy", 3), ("gz", 4)), 1)
        return mapped_padded(padded, link_wide)

    previous = vectors
    current = one_pass(vectors)
    for step in range(3):
        following = 2.0 * one_pass(current) - previous
        previous = current
        current = following
    gram_part = packed(*gram_parts(current, current))
    proj_part = packed(*gram_parts(current, laplace_whole(current, link_wide)))
    width = gram_part.shape[0]
    parts = jnp.stack([gram_part, proj_part]).reshape(2, 16, width // 16, width)
    sums = reduced(jnp.swapaxes(parts, 0, 1)) / sites_all
    sums = jnp.swapaxes(sums, 0, 1).reshape(2, width, width)
    gram_re, gram_im = unpacked(sums[0])
    proj_re, proj_im = unpacked(sums[1])
    root_re, root_im = inverse_root(gram_re, gram_im)
    basis = combine(current, root_re, root_im)
    half = combine(jnp.stack([proj_re, proj_im]), root_re, root_im)
    left = jnp.stack([root_re, root_im])
    ritz_re, ritz_im = gram_parts(left, half)
    return (basis, jnp.stack([ritz_re, ritz_im]))


def solution(mesh):
    return jax.shard_map(
        shards,
        mesh=mesh,
        in_specs=(
            P(None, None, "gx", "gy", "gz", None),
            P(None, None, None, None, "gx", "gy", "gz"),
        ),
        out_specs=(P(None, None, "gx", "gy", "gz", None), P()),
        check_vma=False,
    )
```

```python
import jax
import jax.numpy as jnp
from jax import lax
from jax.experimental import pallas as pl
from jax.experimental.pallas import tpu as pltpu
from jax.sharding import PartitionSpec as P

NS_STEPS = 10
FILTER_STEPS = 4

filter_low = 1.0
filter_high = 12.0

MESH = pl.DeviceIdType.MESH
HOP = -4.0 / (filter_high - filter_low)
SELF = 2.0 * (12.0 - filter_high - filter_low) / (filter_high - filter_low)
SUBLANES = ((0,), (0,))
f32 = jnp.float32
bf16 = jnp.bfloat16


def places():
    gx = lax.axis_index("gx")
    gy = lax.axis_index("gy")
    gz = lax.axis_index("gz")
    return gx, gy, gz // 2, gz % 2


def plane_mate(step):
    gx, gy, row, core = places()
    other_y = (gy + step // 4) % 4
    other_row = (row + step % 4) % 4
    return (gx, other_y, other_row * 2 + core), other_y * 4 + other_row


def line_mate(step):
    gx, gy, row, core = places()
    other_x = (gx + step // 2) % 8
    other_core = (core + step % 2) % 2
    return (other_x, gy, row * 2 + other_core)


def neighbour(axis, sign):
    place = [lax.axis_index("gx"), lax.axis_index("gy"), lax.axis_index("gz")]
    count = (8, 4, 8)[axis]
    place[axis] = (place[axis] + sign + count) % count
    return tuple(place)


def forward(link, field):
    out = [[None] * 3, [None] * 3]
    for r in range(3):
        re = im = None
        for c in range(3):
            ur, ui = link[0][r][c], link[1][r][c]
            vr, vi = field[0][c], field[1][c]
            re_term = ur * vr - ui * vi
            im_term = ur * vi + ui * vr
            re = re_term if re is None else re + re_term
            im = im_term if im is None else im + im_term
        out[0][r], out[1][r] = re, im
    return out


def backward(link, field):
    out = [[None] * 3, [None] * 3]
    for r in range(3):
        re = im = None
        for c in range(3):
            ur, ui = link[0][c][r], link[1][c][r]
            vr, vi = field[0][c], field[1][c]
            re_term = ur * vr + ui * vi
            im_term = ur * vi - ui * vr
            re = re_term if re is None else re + re_term
            im = im_term if im is None else im + im_term
        out[0][r], out[1][r] = re, im
    return out


def both(fn):
    return [[fn(p, c) for c in range(3)] for p in range(2)]


def plus(left, right):
    return both(lambda p, c: left[p][c] + right[p][c])


def split(value):
    high = value.astype(bf16)
    return high, (value - high.astype(f32)).astype(bf16)


def mul(left, right, dims=((1,), (0,))):
    return lax.dot_general(left, right, (dims, ((), ())), preferred_element_type=f32)


def whole(columns):
    half = columns.shape[0] // 2
    return jnp.concatenate(
        [columns, jnp.concatenate([-columns[half:], columns[:half]], 0)], 1
    )


def halves(columns):
    high, low = split(columns)
    return jnp.concatenate([high, low], 1)


def product(left_split, right_halves):
    width = right_halves.shape[1] // 2
    left = jnp.concatenate(left_split, 0)
    rows = left_split[0].shape[0]
    out = mul(left, right_halves)
    out = out[:, :width] + out[:, width:]
    return out[:rows] + out[rows:]


def lower_mask(order, strict):
    row = lax.broadcasted_iota(jnp.int32, (order, order), 0)
    column = lax.broadcasted_iota(jnp.int32, (order, order), 1)
    return row > column if strict else row >= column


def packed(re_part, im_part):
    return jnp.where(lower_mask(re_part.shape[0], False), re_part, im_part)


def unpacked(mixed):
    zero = jnp.zeros_like(mixed)
    low = jnp.where(lower_mask(mixed.shape[0], False), mixed, zero)
    strict = jnp.where(lower_mask(mixed.shape[0], True), mixed, zero)
    high = mixed - low
    return jnp.concatenate([low + strict.T, high - high.T], 0)


def side_by_side(ref, *index):
    half = [ref[(*index, p)].reshape(-1, ref.shape[-1]) for p in range(2)]
    return jnp.concatenate(half, 1)


def whole_kernel(
    sites_all,
    vec_ref,
    link_ref,
    basis_ref,
    ritz_ref,
    fields,
    hops,
    wide,
    edge,
    send_x,
    send_y,
    send_z,
    low_z,
    ahead_x,
    ahead_y,
    ahead_z,
    behind_x,
    behind_y,
    behind_z,
    part,
    first,
    second,
    summed,
    face_sems,
    sum_sems,
):
    gx, gy, row, core = places()
    mine = gy * 4 + row
    line = gx * 2 + core

    barrier = pltpu.get_barrier_semaphore()

    def greet(step, carry):
        device, _ = plane_mate(step)
        pl.semaphore_signal(barrier, inc=1, device_id=device, device_id_type=MESH)
        pl.semaphore_signal(barrier, inc=1, device_id=line_mate(step), device_id_type=MESH)
        return carry

    for axis in range(3):
        for sign in (-1, 1):
            pl.semaphore_signal(
                barrier, inc=1, device_id=neighbour(axis, sign), device_id_type=MESH
            )
    lax.fori_loop(1, 16, greet, 0)

    keep = (lax.broadcasted_iota(jnp.int32, (8, 128), 0) < 7).astype(f32)

    def widen(entry, carry):
        for mu in range(3):
            for x in range(4):
                tile = link_ref[mu, entry, x] * HOP
                turned = tile.T
                for y in range(8):
                    value = jnp.broadcast_to(turned[:, y : y + 1], (8, 128))
                    if mu == 2:
                        value = value * keep
                    wide[mu, entry, x, pl.ds(8 * y, 8)] = value
                if mu == 1:
                    wide[mu, entry, x, pl.ds(64, 8)] = jnp.zeros((8, 128), f32)
                if mu == 2:
                    edge[entry, x] = jnp.broadcast_to(tile[:, 7:8], (8, 128))
        return carry

    lax.fori_loop(0, 18, widen, 0)

    def halve(x, carry):
        for p in range(2):
            for c in range(3):
                fields[0, p, c, x] = vec_ref[p, c, x] * 0.5
        return carry

    lax.fori_loop(0, 4, halve, 0)

    def tile_link(mu, x, slot):
        rows = pl.ds(pl.multiple_of(8 * slot, 8), 8)
        return [
            [[wide[mu, p * 9 + r * 3 + c, x, rows] for c in range(3)] for r in range(3)]
            for p in range(2)
        ]

    def edge_link(x):
        return [
            [[edge[p * 9 + r * 3 + c, x] for c in range(3)] for r in range(3)]
            for p in range(2)
        ]

    def tile(k, x, y):
        rows = pl.ds(pl.multiple_of(8 * y, 8), 8)
        return both(lambda p, c: fields[k, p, c, x, rows])

    def strided(k, x, z):
        return both(lambda p, c: fields[k, p, c, x, pl.ds(z, 8, stride=8)])

    def low_copies(k):
        pairs = (
            (0, fields.at[k, :, :, 0], ahead_x.at[k]),
            (1, fields.at[k, :, :, :, pl.ds(0, 8)], ahead_y.at[k]),
            (2, low_z.at[k], ahead_z.at[k]),
        )
        return [
            pltpu.make_async_remote_copy(
                src_ref=source,
                dst_ref=target,
                send_sem=face_sems.at[0, k, axis],
                recv_sem=face_sems.at[1, k, axis],
                device_id=neighbour(axis, -1),
                device_id_type=MESH,
            )
            for axis, source, target in pairs
        ]

    def high_copies(k):
        pairs = (
            (0, send_x.at[k], behind_x.at[k]),
            (1, send_y.at[k], behind_y.at[k]),
            (2, send_z.at[k], behind_z.at[k]),
        )
        return [
            pltpu.make_async_remote_copy(
                src_ref=source,
                dst_ref=target,
                send_sem=face_sems.at[2, k, axis],
                recv_sem=face_sems.at[3, k, axis],
                device_id=neighbour(axis, 1),
                device_id_type=MESH,
            )
            for axis, source, target in pairs
        ]

    def make_low_z(k):
        def body(x, carry):
            value = strided(k, x, 0)
            for p in range(2):
                for c in range(3):
                    low_z[k, p, c, x] = value[p][c]
            return carry

        lax.fori_loop(0, 4, body, 0)

    def make_high_x(k):
        def body(y, carry):
            rows = pl.ds(pl.multiple_of(8 * y, 8), 8)
            value = backward(tile_link(0, 3, y), tile(k, 3, y))
            for p in range(2):
                for c in range(3):
                    send_x[k, p, c, rows] = value[p][c]
            return carry

        lax.fori_loop(0, 8, body, 0)

    def make_high_yz(k):
        def body(x, carry):
            value = backward(tile_link(1, x, 7), tile(k, x, 7))
            other = backward(edge_link(x), strided(k, x, 7))
            for p in range(2):
                for c in range(3):
                    send_y[k, p, c, x] = value[p][c]
                    send_z[k, p, c, x] = other[p][c]
            return carry

        lax.fori_loop(0, 4, body, 0)

    def local_pass(k):
        again = jnp.where(k == 0, 0.0, jnp.where(k == 1, 2.0, 1.0)).astype(f32)
        before = jnp.maximum(k - 1, 0)

        def body(y, carry):
            rows = pl.ds(pl.multiple_of(8 * y, 8), 8)
            up = jnp.minimum(y + 1, 7)
            down = jnp.maximum(y - 1, 0)
            up_slot = jnp.where(y == 7, 8, y)
            down_slot = jnp.where(y == 0, 8, y - 1)
            for x in range(4):
                here = tile(k, x, y)
                old = tile(before, x, y)
                acc = both(lambda p, c: SELF * here[p][c] - again * old[p][c])
                link = tile_link(2, x, y)
                rolled = both(lambda p, c: pltpu.roll(here[p][c], 7, 0))
                acc = plus(acc, forward(link, rolled))
                back = backward(link, here)
                acc = plus(acc, both(lambda p, c: pltpu.roll(back[p][c], 1, 0)))
                if x < 3:
                    acc = plus(acc, forward(tile_link(0, x, y), tile(k, x + 1, y)))
                if x > 0:
                    acc = plus(acc, backward(tile_link(0, x - 1, y), tile(k, x - 1, y)))
                acc = plus(acc, forward(tile_link(1, x, up_slot), tile(k, x, up)))
                acc = plus(acc, backward(tile_link(1, x, down_slot), tile(k, x, down)))
                for p in range(2):
                    for c in range(3):
                        fields[k + 1, p, c, x, rows] = acc[p][c]
            return carry

        lax.fori_loop(0, 8, body, 0)

    def forward_pass(k):
        def body(y, carry):
            rows = pl.ds(pl.multiple_of(8 * y, 8), 8)
            up = jnp.minimum(y + 1, 7)
            up_slot = jnp.where(y == 7, 8, y)
            for x in range(4):
                here = tile(k, x, y)
                rolled = both(lambda p, c: pltpu.roll(here[p][c], 7, 0))
                acc = forward(tile_link(2, x, y), rolled)
                if x < 3:
                    acc = plus(acc, forward(tile_link(0, x, y), tile(k, x + 1, y)))
                acc = plus(acc, forward(tile_link(1, x, up_slot), tile(k, x, up)))
                for p in range(2):
                    for c in range(3):
                        hops[p, c, x, rows] = acc[p][c]
            return carry

        lax.fori_loop(0, 8, body, 0)

    def add_yz(target, index, k, with_behind):
        def body(x, carry):
            value = forward(
                tile_link(1, x, 7), both(lambda p, c: ahead_y[k, p, c, x])
            )
            other = forward(edge_link(x), both(lambda p, c: ahead_z[k, p, c, x]))
            last = pl.ds(56, 8)
            top = pl.ds(7, 8, stride=8)
            bottom = pl.ds(0, 8, stride=8)
            for p in range(2):
                for c in range(3):
                    at = (*index, p, c, x)
                    target[(*at, last)] = target[(*at, last)] + value[p][c]
                    target[(*at, top)] = target[(*at, top)] + other[p][c]
                    if with_behind:
                        head = pl.ds(0, 8)
                        target[(*at, head)] = target[(*at, head)] + behind_y[k, p, c, x]
                        target[(*at, bottom)] = target[(*at, bottom)] + behind_z[k, p, c, x]
            return carry

        lax.fori_loop(0, 4, body, 0)

    def add_x(target, index, k, with_behind):
        def body(y, carry):
            rows = pl.ds(pl.multiple_of(8 * y, 8), 8)
            value = forward(
                tile_link(0, 3, y), both(lambda p, c: ahead_x[k, p, c, rows])
            )
            for p in range(2):
                for c in range(3):
                    at = (*index, p, c, 3, rows)
                    target[at] = target[at] + value[p][c]
                    if with_behind:
                        at = (*index, p, c, 0, rows)
                        target[at] = target[at] + behind_x[k, p, c, rows]
            return carry

        lax.fori_loop(0, 8, body, 0)

    def scatter(j, step):
        device, index = plane_mate(step)
        return pltpu.make_async_remote_copy(
            src_ref=part.at[j, index],
            dst_ref=first.at[j, step],
            send_sem=sum_sems.at[j, 0, step],
            recv_sem=sum_sems.at[j, 1, step],
            device_id=device,
            device_id_type=MESH,
        )

    def across(j, step):
        return pltpu.make_async_remote_copy(
            src_ref=second.at[j, line],
            dst_ref=second.at[j, line],
            send_sem=sum_sems.at[j, 2, step],
            recv_sem=sum_sems.at[j, 3, step],
            device_id=line_mate(step),
            device_id_type=MESH,
        )

    def gather(j, step):
        device, _ = plane_mate(step)
        return pltpu.make_async_remote_copy(
            src_ref=summed.at[j, mine],
            dst_ref=summed.at[j, mine],
            send_sem=sum_sems.at[j, 4, step],
            recv_sem=sum_sems.at[j, 5, step],
            device_id=device,
            device_id_type=MESH,
        )

    def each(fn):
        def body(step, carry):
            fn(step)
            return carry

        lax.fori_loop(1, 16, body, 0)

    def start_all(make, j):
        each(lambda step: make(j, step).start())

    def wait_all(make, j):
        each(lambda step: make(j, step).wait())

    def sum_begin(j, value):
        for piece in range(16):
            part[j, piece] = value[8 * piece : 8 * piece + 8]
        start_all(scatter, j)

    def sum_middle(j):
        first[j, 0] = part[j, mine]
        wait_all(scatter, j)
        total = first[j, 0]
        for step in range(1, 16):
            total = total + first[j, step]
        second[j, line] = total
        start_all(across, j)

    def sum_last(j):
        wait_all(across, j)
        total = second[j, 0]
        for step in range(1, 16):
            total = total + second[j, step]
        summed[j, mine] = total
        start_all(gather, j)

    def sum_end(j):
        wait_all(gather, j)
        return summed[j].reshape(128, 128)

    def prepare(k):
        make_high_x(k)
        make_high_yz(k)
        make_low_z(k)

    def send(k):
        for low, high in zip(low_copies(k), high_copies(k)):
            low.start()
            high.start()

    prepare(0)
    pl.semaphore_wait(barrier, 36)
    send(0)

    def filter_step(k, carry):
        local_pass(k)
        low = low_copies(k)
        high = high_copies(k)
        for axis in (2, 1):
            low[axis].wait()
            high[axis].wait()
        add_yz(fields, (k + 1,), k, True)
        low[0].wait()
        high[0].wait()
        add_x(fields, (k + 1,), k, True)

        @pl.when(k < FILTER_STEPS - 1)
        def _():
            prepare(k + 1)
            send(k + 1)

        return carry

    lax.fori_loop(0, FILTER_STEPS, filter_step, 0)

    last = FILTER_STEPS
    make_low_z(last)
    for copy in low_copies(last):
        copy.start()

    high, low = split(side_by_side(fields, last))
    gram = mul(high, high, SUBLANES)
    cross = mul(high, low, SUBLANES)
    gram = gram + (cross + cross.T)
    half = gram.shape[0] // 2
    sum_begin(
        0,
        packed(
            gram[:half, :half] + gram[half:, half:],
            gram[:half, half:] - gram[half:, :half],
        ),
    )

    forward_pass(last)
    low_faces = low_copies(last)
    for axis in (2, 1):
        low_faces[axis].wait()
    add_yz(hops, (), last, False)
    low_faces[0].wait()
    add_x(hops, (), last, False)
    sum_middle(0)
    hop_high, hop_low = split(side_by_side(hops))
    proj = mul(high, hop_high, SUBLANES)
    proj = proj + mul(high, hop_low, SUBLANES)
    proj = proj + mul(low, hop_high, SUBLANES)
    proj_re = proj[:half, :half] + proj[half:, half:]
    proj_im = proj[:half, half:] - proj[half:, :half]
    sum_begin(1, packed(proj_re + proj_re.T, proj_im - proj_im.T))
    sum_last(0)
    sum_middle(1)
    gram_sum = unpacked(sum_end(0)) / sites_all
    sum_last(1)

    scale = jnp.sqrt(2.0 * jnp.sum(gram_sum * gram_sum, keepdims=True))
    eye = (
        lax.broadcasted_iota(jnp.int32, (2 * half, half), 0)
        == lax.broadcasted_iota(jnp.int32, (2 * half, half), 1)
    ).astype(f32)
    iterate = gram_sum / scale
    factor = 1.5 * eye - 0.5 * iterate
    iterate = product(split(whole(iterate)), halves(factor))
    result = factor

    def newton(step, carry):
        iterate, result = carry
        result_split = split(whole(result))
        factor = 1.5 * eye - 0.5 * product(result_split, halves(iterate))
        right = halves(factor)
        return (product(split(whole(iterate)), right), product(result_split, right))

    iterate, result = lax.fori_loop(1, NS_STEPS - 1, newton, (iterate, result))
    result_split = split(whole(result))
    factor = 1.5 * eye - 0.5 * product(result_split, halves(iterate))
    result = product(result_split, halves(factor))
    root = result / jnp.sqrt(scale)

    turn = jnp.concatenate(
        [
            jnp.concatenate([root[:half], root[half:]], 1),
            jnp.concatenate([-root[half:], root[:half]], 1),
        ],
        0,
    )
    turn_high, turn_low = split(turn)

    def rotate(x, carry):
        for c in range(3):
            left = jnp.concatenate([fields[last, 0, c, x], fields[last, 1, c, x]], 1)
            left_high, left_low = split(left)
            out = mul(left_high, turn_high) + (
                mul(left_high, turn_low) + mul(left_low, turn_high)
            )
            basis_ref[0, c, x] = out[:, :half]
            basis_ref[1, c, x] = out[:, half:]
        return carry

    lax.fori_loop(0, 4, rotate, 0)

    proj_sum = unpacked(sum_end(1)) / sites_all
    proj_sum = 6.0 * gram_sum + (-1.0 / HOP) * proj_sum
    root_split = split(whole(root))
    ritz = product(split(whole(proj_sum)), halves(root))
    ritz = product(root_split, halves(ritz))
    ritz_ref[...] = ritz


def shards(vectors, links):
    brick = vectors.shape
    sites_all = float(
        vectors.shape[2]
        * lax.axis_size("gx")
        * vectors.shape[3]
        * lax.axis_size("gy")
        * vectors.shape[4]
        * lax.axis_size("gz")
    )
    vec = vectors.reshape(2, 3, 4, 64, 128)
    link = links.reshape(3, 18, 4, 8, 8)
    steps = FILTER_STEPS
    face_x = (2, 3, 64, 128)
    face = (2, 3, 4, 8, 128)
    vmem = lambda *shape: pltpu.VMEM(shape, f32)
    space = pl.BlockSpec(memory_space=pltpu.VMEM)
    basis, ritz = pl.pallas_call(
        lambda *refs: whole_kernel(sites_all, *refs),
        out_shape=(
            jax.ShapeDtypeStruct(vec.shape, f32),
            jax.ShapeDtypeStruct((256, 128), f32),
        ),
        in_specs=[space, space],
        out_specs=(space, space),
        scratch_shapes=[
            vmem(steps + 1, *vec.shape),
            vmem(*vec.shape),
            vmem(3, 18, 4, 72, 128),
            vmem(18, 4, 8, 128),
            vmem(steps, *face_x),
            vmem(steps, *face),
            vmem(steps, *face),
            vmem(steps + 1, *face),
            vmem(steps + 1, *face_x),
            vmem(steps + 1, *face),
            vmem(steps + 1, *face),
            vmem(steps, *face_x),
            vmem(steps, *face),
            vmem(steps, *face),
            vmem(2, 16, 8, 128),
            vmem(2, 16, 8, 128),
            vmem(2, 16, 8, 128),
            vmem(2, 16, 8, 128),
            pltpu.SemaphoreType.DMA((4, steps + 1, 3)),
            pltpu.SemaphoreType.DMA((2, 6, 16)),
        ],
        compiler_params=pltpu.CompilerParams(
            collective_id=0, has_side_effects=True, vmem_limit_bytes=48 * 1024 * 1024
        ),
    )(vec, link)
    return (basis.reshape(brick), ritz.reshape(2, 128, 128))


def solution(mesh):
    return jax.shard_map(
        shards,
        mesh=mesh,
        in_specs=(
            P(None, None, "gx", "gy", "gz", None),
            P(None, None, None, None, "gx", "gy", "gz"),
        ),
        out_specs=(P(None, None, "gx", "gy", "gz", None), P()),
        check_vma=False,
    )
```

```python
import jax
import jax.numpy as jnp
from jax import lax
from jax.experimental import pallas as pl
from jax.experimental.pallas import tpu as pltpu
from jax.sharding import PartitionSpec as P

NS_STEPS = 10
FILTER_STEPS = 4

filter_low = 1.0
filter_high = 12.0

MESH = pl.DeviceIdType.MESH
HOP = -4.0 / (filter_high - filter_low)
SELF = 2.0 * (12.0 - filter_high - filter_low) / (filter_high - filter_low)
SUBLANES = ((0,), (0,))
f32 = jnp.float32
bf16 = jnp.bfloat16


def places():
    gx = lax.axis_index("gx")
    gy = lax.axis_index("gy")
    gz = lax.axis_index("gz")
    return gx, gy, gz // 2, gz % 2


def plane_mate(step):
    gx, gy, row, core = places()
    other_y = (gy + step // 4) % 4
    other_row = (row + step % 4) % 4
    return (gx, other_y, other_row * 2 + core), other_y * 4 + other_row


def line_mate(step):
    gx, gy, row, core = places()
    other_x = (gx + step // 2) % 8
    other_core = (core + step % 2) % 2
    return (other_x, gy, row * 2 + other_core)


def neighbour(axis, sign):
    place = [lax.axis_index("gx"), lax.axis_index("gy"), lax.axis_index("gz")]
    count = (8, 4, 8)[axis]
    place[axis] = (place[axis] + sign + count) % count
    return tuple(place)


def forward(link, field):
    out = [[None] * 3, [None] * 3]
    for r in range(3):
        re = im = None
        for c in range(3):
            ur, ui = link[0][r][c], link[1][r][c]
            vr, vi = field[0][c], field[1][c]
            re_term = ur * vr - ui * vi
            im_term = ur * vi + ui * vr
            re = re_term if re is None else re + re_term
            im = im_term if im is None else im + im_term
        out[0][r], out[1][r] = re, im
    return out


def backward(link, field):
    out = [[None] * 3, [None] * 3]
    for r in range(3):
        re = im = None
        for c in range(3):
            ur, ui = link[0][c][r], link[1][c][r]
            vr, vi = field[0][c], field[1][c]
            re_term = ur * vr + ui * vi
            im_term = ur * vi - ui * vr
            re = re_term if re is None else re + re_term
            im = im_term if im is None else im + im_term
        out[0][r], out[1][r] = re, im
    return out


def both(fn):
    return [[fn(p, c) for c in range(3)] for p in range(2)]


def plus(left, right):
    return both(lambda p, c: left[p][c] + right[p][c])


def split(value):
    high = value.astype(bf16)
    return high, (value - high.astype(f32)).astype(bf16)


def mul(left, right, dims=((1,), (0,))):
    return lax.dot_general(left, right, (dims, ((), ())), preferred_element_type=f32)


def whole(columns):
    half = columns.shape[0] // 2
    return jnp.concatenate(
        [columns, jnp.concatenate([-columns[half:], columns[:half]], 0)], 1
    )


def halves(columns):
    high, low = split(columns)
    return jnp.concatenate([high, low], 1)


def product(left_split, right_halves):
    width = right_halves.shape[1] // 2
    left = jnp.concatenate(left_split, 0)
    rows = left_split[0].shape[0]
    out = mul(left, right_halves)
    out = out[:, :width] + out[:, width:]
    return out[:rows] + out[rows:]


def lower_mask(order, strict):
    row = lax.broadcasted_iota(jnp.int32, (order, order), 0)
    column = lax.broadcasted_iota(jnp.int32, (order, order), 1)
    return row > column if strict else row >= column


def packed(re_part, im_part):
    return jnp.where(lower_mask(re_part.shape[0], False), re_part, im_part)


def unpacked(mixed):
    zero = jnp.zeros_like(mixed)
    low = jnp.where(lower_mask(mixed.shape[0], False), mixed, zero)
    strict = jnp.where(lower_mask(mixed.shape[0], True), mixed, zero)
    high = mixed - low
    return jnp.concatenate([low + strict.T, high - high.T], 0)


def side_by_side(ref, *index):
    half = [ref[(*index, p)].reshape(-1, ref.shape[-1]) for p in range(2)]
    return jnp.concatenate(half, 1)


def whole_kernel(
    sites_all,
    vec_hbm,
    link_hbm,
    basis_ref,
    ritz_ref,
    fields,
    hops,
    wide,
    edge,
    send_x,
    send_y,
    send_z,
    low_z,
    ahead_x,
    ahead_y,
    ahead_z,
    behind_x,
    behind_y,
    behind_z,
    part,
    first,
    second,
    summed,
    link_ref,
    load_sems,
    face_sems,
    sum_sems,
):
    gx, gy, row, core = places()
    mine = gy * 4 + row
    line = gx * 2 + core

    load_links = pltpu.make_async_copy(link_hbm, link_ref, load_sems.at[0])
    load_field = pltpu.make_async_copy(vec_hbm, fields.at[0], load_sems.at[1])
    load_links.start()
    load_field.start()
    barrier = pltpu.get_barrier_semaphore()

    def greet(step, carry):
        device, _ = plane_mate(step)
        pl.semaphore_signal(barrier, inc=1, device_id=device, device_id_type=MESH)
        pl.semaphore_signal(barrier, inc=1, device_id=line_mate(step), device_id_type=MESH)
        return carry

    for axis in range(3):
        for sign in (-1, 1):
            pl.semaphore_signal(
                barrier, inc=1, device_id=neighbour(axis, sign), device_id_type=MESH
            )
    lax.fori_loop(1, 16, greet, 0)

    keep = (lax.broadcasted_iota(jnp.int32, (8, 128), 0) < 7).astype(f32)

    def widen(entry, carry):
        for mu in range(3):
            for x in range(4):
                tile = link_ref[mu, entry, x] * HOP
                turned = tile.T
                for y in range(8):
                    value = jnp.broadcast_to(turned[:, y : y + 1], (8, 128))
                    if mu == 2:
                        value = value * keep
                    wide[mu, entry, x, pl.ds(8 * y, 8)] = value
                if mu == 1:
                    wide[mu, entry, x, pl.ds(64, 8)] = jnp.zeros((8, 128), f32)
                if mu == 2:
                    edge[entry, x] = jnp.broadcast_to(tile[:, 7:8], (8, 128))
        return carry

    load_links.wait()
    lax.fori_loop(0, 18, widen, 0)

    def halve(x, carry):
        for p in range(2):
            for c in range(3):
                fields[0, p, c, x] = fields[0, p, c, x] * 0.5
        return carry

    load_field.wait()
    lax.fori_loop(0, 4, halve, 0)

    def tile_link(mu, x, slot):
        rows = pl.ds(pl.multiple_of(8 * slot, 8), 8)
        return [
            [[wide[mu, p * 9 + r * 3 + c, x, rows] for c in range(3)] for r in range(3)]
            for p in range(2)
        ]

    def edge_link(x):
        return [
            [[edge[p * 9 + r * 3 + c, x] for c in range(3)] for r in range(3)]
            for p in range(2)
        ]

    def tile(k, x, y):
        rows = pl.ds(pl.multiple_of(8 * y, 8), 8)
        return both(lambda p, c: fields[k, p, c, x, rows])

    def strided(k, x, z):
        return both(lambda p, c: fields[k, p, c, x, pl.ds(z, 8, stride=8)])

    def low_copy(k, axis):
        source, target = (
            lambda: (fields.at[k, :, :, 0], ahead_x.at[k]),
            lambda: (fields.at[k, :, :, :, pl.ds(0, 8)], ahead_y.at[k]),
            lambda: (low_z.at[k], ahead_z.at[k]),
        )[axis]()
        return pltpu.make_async_remote_copy(
            src_ref=source,
            dst_ref=target,
            send_sem=face_sems.at[0, k, axis],
            recv_sem=face_sems.at[1, k, axis],
            device_id=neighbour(axis, -1),
            device_id_type=MESH,
        )

    def high_copy(k, axis):
        source, target = (
            lambda: (send_x.at[k], behind_x.at[k]),
            lambda: (send_y.at[k], behind_y.at[k]),
            lambda: (send_z.at[k], behind_z.at[k]),
        )[axis]()
        return pltpu.make_async_remote_copy(
            src_ref=source,
            dst_ref=target,
            send_sem=face_sems.at[2, k, axis],
            recv_sem=face_sems.at[3, k, axis],
            device_id=neighbour(axis, 1),
            device_id_type=MESH,
        )

    def last_copies():
        k = FILTER_STEPS
        some, rest = pl.ds(0, 2), pl.ds(2, 2)
        less, more = pl.ds(0, 32), pl.ds(32, 32)
        low = (
            (0, fields.at[k, :, :, 0, less], ahead_x.at[k, :, :, less]),
            (1, fields.at[k, :, :, some, pl.ds(0, 8)], ahead_y.at[k, :, :, some]),
            (2, low_z.at[k, :, :, some], ahead_z.at[k, :, :, some]),
        )
        high = (
            (0, send_x.at[k, :, :, more], behind_x.at[k, :, :, more]),
            (1, send_y.at[k, :, :, rest], behind_y.at[k, :, :, rest]),
            (2, send_z.at[k, :, :, rest], behind_z.at[k, :, :, rest]),
        )
        return [
            pltpu.make_async_remote_copy(
                src_ref=source,
                dst_ref=target,
                send_sem=face_sems.at[0 if sign < 0 else 2, k, axis],
                recv_sem=face_sems.at[1 if sign < 0 else 3, k, axis],
                device_id=neighbour(axis, sign),
                device_id_type=MESH,
            )
            for sign, group in ((-1, low), (1, high))
            for axis, source, target in group
        ]

    def make_low_z(k, count=4):
        def body(x, carry):
            value = strided(k, x, 0)
            for p in range(2):
                for c in range(3):
                    low_z[k, p, c, x] = value[p][c]
            return carry

        lax.fori_loop(0, count, body, 0)

    def make_high_x(k, begin=0):
        def body(y, carry):
            rows = pl.ds(pl.multiple_of(8 * y, 8), 8)
            value = backward(tile_link(0, 3, y), tile(k, 3, y))
            for p in range(2):
                for c in range(3):
                    send_x[k, p, c, rows] = value[p][c]
            return carry

        lax.fori_loop(begin, 8, body, 0)

    def make_high_yz(k, begin=0):
        def body(x, carry):
            value = backward(tile_link(1, x, 7), tile(k, x, 7))
            other = backward(edge_link(x), strided(k, x, 7))
            for p in range(2):
                for c in range(3):
                    send_y[k, p, c, x] = value[p][c]
                    send_z[k, p, c, x] = other[p][c]
            return carry

        lax.fori_loop(begin, 4, body, 0)

    def local_pass(k):
        again = jnp.where(k == 0, 0.0, jnp.where(k == 1, 2.0, 1.0)).astype(f32)
        before = jnp.maximum(k - 1, 0)

        def body(y, carry):
            rows = pl.ds(pl.multiple_of(8 * y, 8), 8)
            up = jnp.minimum(y + 1, 7)
            down = jnp.maximum(y - 1, 0)
            up_slot = jnp.where(y == 7, 8, y)
            down_slot = jnp.where(y == 0, 8, y - 1)
            for x in range(4):
                here = tile(k, x, y)
                old = tile(before, x, y)
                acc = both(lambda p, c: SELF * here[p][c] - again * old[p][c])
                link = tile_link(2, x, y)
                rolled = both(lambda p, c: pltpu.roll(here[p][c], 7, 0))
                acc = plus(acc, forward(link, rolled))
                back = backward(link, here)
                acc = plus(acc, both(lambda p, c: pltpu.roll(back[p][c], 1, 0)))
                if x < 3:
                    acc = plus(acc, forward(tile_link(0, x, y), tile(k, x + 1, y)))
                if x > 0:
                    acc = plus(acc, backward(tile_link(0, x - 1, y), tile(k, x - 1, y)))
                acc = plus(acc, forward(tile_link(1, x, up_slot), tile(k, x, up)))
                acc = plus(acc, backward(tile_link(1, x, down_slot), tile(k, x, down)))
                for p in range(2):
                    for c in range(3):
                        fields[k + 1, p, c, x, rows] = acc[p][c]
            return carry

        lax.fori_loop(0, 8, body, 0)

    def forward_pass(k):
        def body(y, carry):
            rows = pl.ds(pl.multiple_of(8 * y, 8), 8)
            up = jnp.minimum(y + 1, 7)
            up_slot = jnp.where(y == 7, 8, y)
            for x in range(4):
                here = tile(k, x, y)
                rolled = both(lambda p, c: pltpu.roll(here[p][c], 7, 0))
                acc = forward(tile_link(2, x, y), rolled)
                if x < 3:
                    acc = plus(acc, forward(tile_link(0, x, y), tile(k, x + 1, y)))
                acc = plus(acc, forward(tile_link(1, x, up_slot), tile(k, x, up)))
                for p in range(2):
                    for c in range(3):
                        hops[p, c, x, rows] = acc[p][c]
            return carry

        lax.fori_loop(0, 8, body, 0)

    def ahead_yz(target, index, k, begin, end):
        def body(x, carry):
            value = forward(
                tile_link(1, x, 7), both(lambda p, c: ahead_y[k, p, c, x])
            )
            other = forward(edge_link(x), both(lambda p, c: ahead_z[k, p, c, x]))
            last = pl.ds(56, 8)
            top = pl.ds(7, 8, stride=8)
            for p in range(2):
                for c in range(3):
                    at = (*index, p, c, x)
                    target[(*at, last)] = target[(*at, last)] + value[p][c]
                    target[(*at, top)] = target[(*at, top)] + other[p][c]
            return carry

        lax.fori_loop(begin, end, body, 0)

    def behind_yz(target, index, k, begin, end):
        def body(x, carry):
            head = pl.ds(0, 8)
            bottom = pl.ds(0, 8, stride=8)
            for p in range(2):
                for c in range(3):
                    at = (*index, p, c, x)
                    target[(*at, head)] = target[(*at, head)] + behind_y[k, p, c, x]
                    target[(*at, bottom)] = target[(*at, bottom)] + behind_z[k, p, c, x]
            return carry

        lax.fori_loop(begin, end, body, 0)

    def from_ahead_x(target, index, k, begin, end):
        def body(y, carry):
            rows = pl.ds(pl.multiple_of(8 * y, 8), 8)
            value = forward(
                tile_link(0, 3, y), both(lambda p, c: ahead_x[k, p, c, rows])
            )
            for p in range(2):
                for c in range(3):
                    at = (*index, p, c, 3, rows)
                    target[at] = target[at] + value[p][c]
            return carry

        lax.fori_loop(begin, end, body, 0)

    def from_behind_x(target, index, k, begin, end):
        def body(y, carry):
            rows = pl.ds(pl.multiple_of(8 * y, 8), 8)
            for p in range(2):
                for c in range(3):
                    at = (*index, p, c, 0, rows)
                    target[at] = target[at] + behind_x[k, p, c, rows]
            return carry

        lax.fori_loop(begin, end, body, 0)

    def scatter(j, step):
        device, index = plane_mate(step)
        return pltpu.make_async_remote_copy(
            src_ref=part.at[j, index],
            dst_ref=first.at[j, step],
            send_sem=sum_sems.at[j, 0, step],
            recv_sem=sum_sems.at[j, 1, step],
            device_id=device,
            device_id_type=MESH,
        )

    def across(j, step):
        return pltpu.make_async_remote_copy(
            src_ref=second.at[j, line],
            dst_ref=second.at[j, line],
            send_sem=sum_sems.at[j, 2, step],
            recv_sem=sum_sems.at[j, 3, step],
            device_id=line_mate(step),
            device_id_type=MESH,
        )

    def gather(j, step):
        device, _ = plane_mate(step)
        return pltpu.make_async_remote_copy(
            src_ref=summed.at[j, mine],
            dst_ref=summed.at[j, mine],
            send_sem=sum_sems.at[j, 4, step],
            recv_sem=sum_sems.at[j, 5, step],
            device_id=device,
            device_id_type=MESH,
        )

    def each(fn):
        def body(step, carry):
            fn(step)
            return carry

        lax.fori_loop(1, 16, body, 0)

    def start_all(make, j):
        each(lambda step: make(j, step).start())

    def wait_all(make, j):
        each(lambda step: make(j, step).wait())

    def sum_begin(j, value):
        for piece in range(16):
            part[j, piece] = value[8 * piece : 8 * piece + 8]
        start_all(scatter, j)

    def sum_middle(j):
        first[j, 0] = part[j, mine]
        wait_all(scatter, j)
        total = first[j, 0]
        for step in range(1, 16):
            total = total + first[j, step]
        second[j, line] = total
        start_all(across, j)

    def sum_last(j):
        wait_all(across, j)
        total = second[j, 0]
        for step in range(1, 16):
            total = total + second[j, step]
        summed[j, mine] = total
        start_all(gather, j)

    def sum_end(j):
        wait_all(gather, j)
        return summed[j].reshape(128, 128)

    make_high_x(0)
    make_high_yz(0)
    make_low_z(0)
    pl.semaphore_wait(barrier, 36)
    for axis in range(3):
        low_copy(0, axis).start()
        high_copy(0, axis).start()

    def filter_step(k, carry):
        local_pass(k)
        for axis in (2, 1):
            low_copy(k, axis).wait()
            high_copy(k, axis).wait()
        ahead_yz(fields, (k + 1,), k, 0, 4)
        behind_yz(fields, (k + 1,), k, 0, 4)
        low_copy(k, 0).wait()
        from_ahead_x(fields, (k + 1,), k, 0, 8)
        high_copy(k, 0).wait()
        from_behind_x(fields, (k + 1,), k, 0, 8)

        @pl.when(k < FILTER_STEPS - 1)
        def _():
            low_copy(k + 1, 0).start()
            make_high_x(k + 1)
            high_copy(k + 1, 0).start()
            low_copy(k + 1, 1).start()
            make_high_yz(k + 1)
            high_copy(k + 1, 1).start()
            high_copy(k + 1, 2).start()
            make_low_z(k + 1)
            low_copy(k + 1, 2).start()

        return carry

    lax.fori_loop(0, FILTER_STEPS, filter_step, 0)

    last = FILTER_STEPS
    half_faces = last_copies()
    half_faces[0].start()
    make_high_x(last, 4)
    half_faces[3].start()
    half_faces[1].start()
    make_high_yz(last, 2)
    half_faces[4].start()
    half_faces[5].start()
    make_low_z(last, 2)
    half_faces[2].start()

    high, low = split(side_by_side(fields, last))
    gram = mul(high, high, SUBLANES)
    cross = mul(high, low, SUBLANES)
    gram = gram + (cross + cross.T)
    half = gram.shape[0] // 2
    sum_begin(
        0,
        packed(
            gram[:half, :half] + gram[half:, half:],
            gram[:half, half:] - gram[half:, :half],
        ),
    )

    forward_pass(last)
    for copy in half_faces:
        copy.wait()
    ahead_yz(hops, (), last, 0, 2)
    behind_yz(hops, (), last, 2, 4)
    from_ahead_x(hops, (), last, 0, 4)
    from_behind_x(hops, (), last, 4, 8)
    hop_high, hop_low = split(side_by_side(hops))
    proj = mul(high, hop_high, SUBLANES)
    proj = proj + mul(high, hop_low, SUBLANES)
    proj = proj + mul(low, hop_high, SUBLANES)
    proj_re = proj[:half, :half] + proj[half:, half:]
    proj_im = proj[:half, half:] - proj[half:, :half]
    sum_begin(1, packed(proj_re + proj_re.T, proj_im - proj_im.T))
    sum_middle(0)
    sum_middle(1)
    sum_last(0)
    sum_last(1)
    gram_sum = unpacked(sum_end(0)) / sites_all

    scale = jnp.sqrt(2.0 * jnp.sum(gram_sum * gram_sum, keepdims=True))
    eye = (
        lax.broadcasted_iota(jnp.int32, (2 * half, half), 0)
        == lax.broadcasted_iota(jnp.int32, (2 * half, half), 1)
    ).astype(f32)
    iterate = gram_sum / scale
    factor = 1.5 * eye - 0.5 * iterate
    iterate = product(split(whole(iterate)), halves(factor))
    result = factor

    def newton(step, carry):
        iterate, result = carry
        result_split = split(whole(result))
        factor = 1.5 * eye - 0.5 * product(result_split, halves(iterate))
        right = halves(factor)
        return (product(split(whole(iterate)), right), product(result_split, right))

    iterate, result = lax.fori_loop(1, NS_STEPS - 1, newton, (iterate, result))
    result_split = split(whole(result))
    factor = 1.5 * eye - 0.5 * product(result_split, halves(iterate))
    result = product(result_split, halves(factor))
    root = result / jnp.sqrt(scale)

    turn = jnp.concatenate(
        [
            jnp.concatenate([root[:half], root[half:]], 1),
            jnp.concatenate([-root[half:], root[:half]], 1),
        ],
        0,
    )
    turn_high, turn_low = split(turn)

    def rotate(x, carry):
        for c in range(3):
            left = jnp.concatenate([fields[last, 0, c, x], fields[last, 1, c, x]], 1)
            left_high, left_low = split(left)
            out = mul(left_high, turn_high) + (
                mul(left_high, turn_low) + mul(left_low, turn_high)
            )
            basis_ref[0, c, x] = out[:, :half]
            basis_ref[1, c, x] = out[:, half:]
        return carry

    lax.fori_loop(0, 4, rotate, 0)

    proj_sum = unpacked(sum_end(1)) / sites_all
    proj_sum = 6.0 * gram_sum + (-1.0 / HOP) * proj_sum
    root_split = split(whole(root))
    ritz = product(split(whole(proj_sum)), halves(root))
    ritz = product(root_split, halves(ritz))
    ritz_ref[...] = ritz


def deliver(basis_in, ritz_in, basis_out, ritz_out, sems):
    copies = [
        pltpu.make_async_copy(basis_in, basis_out, sems.at[0]),
        pltpu.make_async_copy(ritz_in, ritz_out, sems.at[1]),
    ]
    for copy in copies:
        copy.start()
    for copy in copies:
        copy.wait()


def shards(vectors, links):
    brick = vectors.shape
    sites_all = float(
        vectors.shape[2]
        * lax.axis_size("gx")
        * vectors.shape[3]
        * lax.axis_size("gy")
        * vectors.shape[4]
        * lax.axis_size("gz")
    )
    vec = vectors.reshape(2, 3, 4, 64, 128)
    link = links.reshape(3, 18, 4, 8, 8)
    steps = FILTER_STEPS
    face_x = (2, 3, 64, 128)
    face = (2, 3, 4, 8, 128)
    vmem = lambda *shape: pltpu.VMEM(shape, f32)
    space = pl.BlockSpec(memory_space=pltpu.VMEM)
    far = pl.BlockSpec(memory_space=pltpu.HBM)
    basis, ritz = pl.pallas_call(
        lambda *refs: whole_kernel(sites_all, *refs),
        out_shape=(
            jax.ShapeDtypeStruct(vec.shape, f32),
            jax.ShapeDtypeStruct((256, 128), f32),
        ),
        in_specs=[far, far],
        out_specs=(space, space),
        scratch_shapes=[
            vmem(steps + 1, *vec.shape),
            vmem(*vec.shape),
            vmem(3, 18, 4, 72, 128),
            vmem(18, 4, 8, 128),
            vmem(steps + 1, *face_x),
            vmem(steps + 1, *face),
            vmem(steps + 1, *face),
            vmem(steps + 1, *face),
            vmem(steps + 1, *face_x),
            vmem(steps + 1, *face),
            vmem(steps + 1, *face),
            vmem(steps + 1, *face_x),
            vmem(steps + 1, *face),
            vmem(steps + 1, *face),
            vmem(2, 16, 8, 128),
            vmem(2, 16, 8, 128),
            vmem(2, 16, 8, 128),
            vmem(2, 16, 8, 128),
            vmem(*link.shape),
            pltpu.SemaphoreType.DMA((2,)),
            pltpu.SemaphoreType.DMA((4, steps + 1, 3)),
            pltpu.SemaphoreType.DMA((2, 6, 16)),
        ],
        compiler_params=pltpu.CompilerParams(
            collective_id=0, has_side_effects=True, vmem_limit_bytes=48 * 1024 * 1024
        ),
    )(
        pltpu.with_memory_space_constraint(vec, pltpu.HBM),
        pltpu.with_memory_space_constraint(link, pltpu.HBM),
    )
    basis, ritz = pl.pallas_call(
        deliver,
        out_shape=(
            jax.ShapeDtypeStruct(vec.shape, f32),
            jax.ShapeDtypeStruct((256, 128), f32),
        ),
        in_specs=[pl.BlockSpec(memory_space=pl.ANY)] * 2,
        out_specs=(far, far),
        scratch_shapes=[pltpu.SemaphoreType.DMA((2,))],
    )(basis, ritz)
    return (basis.reshape(brick), ritz.reshape(2, 128, 128))


def solution(mesh):
    return jax.shard_map(
        shards,
        mesh=mesh,
        in_specs=(
            P(None, None, "gx", "gy", "gz", None),
            P(None, None, None, None, "gx", "gy", "gz"),
        ),
        out_specs=(P(None, None, "gx", "gy", "gz", None), P()),
        check_vma=False,
    )
```

```python
import jax
import jax.numpy as jnp
from jax import lax
from jax.experimental import pallas as pl
from jax.experimental.pallas import tpu as pltpu
from jax.sharding import PartitionSpec as P

NS_STEPS = 10
FILTER_STEPS = 4

filter_low = 1.0
filter_high = 12.0

MESH = pl.DeviceIdType.MESH
HOP = -4.0 / (filter_high - filter_low)
SELF = 2.0 * (12.0 - filter_high - filter_low) / (filter_high - filter_low)
SUBLANES = ((0,), (0,))
f32 = jnp.float32
bf16 = jnp.bfloat16


def places():
    gx = lax.axis_index("gx")
    gy = lax.axis_index("gy")
    gz = lax.axis_index("gz")
    return gx, gy, gz // 2, gz % 2


def plane_mate(step):
    gx, gy, row, core = places()
    other_y = (gy + step // 4) % 4
    other_row = (row + step % 4) % 4
    return (gx, other_y, other_row * 2 + core), other_y * 4 + other_row


def line_mate(step):
    gx, gy, row, core = places()
    other_x = (gx + step // 2) % 8
    other_core = (core + step % 2) % 2
    return (other_x, gy, row * 2 + other_core)


def neighbour(axis, sign):
    place = [lax.axis_index("gx"), lax.axis_index("gy"), lax.axis_index("gz")]
    count = (8, 4, 8)[axis]
    place[axis] = (place[axis] + sign + count) % count
    return tuple(place)


def forward(link, field):
    out = [[None] * 3, [None] * 3]
    for r in range(3):
        re = im = None
        for c in range(3):
            ur, ui = link[0][r][c], link[1][r][c]
            vr, vi = field[0][c], field[1][c]
            re_term = ur * vr - ui * vi
            im_term = ur * vi + ui * vr
            re = re_term if re is None else re + re_term
            im = im_term if im is None else im + im_term
        out[0][r], out[1][r] = re, im
    return out


def backward(link, field):
    out = [[None] * 3, [None] * 3]
    for r in range(3):
        re = im = None
        for c in range(3):
            ur, ui = link[0][c][r], link[1][c][r]
            vr, vi = field[0][c], field[1][c]
            re_term = ur * vr + ui * vi
            im_term = ur * vi - ui * vr
            re = re_term if re is None else re + re_term
            im = im_term if im is None else im + im_term
        out[0][r], out[1][r] = re, im
    return out


def both(fn):
    return [[fn(p, c) for c in range(3)] for p in range(2)]


def plus(left, right):
    return both(lambda p, c: left[p][c] + right[p][c])


def split(value):
    high = value.astype(bf16)
    return high, (value - high.astype(f32)).astype(bf16)


def mul(left, right, dims=((1,), (0,))):
    return lax.dot_general(left, right, (dims, ((), ())), preferred_element_type=f32)


def whole(columns):
    half = columns.shape[0] // 2
    return jnp.concatenate(
        [columns, jnp.concatenate([-columns[half:], columns[:half]], 0)], 1
    )


def halves(columns):
    high, low = split(columns)
    return jnp.concatenate([high, low], 1)


def product(left_split, right_halves):
    width = right_halves.shape[1] // 2
    left = jnp.concatenate(left_split, 0)
    rows = left_split[0].shape[0]
    out = mul(left, right_halves)
    out = out[:, :width] + out[:, width:]
    return out[:rows] + out[rows:]


def lower_mask(order, strict):
    row = lax.broadcasted_iota(jnp.int32, (order, order), 0)
    column = lax.broadcasted_iota(jnp.int32, (order, order), 1)
    return row > column if strict else row >= column


def packed(re_part, im_part):
    return jnp.where(lower_mask(re_part.shape[0], False), re_part, im_part)


def unpacked(mixed):
    zero = jnp.zeros_like(mixed)
    low = jnp.where(lower_mask(mixed.shape[0], False), mixed, zero)
    strict = jnp.where(lower_mask(mixed.shape[0], True), mixed, zero)
    high = mixed - low
    return jnp.concatenate([low + strict.T, high - high.T], 0)


def side_by_side(ref, *index):
    half = [ref[(*index, p)].reshape(-1, ref.shape[-1]) for p in range(2)]
    return jnp.concatenate(half, 1)


def transposed(tiles):
    block = lax.broadcasted_iota(jnp.int32, (8, 128), 1) // 32
    low = block < 2
    even = block % 2 == 0
    a, b, c, d = tiles
    pairs = [
        jnp.where(low, a, pltpu.roll(c, 64, 1)),
        jnp.where(low, b, pltpu.roll(d, 64, 1)),
        jnp.where(low, pltpu.roll(a, 64, 1), c),
        jnp.where(low, pltpu.roll(b, 64, 1), d),
    ]
    out = []
    for first, second in (pairs[:2], pairs[2:]):
        out.append(jnp.where(even, first, pltpu.roll(second, 32, 1)))
        out.append(jnp.where(even, pltpu.roll(first, 96, 1), second))
    return out


def lane_roll(value, blocks):
    shift = 32 * (blocks % 4)
    return value if shift == 0 else pltpu.roll(value, shift, 1)


def whole_kernel(
    sites_all,
    vec_hbm,
    link_hbm,
    basis_ref,
    ritz_ref,
    plain,
    hops,
    fields,
    packed_hops,
    wide,
    face_y,
    face_z,
    send_x,
    send_y,
    send_z,
    low_y,
    low_z,
    ahead_x,
    ahead_y,
    ahead_z,
    behind_x,
    behind_y,
    behind_z,
    part,
    first,
    second,
    summed,
    link_ref,
    load_sems,
    face_sems,
    sum_sems,
):
    gx, gy, row, core = places()
    mine = gy * 4 + row
    line = gx * 2 + core

    barrier = pltpu.get_barrier_semaphore()
    load_field = pltpu.make_async_copy(vec_hbm, plain, load_sems.at[0])
    load_links = pltpu.make_async_copy(link_hbm, link_ref, load_sems.at[1])
    for axis in range(3):
        for sign in (-1, 1):
            pl.semaphore_signal(
                barrier, inc=1, device_id=neighbour(axis, sign), device_id_type=MESH
            )
    load_links.start()
    load_field.start()

    def greet(step, carry):
        device, _ = plane_mate(step)
        pl.semaphore_signal(barrier, inc=1, device_id=device, device_id_type=MESH)
        pl.semaphore_signal(barrier, inc=1, device_id=line_mate(step), device_id_type=MESH)
        return carry

    lax.fori_loop(1, 16, greet, 0)

    block = lax.broadcasted_iota(jnp.int32, (8, 128), 1) // 32
    zero = jnp.zeros((8, 128), f32)

    def rows_of(x, odd):
        return pl.ds(16 * x + 8 * odd, 8)

    def widen(entry, carry):
        for mu in range(3):
            for x in range(4):
                turned = (link_ref[mu, entry, x] * HOP).T
                for odd in range(2):
                    lanes = [
                        jnp.broadcast_to(turned[:, y : y + 1], (8, 128))
                        for y in range(odd, 8, 2)
                    ]
                    value = jnp.where(
                        block < 2,
                        jnp.where(block == 0, lanes[0], lanes[1]),
                        jnp.where(block == 2, lanes[2], lanes[3]),
                    )
                    wide[mu, entry, rows_of(x, odd)] = value
        across_y = zero
        for x in range(4):
            value = wide[1, entry, rows_of(x, 1)]
            across_y = jnp.where(block == x, lane_roll(value, x + 1), across_y)
            wide[1, entry, rows_of(x, 1)] = jnp.where(block == 3, zero, value)
        face_y[entry] = across_y
        face_z[entry] = wide[2, entry, pl.ds(7, 8, stride=8)]
        wide[2, entry, pl.ds(7, 8, stride=8)] = zero
        return carry

    def pack(x, carry):
        for p in range(2):
            for c in range(3):
                for odd in range(2):
                    tiles = transposed(
                        [plain[p, c, x, pl.ds(8 * y, 8)] * 0.5 for y in range(odd, 8, 2)]
                    )
                    rows = pl.ds(pl.multiple_of(16 * x + 8 * odd, 8), 8)
                    for g in range(4):
                        fields[0, g, p, c, rows] = tiles[g]
        return carry

    def unpack(read, target):
        def body(x, carry):
            for p in range(2):
                for c in range(3):
                    for odd in range(2):
                        rows = pl.ds(pl.multiple_of(16 * x + 8 * odd, 8), 8)
                        tiles = transposed([read(g, p, c, rows) for g in range(4)])
                        for q in range(4):
                            target[p, c, x, pl.ds(8 * (odd + 2 * q), 8)] = tiles[q]
            return carry

        lax.fori_loop(0, 4, body, 0)

    def tile_link(mu, x, odd):
        rows = rows_of(x, odd)
        return [
            [[wide[mu, p * 9 + r * 3 + c, rows] for c in range(3)] for r in range(3)]
            for p in range(2)
        ]

    def face_link(ref):
        return [
            [[ref[p * 9 + r * 3 + c] for c in range(3)] for r in range(3)]
            for p in range(2)
        ]

    def tile(k, g, x, odd):
        return both(lambda p, c: fields[k, g, p, c, rows_of(x, odd)])

    def store(ref, value, *index):
        for p in range(2):
            for c in range(3):
                ref[(*index[:2], p, c, *index[2:])] = value[p][c]

    def face_copy(sign, axis, k, g):
        last = isinstance(k, int) and k == FILTER_STEPS
        if sign < 0:
            source, target = (
                lambda: (fields.at[k, g, :, :, pl.ds(0, 16)], ahead_x.at[k, g]),
                lambda: (low_y.at[k, g], ahead_y.at[k, g]),
                lambda: (low_z.at[k, g], ahead_z.at[k, g]),
            )[axis]()
            if last and axis == 0:
                some = pl.ds(0, 8)
                source = fields.at[k, g, :, :, some]
                target = ahead_x.at[k, g, :, :, some]
        else:
            source, target = (
                lambda: (send_x.at[k, g], behind_x.at[k, g]),
                lambda: (send_y.at[k, g], behind_y.at[k, g]),
                lambda: (send_z.at[k, g], behind_z.at[k, g]),
            )[axis]()
            if last:
                rest = pl.ds(8, 8)
                source = send_x.at[k, g, :, :, rest]
                target = behind_x.at[k, g, :, :, rest]
        side = 0 if sign < 0 else 2
        return pltpu.make_async_remote_copy(
            src_ref=source,
            dst_ref=target,
            send_sem=face_sems.at[side, k, g, axis],
            recv_sem=face_sems.at[side + 1, k, g, axis],
            device_id=neighbour(axis, sign),
            device_id_type=MESH,
        )

    def gather_y(k, g, odd, blocks):
        def one(p, c):
            out = fields[k, g, p, c, rows_of(0, odd)]
            out = lane_roll(out, blocks)
            for x in range(1, 4):
                value = lane_roll(fields[k, g, p, c, rows_of(x, odd)], blocks + x)
                out = jnp.where(block == x, value, out)
            return out

        return both(one)

    def strided(k, g, z):
        return both(lambda p, c: fields[k, g, p, c, pl.ds(z, 8, stride=8)])

    def make_high_x(k, g, odds=(0, 1)):
        for odd in odds:
            value = backward(tile_link(0, 3, odd), tile(k, g, 3, odd))
            store(send_x, value, k, g, pl.ds(8 * odd, 8))

    def make_low_y(k, g):
        store(low_y, gather_y(k, g, 0, 0), k, g)

    def make_high_y(k, g):
        store(send_y, backward(face_link(face_y), gather_y(k, g, 1, 1)), k, g)

    def make_low_z(k, g):
        store(low_z, strided(k, g, 0), k, g)

    def make_high_z(k, g):
        store(send_z, backward(face_link(face_z), strided(k, g, 7)), k, g)

    def send_faces(k, g):
        face_copy(-1, 0, k, g).start()
        make_high_x(k, g)
        face_copy(1, 0, k, g).start()
        make_low_y(k, g)
        face_copy(-1, 1, k, g).start()
        make_high_y(k, g)
        face_copy(1, 1, k, g).start()
        make_low_z(k, g)
        face_copy(-1, 2, k, g).start()
        make_high_z(k, g)
        face_copy(1, 2, k, g).start()

    def send_last(g):
        k = FILTER_STEPS
        face_copy(-1, 0, k, g).start()
        make_high_x(k, g, (1,))
        face_copy(1, 0, k, g).start()
        make_low_y(k, g)
        face_copy(-1, 1, k, g).start()
        make_low_z(k, g)
        face_copy(-1, 2, k, g).start()

    def forward_hops(k, g, x, odd, here, acc):
        rolled = both(lambda p, c: pltpu.roll(here[p][c], 7, 0))
        value = forward(tile_link(2, x, odd), rolled)
        acc = value if acc is None else plus(acc, value)
        if x < 3:
            acc = plus(acc, forward(tile_link(0, x, odd), tile(k, g, x + 1, odd)))
        other = tile(k, g, x, 1 - odd)
        if odd:
            other = both(lambda p, c: lane_roll(other_of(k, g, p, c, x), 3))
        return plus(acc, forward(tile_link(1, x, odd), other))

    def other_of(k, g, p, c, x):
        return fields[k, g, p, c, rows_of(x, 0)]

    def local_pass(k, g):
        again = jnp.where(k == 0, 0.0, jnp.where(k == 1, 2.0, 1.0)).astype(f32)
        before = jnp.maximum(k - 1, 0)
        for x in range(4):
            for odd in range(2):
                here = tile(k, g, x, odd)
                old = tile(before, g, x, odd)
                acc = both(lambda p, c: SELF * here[p][c] - again * old[p][c])
                acc = forward_hops(k, g, x, odd, here, acc)
                back = backward(tile_link(2, x, odd), here)
                acc = plus(acc, both(lambda p, c: pltpu.roll(back[p][c], 1, 0)))
                if x > 0:
                    acc = plus(acc, backward(tile_link(0, x - 1, odd), tile(k, g, x - 1, odd)))
                back = backward(tile_link(1, x, 1 - odd), tile(k, g, x, 1 - odd))
                if not odd:
                    back_y = back
                    back = both(lambda p, c: lane_roll(back_y[p][c], 1))
                acc = plus(acc, back)
                store(fields, acc, k + 1, g, rows_of(x, odd))

    def forward_pass(k, g):
        for x in range(4):
            for odd in range(2):
                acc = forward_hops(k, g, x, odd, tile(k, g, x, odd), None)
                for p in range(2):
                    for c in range(3):
                        packed_hops[g, p, c, rows_of(x, odd)] = acc[p][c]

    def from_ahead_x(at, k, g, odds=(0, 1)):
        for odd in odds:
            value = forward(
                tile_link(0, 3, odd),
                both(lambda p, c: ahead_x[k, g, p, c, pl.ds(8 * odd, 8)]),
            )
            for p in range(2):
                for c in range(3):
                    ref, index = at(p, c)
                    rows = (*index, rows_of(3, odd))
                    ref[rows] = ref[rows] + value[p][c]

    def from_behind_x(at, k, g, odds=(0, 1)):
        for odd in odds:
            for p in range(2):
                for c in range(3):
                    ref, index = at(p, c)
                    rows = (*index, rows_of(0, odd))
                    ref[rows] = ref[rows] + behind_x[k, g, p, c, pl.ds(8 * odd, 8)]

    def from_ahead_yz(at, k, g):
        value = forward(face_link(face_y), both(lambda p, c: ahead_y[k, g, p, c]))
        other = forward(face_link(face_z), both(lambda p, c: ahead_z[k, g, p, c]))
        for p in range(2):
            for c in range(3):
                ref, index = at(p, c)
                for x in range(4):
                    rows = (*index, rows_of(x, 1))
                    term = jnp.where(block == 3, lane_roll(value[p][c], 3 - x), zero)
                    ref[rows] = ref[rows] + term
                rows = (*index, pl.ds(7, 8, stride=8))
                ref[rows] = ref[rows] + other[p][c]

    def from_behind_yz(at, k, g):
        for p in range(2):
            for c in range(3):
                ref, index = at(p, c)
                value = behind_y[k, g, p, c]
                for x in range(4):
                    rows = (*index, rows_of(x, 0))
                    term = jnp.where(block == 0, lane_roll(value, 4 - x), zero)
                    ref[rows] = ref[rows] + term
                rows = (*index, pl.ds(0, 8, stride=8))
                ref[rows] = ref[rows] + behind_z[k, g, p, c]

    def finish(k, g):
        at = lambda p, c: (fields, (k + 1, g, p, c))
        for axis in (2, 1):
            face_copy(-1, axis, k, g).wait()
            face_copy(1, axis, k, g).wait()
        from_ahead_yz(at, k, g)
        from_behind_yz(at, k, g)
        face_copy(-1, 0, k, g).wait()
        from_ahead_x(at, k, g)
        face_copy(1, 0, k, g).wait()
        from_behind_x(at, k, g)

    def finish_hops(g):
        k = FILTER_STEPS
        at = lambda p, c: (packed_hops, (g, p, c))
        for axis in (2, 1):
            face_copy(-1, axis, k, g).wait()
        from_ahead_yz(at, k, g)
        face_copy(-1, 0, k, g).wait()
        from_ahead_x(at, k, g, (0,))
        face_copy(1, 0, k, g).wait()
        from_behind_x(at, k, g, (1,))

    def groups(fn, begin=0, end=4):
        def body(g, carry):
            fn(g)
            return carry

        lax.fori_loop(begin, end, body, 0)

    def scatter(j, step):
        device, index = plane_mate(step)
        return pltpu.make_async_remote_copy(
            src_ref=part.at[j, index],
            dst_ref=first.at[j, step],
            send_sem=sum_sems.at[j, 0, step],
            recv_sem=sum_sems.at[j, 1, step],
            device_id=device,
            device_id_type=MESH,
        )

    def across(j, step):
        return pltpu.make_async_remote_copy(
            src_ref=second.at[j, line],
            dst_ref=second.at[j, line],
            send_sem=sum_sems.at[j, 2, step],
            recv_sem=sum_sems.at[j, 3, step],
            device_id=line_mate(step),
            device_id_type=MESH,
        )

    def gather(j, step):
        device, _ = plane_mate(step)
        return pltpu.make_async_remote_copy(
            src_ref=summed.at[j, mine],
            dst_ref=summed.at[j, mine],
            send_sem=sum_sems.at[j, 4, step],
            recv_sem=sum_sems.at[j, 5, step],
            device_id=device,
            device_id_type=MESH,
        )

    def each(fn):
        def body(step, carry):
            fn(step)
            return carry

        lax.fori_loop(1, 16, body, 0)

    def start_all(make, j):
        each(lambda step: make(j, step).start())

    def wait_all(make, j):
        each(lambda step: make(j, step).wait())

    def sum_begin(j, value):
        for piece in range(16):
            part[j, piece] = value[8 * piece : 8 * piece + 8]
        start_all(scatter, j)

    def sum_middle(j):
        first[j, 0] = part[j, mine]
        wait_all(scatter, j)
        total = first[j, 0]
        for step in range(1, 16):
            total = total + first[j, step]
        second[j, line] = total
        start_all(across, j)

    def sum_last(j):
        wait_all(across, j)
        total = second[j, 0]
        for step in range(1, 16):
            total = total + second[j, step]
        summed[j, mine] = total
        start_all(gather, j)

    def sum_end(j):
        wait_all(gather, j)
        return summed[j].reshape(128, 128)

    load_links.wait()
    lax.fori_loop(0, 18, widen, 0)
    load_field.wait()
    lax.fori_loop(0, 4, pack, 0)
    pl.semaphore_wait(barrier, 36)
    groups(lambda g: send_faces(0, g))
    groups(lambda g: local_pass(0, g))

    def turn_of(index):
        k = index // 4
        g = index % 4
        finish(k, g)
        send_faces(k + 1, g)
        local_pass(k + 1, g)

    groups(turn_of, 0, 4 * (FILTER_STEPS - 1))

    def last_turn(g):
        finish(FILTER_STEPS - 1, g)
        send_last(g)

    groups(last_turn)
    last = FILTER_STEPS
    unpack(lambda g, p, c, rows: fields[last, g, p, c, rows], plain)

    high, low = split(side_by_side(plain))
    gram = mul(high, high, SUBLANES)
    cross = mul(high, low, SUBLANES)
    gram = gram + (cross + cross.T)
    half = gram.shape[0] // 2
    sum_begin(
        0,
        packed(
            gram[:half, :half] + gram[half:, half:],
            gram[:half, half:] - gram[half:, :half],
        ),
    )

    groups(lambda g: forward_pass(last, g))
    groups(finish_hops)
    unpack(lambda g, p, c, rows: packed_hops[g, p, c, rows], hops)
    hop_high, hop_low = split(side_by_side(hops))
    proj = mul(high, hop_high, SUBLANES)
    proj = proj + mul(high, hop_low, SUBLANES)
    proj = proj + mul(low, hop_high, SUBLANES)
    proj_re = proj[:half, :half] + proj[half:, half:]
    proj_im = proj[:half, half:] - proj[half:, :half]
    sum_begin(1, packed(proj_re + proj_re.T, proj_im - proj_im.T))
    sum_middle(0)
    sum_middle(1)
    sum_last(0)
    sum_last(1)
    gram_sum = unpacked(sum_end(0)) / sites_all

    scale = jnp.sqrt(2.0 * jnp.sum(gram_sum * gram_sum, keepdims=True))
    eye = (
        lax.broadcasted_iota(jnp.int32, (2 * half, half), 0)
        == lax.broadcasted_iota(jnp.int32, (2 * half, half), 1)
    ).astype(f32)
    iterate = gram_sum / scale
    factor = 1.5 * eye - 0.5 * iterate
    iterate = product(split(whole(iterate)), halves(factor))
    result = factor

    def newton(step, carry):
        iterate, result = carry
        result_split = split(whole(result))
        factor = 1.5 * eye - 0.5 * product(result_split, halves(iterate))
        right = halves(factor)
        return (product(split(whole(iterate)), right), product(result_split, right))

    iterate, result = lax.fori_loop(1, NS_STEPS - 1, newton, (iterate, result))
    result_split = split(whole(result))
    factor = 1.5 * eye - 0.5 * product(result_split, halves(iterate))
    result = product(result_split, halves(factor))
    root = result / jnp.sqrt(scale)

    turn = jnp.concatenate(
        [
            jnp.concatenate([root[:half], root[half:]], 1),
            jnp.concatenate([-root[half:], root[:half]], 1),
        ],
        0,
    )
    turn_high, turn_low = split(turn)

    def rotate(x, carry):
        for c in range(3):
            left = jnp.concatenate([plain[0, c, x], plain[1, c, x]], 1)
            left_high, left_low = split(left)
            out = mul(left_high, turn_high) + (
                mul(left_high, turn_low) + mul(left_low, turn_high)
            )
            basis_ref[0, c, x] = out[:, :half]
            basis_ref[1, c, x] = out[:, half:]
        return carry

    lax.fori_loop(0, 4, rotate, 0)

    proj_sum = unpacked(sum_end(1)) / sites_all
    proj_sum = 6.0 * gram_sum + (-1.0 / HOP) * proj_sum
    root_split = split(whole(root))
    ritz = product(split(whole(proj_sum)), halves(root))
    ritz = product(root_split, halves(ritz))
    ritz_ref[...] = ritz


def deliver(basis_in, ritz_in, basis_out, ritz_out, sems):
    copies = [
        pltpu.make_async_copy(basis_in, basis_out, sems.at[0]),
        pltpu.make_async_copy(ritz_in, ritz_out, sems.at[1]),
    ]
    for copy in copies:
        copy.start()
    for copy in copies:
        copy.wait()


def shards(vectors, links):
    brick = vectors.shape
    sites_all = float(
        vectors.shape[2]
        * lax.axis_size("gx")
        * vectors.shape[3]
        * lax.axis_size("gy")
        * vectors.shape[4]
        * lax.axis_size("gz")
    )
    vec = vectors.reshape(2, 3, 4, 64, 128)
    link = links.reshape(3, 18, 4, 8, 8)
    steps = FILTER_STEPS
    face_x = (steps + 1, 4, 2, 3, 16, 128)
    face = (steps + 1, 4, 2, 3, 8, 128)
    vmem = lambda *shape: pltpu.VMEM(shape, f32)
    space = pl.BlockSpec(memory_space=pltpu.VMEM)
    far = pl.BlockSpec(memory_space=pltpu.HBM)
    basis, ritz = pl.pallas_call(
        lambda *refs: whole_kernel(sites_all, *refs),
        out_shape=(
            jax.ShapeDtypeStruct(vec.shape, f32),
            jax.ShapeDtypeStruct((256, 128), f32),
        ),
        in_specs=[far, far],
        out_specs=(space, space),
        scratch_shapes=[
            vmem(*vec.shape),
            vmem(*vec.shape),
            vmem(steps + 1, 4, 2, 3, 64, 128),
            vmem(4, 2, 3, 64, 128),
            vmem(3, 18, 64, 128),
            vmem(18, 8, 128),
            vmem(18, 8, 128),
            vmem(*face_x),
            vmem(*face),
            vmem(*face),
            vmem(*face),
            vmem(*face),
            vmem(*face_x),
            vmem(*face),
            vmem(*face),
            vmem(*face_x),
            vmem(*face),
            vmem(*face),
            vmem(2, 16, 8, 128),
            vmem(2, 16, 8, 128),
            vmem(2, 16, 8, 128),
            vmem(2, 16, 8, 128),
            vmem(*link.shape),
            pltpu.SemaphoreType.DMA((2,)),
            pltpu.SemaphoreType.DMA((4, steps + 1, 4, 3)),
            pltpu.SemaphoreType.DMA((2, 6, 16)),
        ],
        compiler_params=pltpu.CompilerParams(
            collective_id=0, has_side_effects=True, vmem_limit_bytes=48 * 1024 * 1024
        ),
    )(
        pltpu.with_memory_space_constraint(vec, pltpu.HBM),
        pltpu.with_memory_space_constraint(link, pltpu.HBM),
    )
    basis, ritz = pl.pallas_call(
        deliver,
        out_shape=(
            jax.ShapeDtypeStruct(vec.shape, f32),
            jax.ShapeDtypeStruct((256, 128), f32),
        ),
        in_specs=[space, space],
        out_specs=(far, far),
        scratch_shapes=[pltpu.SemaphoreType.DMA((2,))],
        compiler_params=pltpu.CompilerParams(vmem_limit_bytes=4 * 1024 * 1024),
    )(basis, ritz)
    return (basis.reshape(brick), ritz.reshape(2, 128, 128))


def solution(mesh):
    return jax.shard_map(
        shards,
        mesh=mesh,
        in_specs=(
            P(None, None, "gx", "gy", "gz", None),
            P(None, None, None, None, "gx", "gy", "gz"),
        ),
        out_specs=(P(None, None, "gx", "gy", "gz", None), P()),
        check_vma=False,
    )
```

```python
import jax
import jax.numpy as jnp
from jax import lax
from jax.experimental import pallas as pl
from jax.experimental.pallas import tpu as pltpu
from jax.sharding import PartitionSpec as P

NS_STEPS = 10
FILTER_STEPS = 4

filter_low = 1.0
filter_high = 12.0

MESH = pl.DeviceIdType.MESH
HOP = -4.0 / (filter_high - filter_low)
SELF = 2.0 * (12.0 - filter_high - filter_low) / (filter_high - filter_low)
SUBLANES = ((0,), (0,))
f32 = jnp.float32
bf16 = jnp.bfloat16


def places():
    gx = lax.axis_index("gx")
    gy = lax.axis_index("gy")
    gz = lax.axis_index("gz")
    return gx, gy, gz // 2, gz % 2


def plane_mate(step):
    gx, gy, row, core = places()
    other_y = (gy + step // 4) % 4
    other_row = (row + step % 4) % 4
    return (gx, other_y, other_row * 2 + core), other_y * 4 + other_row


def line_mate(step):
    gx, gy, row, core = places()
    other_x = (gx + step // 2) % 8
    other_core = (core + step % 2) % 2
    return (other_x, gy, row * 2 + other_core)


def neighbour(axis, sign):
    place = [lax.axis_index("gx"), lax.axis_index("gy"), lax.axis_index("gz")]
    count = (8, 4, 8)[axis]
    place[axis] = (place[axis] + sign + count) % count
    return tuple(place)


def forward(link, field):
    out = [[None] * 3, [None] * 3]
    for r in range(3):
        re = im = None
        for c in range(3):
            ur, ui = link[0][r][c], link[1][r][c]
            vr, vi = field[0][c], field[1][c]
            re_term = ur * vr - ui * vi
            im_term = ur * vi + ui * vr
            re = re_term if re is None else re + re_term
            im = im_term if im is None else im + im_term
        out[0][r], out[1][r] = re, im
    return out


def backward(link, field):
    out = [[None] * 3, [None] * 3]
    for r in range(3):
        re = im = None
        for c in range(3):
            ur, ui = link[0][c][r], link[1][c][r]
            vr, vi = field[0][c], field[1][c]
            re_term = ur * vr + ui * vi
            im_term = ur * vi - ui * vr
            re = re_term if re is None else re + re_term
            im = im_term if im is None else im + im_term
        out[0][r], out[1][r] = re, im
    return out


def both(fn):
    return [[fn(p, c) for c in range(3)] for p in range(2)]


def plus(left, right):
    return both(lambda p, c: left[p][c] + right[p][c])


def split(value):
    high = value.astype(bf16)
    return high, (value - high.astype(f32)).astype(bf16)


def mul(left, right, dims=((1,), (0,))):
    return lax.dot_general(left, right, (dims, ((), ())), preferred_element_type=f32)


def whole(columns):
    half = columns.shape[0] // 2
    return jnp.concatenate(
        [columns, jnp.concatenate([-columns[half:], columns[:half]], 0)], 1
    )


def whole_split(columns):
    high, low = split(columns)
    return whole(high), whole(low)


def halves(columns):
    high, low = split(columns)
    return jnp.concatenate([high, low], 1)


def product(left_split, right_halves):
    width = right_halves.shape[1] // 2
    left = jnp.concatenate(left_split, 0)
    rows = left_split[0].shape[0]
    out = mul(left, right_halves)
    out = out[:, :width] + out[:, width:]
    return out[:rows] + out[rows:]


def lower_mask(order, strict):
    row = lax.broadcasted_iota(jnp.int32, (order, order), 0)
    column = lax.broadcasted_iota(jnp.int32, (order, order), 1)
    return row > column if strict else row >= column


def packed(re_part, im_part):
    return jnp.where(lower_mask(re_part.shape[0], False), re_part, im_part)


def unpacked(mixed):
    zero = jnp.zeros_like(mixed)
    low = jnp.where(lower_mask(mixed.shape[0], False), mixed, zero)
    strict = jnp.where(lower_mask(mixed.shape[0], True), mixed, zero)
    high = mixed - low
    return jnp.concatenate([low + strict.T, high - high.T], 0)


def side_by_side(ref, *index):
    half = [ref[(*index, p)].reshape(-1, ref.shape[-1]) for p in range(2)]
    return jnp.concatenate(half, 1)


def transposed(tiles):
    block = lax.broadcasted_iota(jnp.int32, (8, 128), 1) // 32
    low = block < 2
    even = block % 2 == 0
    a, b, c, d = tiles
    pairs = [
        jnp.where(low, a, pltpu.roll(c, 64, 1)),
        jnp.where(low, b, pltpu.roll(d, 64, 1)),
        jnp.where(low, pltpu.roll(a, 64, 1), c),
        jnp.where(low, pltpu.roll(b, 64, 1), d),
    ]
    out = []
    for first, second in (pairs[:2], pairs[2:]):
        out.append(jnp.where(even, first, pltpu.roll(second, 32, 1)))
        out.append(jnp.where(even, pltpu.roll(first, 96, 1), second))
    return out


def lane_roll(value, blocks):
    shift = 32 * (blocks % 4)
    return value if shift == 0 else pltpu.roll(value, shift, 1)


def whole_kernel(
    sites_all,
    vec_hbm,
    link_hbm,
    basis_ref,
    ritz_ref,
    plain,
    hops,
    fields,
    packed_hops,
    wide,
    face_y,
    face_z,
    send_x,
    send_y,
    send_z,
    low_y,
    low_z,
    ahead_x,
    ahead_y,
    ahead_z,
    behind_x,
    behind_y,
    behind_z,
    part,
    first,
    second,
    summed,
    link_ref,
    load_sems,
    face_sems,
    sum_sems,
):
    gx, gy, row, core = places()
    mine = gy * 4 + row
    line = gx * 2 + core

    barrier = pltpu.get_barrier_semaphore()
    load_field = pltpu.make_async_copy(vec_hbm, plain, load_sems.at[0])
    load_links = pltpu.make_async_copy(link_hbm, link_ref, load_sems.at[1])
    load_links.start()
    load_field.start()
    for axis in range(3):
        for sign in (-1, 1):
            pl.semaphore_signal(
                barrier, inc=1, device_id=neighbour(axis, sign), device_id_type=MESH
            )

    def greet(step, carry):
        device, _ = plane_mate(step)
        pl.semaphore_signal(barrier, inc=1, device_id=device, device_id_type=MESH)
        pl.semaphore_signal(barrier, inc=1, device_id=line_mate(step), device_id_type=MESH)
        return carry

    lax.fori_loop(1, 16, greet, 0)

    block = lax.broadcasted_iota(jnp.int32, (8, 128), 1) // 32
    zero = jnp.zeros((8, 128), f32)

    def rows_of(x, odd):
        return pl.ds(16 * x + 8 * odd, 8)

    def widen(batch, carry):
        begin = jnp.minimum(4 * batch, 50)
        tiles = link_ref[pl.ds(begin, 4)].reshape(128, 8)
        turned = tiles.T * HOP
        for entry in range(4):
            for x in range(4):
                for odd in range(2):
                    wide[begin + entry, rows_of(x, odd)] = jnp.take_along_axis(
                        turned,
                        32 * entry + 8 * x + odd + 2 * block,
                        axis=1,
                        mode="promise_in_bounds",
                    )
        return carry

    def edges(entry, carry):
        across_y = zero
        for x in range(4):
            value = wide[18 + entry, rows_of(x, 1)]
            across_y = jnp.where(block == x, lane_roll(value, x + 1), across_y)
            wide[18 + entry, rows_of(x, 1)] = jnp.where(block == 3, zero, value)
        face_y[entry] = across_y
        face_z[entry] = wide[36 + entry, pl.ds(7, 8, stride=8)]
        wide[36 + entry, pl.ds(7, 8, stride=8)] = zero
        return carry

    def pack(x, carry):
        for p in range(2):
            for c in range(3):
                for odd in range(2):
                    tiles = transposed(
                        [plain[p, c, x, pl.ds(8 * y, 8)] * 0.5 for y in range(odd, 8, 2)]
                    )
                    rows = pl.ds(pl.multiple_of(16 * x + 8 * odd, 8), 8)
                    for g in range(4):
                        fields[0, g, p, c, rows] = tiles[g]
        return carry

    def unpack(read, target):
        def body(x, carry):
            for p in range(2):
                for c in range(3):
                    for odd in range(2):
                        rows = pl.ds(pl.multiple_of(16 * x + 8 * odd, 8), 8)
                        tiles = transposed([read(g, p, c, rows) for g in range(4)])
                        for q in range(4):
                            target[p, c, x, pl.ds(8 * (odd + 2 * q), 8)] = tiles[q]
            return carry

        lax.fori_loop(0, 4, body, 0, unroll=True)

    def tile_link(mu, x, odd):
        rows = rows_of(x, odd)
        return [
            [[wide[18 * mu + p * 9 + r * 3 + c, rows] for c in range(3)] for r in range(3)]
            for p in range(2)
        ]

    def face_link(ref):
        return [
            [[ref[p * 9 + r * 3 + c] for c in range(3)] for r in range(3)]
            for p in range(2)
        ]

    def tile(k, g, x, odd):
        return both(lambda p, c: fields[k, g, p, c, rows_of(x, odd)])

    def store(ref, value, *index):
        for p in range(2):
            for c in range(3):
                ref[(*index[:2], p, c, *index[2:])] = value[p][c]

    def face_copy(sign, axis, k, g):
        last = isinstance(k, int) and k == FILTER_STEPS
        if sign < 0:
            source, target = (
                lambda: (fields.at[k, g, :, :, pl.ds(0, 16)], ahead_x.at[k, g]),
                lambda: (low_y.at[k, g], ahead_y.at[k, g]),
                lambda: (low_z.at[k, g], ahead_z.at[k, g]),
            )[axis]()
            if last and axis == 0:
                some = pl.ds(0, 8)
                source = fields.at[k, g, :, :, some]
                target = ahead_x.at[k, g, :, :, some]
        else:
            source, target = (
                lambda: (send_x.at[k, g], behind_x.at[k, g]),
                lambda: (send_y.at[k, g], behind_y.at[k, g]),
                lambda: (send_z.at[k, g], behind_z.at[k, g]),
            )[axis]()
            if last:
                rest = pl.ds(8, 8)
                source = send_x.at[k, g, :, :, rest]
                target = behind_x.at[k, g, :, :, rest]
        side = 0 if sign < 0 else 2
        return pltpu.make_async_remote_copy(
            src_ref=source,
            dst_ref=target,
            send_sem=face_sems.at[side, k, g, axis],
            recv_sem=face_sems.at[side + 1, k, g, axis],
            device_id=neighbour(axis, sign),
            device_id_type=MESH,
        )

    def gather_y(k, g, odd, blocks):
        def one(p, c):
            out = fields[k, g, p, c, rows_of(0, odd)]
            out = lane_roll(out, blocks)
            for x in range(1, 4):
                value = lane_roll(fields[k, g, p, c, rows_of(x, odd)], blocks + x)
                out = jnp.where(block == x, value, out)
            return out

        return both(one)

    def strided(k, g, z):
        return both(lambda p, c: fields[k, g, p, c, pl.ds(z, 8, stride=8)])

    def make_high_x(k, g, odds=(0, 1)):
        for odd in odds:
            value = backward(tile_link(0, 3, odd), tile(k, g, 3, odd))
            store(send_x, value, k, g, pl.ds(8 * odd, 8))

    def make_low_y(k, g):
        store(low_y, gather_y(k, g, 0, 0), k, g)

    def make_high_y(k, g):
        store(send_y, backward(face_link(face_y), gather_y(k, g, 1, 1)), k, g)

    def make_low_z(k, g):
        store(low_z, strided(k, g, 0), k, g)

    def make_high_z(k, g):
        store(send_z, backward(face_link(face_z), strided(k, g, 7)), k, g)

    def send_faces(k, g):
        face_copy(-1, 0, k, g).start()
        make_high_x(k, g)
        face_copy(1, 0, k, g).start()
        make_low_y(k, g)
        face_copy(-1, 1, k, g).start()
        make_high_y(k, g)
        face_copy(1, 1, k, g).start()
        make_low_z(k, g)
        face_copy(-1, 2, k, g).start()
        make_high_z(k, g)
        face_copy(1, 2, k, g).start()

    def send_last(g):
        k = FILTER_STEPS
        face_copy(-1, 0, k, g).start()
        make_high_x(k, g, (1,))
        face_copy(1, 0, k, g).start()
        make_low_y(k, g)
        face_copy(-1, 1, k, g).start()
        make_low_z(k, g)
        face_copy(-1, 2, k, g).start()

    def forward_hops(k, g, x, odd, here, acc):
        rolled = both(lambda p, c: pltpu.roll(here[p][c], 7, 0))
        value = forward(tile_link(2, x, odd), rolled)
        acc = value if acc is None else plus(acc, value)
        if x < 3:
            acc = plus(acc, forward(tile_link(0, x, odd), tile(k, g, x + 1, odd)))
        other = tile(k, g, x, 1 - odd)
        if odd:
            other = both(lambda p, c: lane_roll(other_of(k, g, p, c, x), 3))
        return plus(acc, forward(tile_link(1, x, odd), other))

    def other_of(k, g, p, c, x):
        return fields[k, g, p, c, rows_of(x, 0)]

    def local_pass(k, g):
        again = jnp.where(k == 0, 0.0, jnp.where(k == 1, 2.0, 1.0)).astype(f32)
        before = jnp.maximum(k - 1, 0)
        for x in range(4):
            for odd in range(2):
                here = tile(k, g, x, odd)
                old = tile(before, g, x, odd)
                acc = both(lambda p, c: SELF * here[p][c] - again * old[p][c])
                acc = forward_hops(k, g, x, odd, here, acc)
                back = backward(tile_link(2, x, odd), here)
                acc = plus(acc, both(lambda p, c: pltpu.roll(back[p][c], 1, 0)))
                if x > 0:
                    acc = plus(acc, backward(tile_link(0, x - 1, odd), tile(k, g, x - 1, odd)))
                back = backward(tile_link(1, x, 1 - odd), tile(k, g, x, 1 - odd))
                if not odd:
                    back_y = back
                    back = both(lambda p, c: lane_roll(back_y[p][c], 1))
                acc = plus(acc, back)
                store(fields, acc, k + 1, g, rows_of(x, odd))

    def forward_pass(k, g):
        for x in range(4):
            for odd in range(2):
                acc = forward_hops(k, g, x, odd, tile(k, g, x, odd), None)
                for p in range(2):
                    for c in range(3):
                        packed_hops[g, p, c, rows_of(x, odd)] = acc[p][c]

    def from_ahead_x(at, k, g, odds=(0, 1)):
        for odd in odds:
            value = forward(
                tile_link(0, 3, odd),
                both(lambda p, c: ahead_x[k, g, p, c, pl.ds(8 * odd, 8)]),
            )
            for p in range(2):
                for c in range(3):
                    ref, index = at(p, c)
                    rows = (*index, rows_of(3, odd))
                    ref[rows] = ref[rows] + value[p][c]

    def from_behind_x(at, k, g, odds=(0, 1)):
        for odd in odds:
            for p in range(2):
                for c in range(3):
                    ref, index = at(p, c)
                    rows = (*index, rows_of(0, odd))
                    ref[rows] = ref[rows] + behind_x[k, g, p, c, pl.ds(8 * odd, 8)]

    def from_ahead_yz(at, k, g):
        value = forward(face_link(face_y), both(lambda p, c: ahead_y[k, g, p, c]))
        other = forward(face_link(face_z), both(lambda p, c: ahead_z[k, g, p, c]))
        for p in range(2):
            for c in range(3):
                ref, index = at(p, c)
                for x in range(4):
                    rows = (*index, rows_of(x, 1))
                    term = jnp.where(block == 3, lane_roll(value[p][c], 3 - x), zero)
                    ref[rows] = ref[rows] + term
                rows = (*index, pl.ds(7, 8, stride=8))
                ref[rows] = ref[rows] + other[p][c]

    def from_behind_yz(at, k, g):
        for p in range(2):
            for c in range(3):
                ref, index = at(p, c)
                value = behind_y[k, g, p, c]
                for x in range(4):
                    rows = (*index, rows_of(x, 0))
                    term = jnp.where(block == 0, lane_roll(value, 4 - x), zero)
                    ref[rows] = ref[rows] + term
                rows = (*index, pl.ds(0, 8, stride=8))
                ref[rows] = ref[rows] + behind_z[k, g, p, c]

    def finish(k, g):
        at = lambda p, c: (fields, (k + 1, g, p, c))
        for axis in (2, 1):
            face_copy(-1, axis, k, g).wait()
            face_copy(1, axis, k, g).wait()
        from_ahead_yz(at, k, g)
        from_behind_yz(at, k, g)
        face_copy(-1, 0, k, g).wait()
        from_ahead_x(at, k, g)
        face_copy(1, 0, k, g).wait()
        from_behind_x(at, k, g)

    def finish_hops(g):
        k = FILTER_STEPS
        at = lambda p, c: (packed_hops, (g, p, c))
        for axis in (2, 1):
            face_copy(-1, axis, k, g).wait()
        from_ahead_yz(at, k, g)
        face_copy(-1, 0, k, g).wait()
        from_ahead_x(at, k, g, (0,))
        face_copy(1, 0, k, g).wait()
        from_behind_x(at, k, g, (1,))

    def groups(fn, begin=0, end=4):
        def body(g, carry):
            fn(g)
            return carry

        lax.fori_loop(begin, end, body, 0)

    def scatter(j, step):
        device, index = plane_mate(step)
        return pltpu.make_async_remote_copy(
            src_ref=part.at[j, index],
            dst_ref=first.at[j, step],
            send_sem=sum_sems.at[j, 0],
            recv_sem=sum_sems.at[j, 1],
            device_id=device,
            device_id_type=MESH,
        )

    def across(j, step):
        return pltpu.make_async_remote_copy(
            src_ref=second.at[j, line],
            dst_ref=second.at[j, line],
            send_sem=sum_sems.at[j, 2],
            recv_sem=sum_sems.at[j, 3],
            device_id=line_mate(step),
            device_id_type=MESH,
        )

    def gather(j, step):
        device, _ = plane_mate(step)
        return pltpu.make_async_remote_copy(
            src_ref=summed.at[j, mine],
            dst_ref=summed.at[j, mine],
            send_sem=sum_sems.at[j, 4],
            recv_sem=sum_sems.at[j, 5],
            device_id=device,
            device_id_type=MESH,
        )

    def each(fn):
        def body(step, carry):
            fn(step)
            return carry

        lax.fori_loop(1, 16, body, 0)

    def start_all(make, j):
        each(lambda step: make(j, step).start())

    def drain(j, sem):
        pieces = first.at[j, pl.ds(0, 15)]
        pltpu.make_async_copy(pieces, pieces, sum_sems.at[j, sem]).wait()

    def sum_begin(j, value):
        for piece in range(16):
            part[j, piece] = value[8 * piece : 8 * piece + 8]
        start_all(scatter, j)

    def sum_middle(j):
        first[j, 0] = part[j, mine]
        drain(j, 1)
        total = first[j, 0]
        for step in range(1, 16):
            total = total + first[j, step]
        second[j, line] = total
        start_all(across, j)

    def sum_last(j):
        drain(j, 3)
        total = second[j, 0]
        for step in range(1, 16):
            total = total + second[j, step]
        summed[j, mine] = total
        start_all(gather, j)

    def sum_end(j):
        drain(j, 5)
        return summed[j].reshape(128, 128)

    load_field.wait()
    lax.fori_loop(0, 4, pack, 0)
    load_links.wait()
    lax.fori_loop(0, 14, widen, 0, unroll=True)
    lax.fori_loop(0, 18, edges, 0, unroll=True)
    pl.semaphore_wait(barrier, 36)
    groups(lambda g: send_faces(0, g))
    groups(lambda g: local_pass(0, g))

    def turn_of(index):
        k = index // 4
        g = index % 4
        finish(k, g)
        send_faces(k + 1, g)
        local_pass(k + 1, g)

    groups(turn_of, 0, 4 * (FILTER_STEPS - 1))

    def last_turn(g):
        finish(FILTER_STEPS - 1, g)
        send_last(g)

    groups(last_turn)
    last = FILTER_STEPS
    unpack(lambda g, p, c, rows: fields[last, g, p, c, rows], plain)

    high, low = split(side_by_side(plain))
    gram = mul(high, high, SUBLANES)
    cross = mul(high, low, SUBLANES)
    gram = gram + (cross + cross.T)
    half = gram.shape[0] // 2
    sum_begin(
        0,
        packed(
            gram[:half, :half] + gram[half:, half:],
            gram[:half, half:] - gram[half:, :half],
        ),
    )

    groups(lambda g: forward_pass(last, g))
    groups(finish_hops)
    unpack(lambda g, p, c, rows: packed_hops[g, p, c, rows], hops)
    hop_high, hop_low = split(side_by_side(hops))
    proj = mul(high, hop_high, SUBLANES)
    proj = proj + mul(high, hop_low, SUBLANES)
    proj = proj + mul(low, hop_high, SUBLANES)
    proj_re = proj[:half, :half] + proj[half:, half:]
    proj_im = proj[:half, half:] - proj[half:, :half]
    sum_begin(1, packed(proj_re + proj_re.T, proj_im - proj_im.T))
    sum_middle(0)
    sum_middle(1)
    sum_last(0)
    sum_last(1)
    gram_sum = unpacked(sum_end(0)) / sites_all

    scale = jnp.sqrt(2.0 * jnp.sum(gram_sum * gram_sum, keepdims=True))
    eye = (
        lax.broadcasted_iota(jnp.int32, (2 * half, half), 0)
        == lax.broadcasted_iota(jnp.int32, (2 * half, half), 1)
    ).astype(f32)
    iterate = gram_sum / scale
    factor = 1.5 * eye - 0.5 * iterate
    iterate = product(whole_split((iterate)), halves(factor))
    result = factor

    def newton(step, carry):
        iterate, result = carry
        result_split = whole_split((result))
        factor = 1.5 * eye - 0.5 * product(result_split, halves(iterate))
        right = halves(factor)
        return (product(whole_split((iterate)), right), product(result_split, right))

    iterate, result = lax.fori_loop(1, NS_STEPS - 1, newton, (iterate, result))
    result_split = whole_split((result))
    factor = 1.5 * eye - 0.5 * product(result_split, halves(iterate))
    result = product(result_split, halves(factor))
    root = result / jnp.sqrt(scale)

    turn = jnp.concatenate(
        [
            jnp.concatenate([root[:half], root[half:]], 1),
            jnp.concatenate([-root[half:], root[:half]], 1),
        ],
        0,
    )
    turn_high, turn_low = split(turn)

    def rotate(x, carry):
        for c in range(3):
            left = jnp.concatenate([plain[0, c, x], plain[1, c, x]], 1)
            left_high, left_low = split(left)
            out = mul(left_high, turn_high) + (
                mul(left_high, turn_low) + mul(left_low, turn_high)
            )
            basis_ref[0, c, x] = out[:, :half]
            basis_ref[1, c, x] = out[:, half:]
        return carry

    lax.fori_loop(0, 4, rotate, 0, unroll=True)

    proj_sum = unpacked(sum_end(1)) / sites_all
    proj_sum = 6.0 * gram_sum + (-1.0 / HOP) * proj_sum
    root_split = whole_split((root))
    ritz = product(whole_split((proj_sum)), halves(root))
    ritz = product(root_split, halves(ritz))
    ritz_ref[...] = ritz
    for j in range(2):
        for sem in (0, 2, 4):
            drain(j, sem)


def deliver(basis_in, ritz_in, basis_out, ritz_out, sems):
    copies = [
        pltpu.make_async_copy(basis_in, basis_out, sems.at[0]),
        pltpu.make_async_copy(ritz_in, ritz_out, sems.at[1]),
    ]
    for copy in copies:
        copy.start()
    for copy in copies:
        copy.wait()


def shards(vectors, links):
    brick = vectors.shape
    sites_all = float(
        vectors.shape[2]
        * lax.axis_size("gx")
        * vectors.shape[3]
        * lax.axis_size("gy")
        * vectors.shape[4]
        * lax.axis_size("gz")
    )
    vec = vectors.reshape(2, 3, 4, 64, 128)
    link = links.reshape(54, 4, 8, 8)
    steps = FILTER_STEPS
    face_x = (steps + 1, 4, 2, 3, 16, 128)
    face = (steps + 1, 4, 2, 3, 8, 128)
    vmem = lambda *shape: pltpu.VMEM(shape, f32)
    space = pl.BlockSpec(memory_space=pltpu.VMEM)
    far = pl.BlockSpec(memory_space=pltpu.HBM)
    basis, ritz = pl.pallas_call(
        lambda *refs: whole_kernel(sites_all, *refs),
        out_shape=(
            jax.ShapeDtypeStruct(vec.shape, f32),
            jax.ShapeDtypeStruct((256, 128), f32),
        ),
        in_specs=[far, far],
        out_specs=(space, space),
        scratch_shapes=[
            vmem(*vec.shape),
            vmem(*vec.shape),
            vmem(steps + 1, 4, 2, 3, 64, 128),
            vmem(4, 2, 3, 64, 128),
            vmem(54, 64, 128),
            vmem(18, 8, 128),
            vmem(18, 8, 128),
            vmem(*face_x),
            vmem(*face),
            vmem(*face),
            vmem(*face),
            vmem(*face),
            vmem(*face_x),
            vmem(*face),
            vmem(*face),
            vmem(*face_x),
            vmem(*face),
            vmem(*face),
            vmem(2, 16, 8, 128),
            vmem(2, 16, 8, 128),
            vmem(2, 16, 8, 128),
            vmem(2, 16, 8, 128),
            vmem(*link.shape),
            pltpu.SemaphoreType.DMA((2,)),
            pltpu.SemaphoreType.DMA((4, steps + 1, 4, 3)),
            pltpu.SemaphoreType.DMA((2, 6)),
        ],
        compiler_params=pltpu.CompilerParams(
            collective_id=0, has_side_effects=True, vmem_limit_bytes=48 * 1024 * 1024
        ),
    )(
        pltpu.with_memory_space_constraint(vec, pltpu.HBM),
        pltpu.with_memory_space_constraint(link, pltpu.HBM),
    )
    basis, ritz = pl.pallas_call(
        deliver,
        out_shape=(
            jax.ShapeDtypeStruct(vec.shape, f32),
            jax.ShapeDtypeStruct((256, 128), f32),
        ),
        in_specs=[space, space],
        out_specs=(far, far),
        scratch_shapes=[pltpu.SemaphoreType.DMA((2,))],
        compiler_params=pltpu.CompilerParams(vmem_limit_bytes=4 * 1024 * 1024),
    )(basis, ritz)
    return (basis.reshape(brick), ritz.reshape(2, 128, 128))


def solution(mesh):
    return jax.shard_map(
        shards,
        mesh=mesh,
        in_specs=(
            P(None, None, "gx", "gy", "gz", None),
            P(None, None, None, None, "gx", "gy", "gz"),
        ),
        out_specs=(P(None, None, "gx", "gy", "gz", None), P()),
        check_vma=False,
    )
```

```python
import jax
import jax.numpy as jnp
from jax import lax
from jax.experimental import pallas as pl
from jax.experimental.pallas import tpu as pltpu
from jax.sharding import PartitionSpec as P

NS_STEPS = 10
FILTER_STEPS = 4

filter_low = 1.0
filter_high = 12.0

MESH = pl.DeviceIdType.MESH
HOP = -4.0 / (filter_high - filter_low)
SELF = 2.0 * (12.0 - filter_high - filter_low) / (filter_high - filter_low)
SUBLANES = ((0,), (0,))
f32 = jnp.float32
bf16 = jnp.bfloat16


def places():
    gx = lax.axis_index("gx")
    gy = lax.axis_index("gy")
    gz = lax.axis_index("gz")
    return gx, gy, gz // 2, gz % 2


def plane_mate(step):
    def offset(place):
        return jnp.where(place == 0, 2, jnp.where(place == 1, 1, jnp.where(place == 2, 3, 0)))

    gx, gy, row, core = places()
    other_y = (gy + offset(step // 4)) % 4
    other_row = (row + offset(step % 4)) % 4
    return (gx, other_y, other_row * 2 + core), other_y * 4 + other_row


def line_mate(step):
    gx, gy, row, core = places()
    place = step // 2
    offset = jnp.where(place % 2 == 0, 4 + place // 2, 4 - (place + 1) // 2)
    other_x = (gx + offset) % 8
    other_core = (core + (step + 1) % 2) % 2
    return (other_x, gy, row * 2 + other_core)


def neighbour(axis, sign):
    place = [lax.axis_index("gx"), lax.axis_index("gy"), lax.axis_index("gz")]
    count = (8, 4, 8)[axis]
    place[axis] = (place[axis] + sign + count) % count
    return tuple(place)


def forward(link, field):
    out = [[None] * 3, [None] * 3]
    for r in range(3):
        re = im = None
        for c in range(3):
            ur, ui = link[0][r][c], link[1][r][c]
            vr, vi = field[0][c], field[1][c]
            re_term = ur * vr - ui * vi
            im_term = ur * vi + ui * vr
            re = re_term if re is None else re + re_term
            im = im_term if im is None else im + im_term
        out[0][r], out[1][r] = re, im
    return out


def backward(link, field):
    out = [[None] * 3, [None] * 3]
    for r in range(3):
        re = im = None
        for c in range(3):
            ur, ui = link[0][c][r], link[1][c][r]
            vr, vi = field[0][c], field[1][c]
            re_term = ur * vr + ui * vi
            im_term = ur * vi - ui * vr
            re = re_term if re is None else re + re_term
            im = im_term if im is None else im + im_term
        out[0][r], out[1][r] = re, im
    return out


def both(fn):
    return [[fn(p, c) for c in range(3)] for p in range(2)]


def plus(left, right):
    return both(lambda p, c: left[p][c] + right[p][c])


def split(value):
    high = value.astype(bf16)
    return high, (value - high.astype(f32)).astype(bf16)


def mul(left, right, dims=((1,), (0,))):
    return lax.dot_general(left, right, (dims, ((), ())), preferred_element_type=f32)


def whole(rows):
    half = rows.shape[1] // 2
    return jnp.concatenate(
        [rows, jnp.concatenate([-rows[:, half:], rows[:, :half]], 1)], 0
    )


def whole_split(rows):
    high, low = split(rows)
    return whole(high), whole(low)


def product(left, right):
    rows = left[0].shape[0]
    out = mul(jnp.concatenate(left, 0), right[0])
    return out[:rows] + out[rows:] + mul(left[0], right[1])


def lower_mask(order, strict):
    row = lax.broadcasted_iota(jnp.int32, (order, order), 0)
    column = lax.broadcasted_iota(jnp.int32, (order, order), 1)
    return row > column if strict else row >= column


def packed(re_part, im_part):
    return jnp.where(lower_mask(re_part.shape[0], False), re_part, im_part)


def unpacked(mixed):
    zero = jnp.zeros_like(mixed)
    low = jnp.where(lower_mask(mixed.shape[0], False), mixed, zero)
    strict = jnp.where(lower_mask(mixed.shape[0], True), mixed, zero)
    high = mixed - low
    return jnp.concatenate([low + strict.T, high - high.T], 1)


def side_by_side(ref, *index):
    half = [ref[(*index, p)].reshape(-1, ref.shape[-1]) for p in range(2)]
    return jnp.concatenate(half, 1)


def transposed(tiles):
    block = lax.broadcasted_iota(jnp.int32, (8, 128), 1) // 32
    low = block < 2
    even = block % 2 == 0
    a, b, c, d = tiles
    pairs = [
        jnp.where(low, a, pltpu.roll(c, 64, 1)),
        jnp.where(low, b, pltpu.roll(d, 64, 1)),
        jnp.where(low, pltpu.roll(a, 64, 1), c),
        jnp.where(low, pltpu.roll(b, 64, 1), d),
    ]
    out = []
    for first, second in (pairs[:2], pairs[2:]):
        out.append(jnp.where(even, first, pltpu.roll(second, 32, 1)))
        out.append(jnp.where(even, pltpu.roll(first, 96, 1), second))
    return out


def lane_roll(value, blocks):
    shift = 32 * (blocks % 4)
    return value if shift == 0 else pltpu.roll(value, shift, 1)


def whole_kernel(
    sites_all,
    vec_hbm,
    link_hbm,
    plain,
    root_ref,
    summed,
    hops,
    fields,
    packed_hops,
    wide,
    face_y,
    face_z,
    send_x,
    send_y,
    send_z,
    low_y,
    low_z,
    ahead_x,
    ahead_y,
    ahead_z,
    behind_x,
    behind_y,
    behind_z,
    part,
    first,
    second,
    link_ref,
    load_sems,
    face_sems,
    sum_sems,
):
    gx, gy, row, core = places()
    mine = gy * 4 + row
    line = gx * 2 + core

    barrier = pltpu.get_barrier_semaphore()
    load_field = pltpu.make_async_copy(vec_hbm, plain, load_sems.at[0])
    load_links = pltpu.make_async_copy(link_hbm, link_ref, load_sems.at[1])
    load_links.start()
    load_field.start()
    for axis in range(3):
        for sign in (-1, 1):
            pl.semaphore_signal(
                barrier, inc=1, device_id=neighbour(axis, sign), device_id_type=MESH
            )

    def greet(step, carry):
        device, _ = plane_mate(step)
        pl.semaphore_signal(barrier, inc=1, device_id=device, device_id_type=MESH)
        pl.semaphore_signal(barrier, inc=1, device_id=line_mate(step), device_id_type=MESH)
        return carry

    lax.fori_loop(0, 15, greet, 0)

    block = lax.broadcasted_iota(jnp.int32, (8, 128), 1) // 32
    zero = jnp.zeros((8, 128), f32)

    def rows_of(x, odd):
        return pl.ds(16 * x + 8 * odd, 8)

    def widen(batch, carry):
        begin = jnp.minimum(4 * batch, 50)
        tiles = link_ref[pl.ds(begin, 4)].reshape(128, 8)
        turned = tiles.T * HOP
        for entry in range(4):
            for x in range(4):
                for odd in range(2):
                    wide[begin + entry, rows_of(x, odd)] = jnp.take_along_axis(
                        turned,
                        32 * entry + 8 * x + odd + 2 * block,
                        axis=1,
                        mode="promise_in_bounds",
                    )
        return carry

    def edges(entry, carry):
        across_y = zero
        for x in range(4):
            value = wide[18 + entry, rows_of(x, 1)]
            across_y = jnp.where(block == x, lane_roll(value, x + 1), across_y)
            wide[18 + entry, rows_of(x, 1)] = jnp.where(block == 3, zero, value)
        face_y[entry] = across_y
        face_z[entry] = wide[36 + entry, pl.ds(7, 8, stride=8)]
        wide[36 + entry, pl.ds(7, 8, stride=8)] = zero
        return carry

    def pack(x, carry):
        for p in range(2):
            for c in range(3):
                for odd in range(2):
                    tiles = transposed(
                        [plain[p, c, x, pl.ds(8 * y, 8)] * 0.5 for y in range(odd, 8, 2)]
                    )
                    rows = pl.ds(pl.multiple_of(16 * x + 8 * odd, 8), 8)
                    for g in range(4):
                        fields[0, g, p, c, rows] = tiles[g]
        return carry

    def unpack(read, target):
        def body(x, carry):
            for p in range(2):
                for c in range(3):
                    for odd in range(2):
                        rows = pl.ds(pl.multiple_of(16 * x + 8 * odd, 8), 8)
                        tiles = transposed([read(g, p, c, rows) for g in range(4)])
                        for q in range(4):
                            target[p, c, x, pl.ds(8 * (odd + 2 * q), 8)] = tiles[q]
            return carry

        lax.fori_loop(0, 4, body, 0, unroll=True)

    def tile_link(mu, x, odd):
        rows = rows_of(x, odd)
        return [
            [[wide[18 * mu + p * 9 + r * 3 + c, rows] for c in range(3)] for r in range(3)]
            for p in range(2)
        ]

    def face_link(ref):
        return [
            [[ref[p * 9 + r * 3 + c] for c in range(3)] for r in range(3)]
            for p in range(2)
        ]

    def tile(k, g, x, odd):
        return both(lambda p, c: fields[k, g, p, c, rows_of(x, odd)])

    def store(ref, value, *index):
        for p in range(2):
            for c in range(3):
                ref[(*index[:2], p, c, *index[2:])] = value[p][c]

    def face_copy(sign, axis, k, g):
        last = isinstance(k, int) and k == FILTER_STEPS
        if sign < 0:
            source, target = (
                lambda: (fields.at[k, g, :, :, pl.ds(0, 16)], ahead_x.at[k, g]),
                lambda: (low_y.at[k, g], ahead_y.at[k, g]),
                lambda: (low_z.at[k, g], ahead_z.at[k, g]),
            )[axis]()
            if last and axis == 0:
                some = pl.ds(0, 8)
                source = fields.at[k, g, :, :, some]
                target = ahead_x.at[k, g, :, :, some]
        else:
            source, target = (
                lambda: (send_x.at[k, g], behind_x.at[k, g]),
                lambda: (send_y.at[k, g], behind_y.at[k, g]),
                lambda: (send_z.at[k, g], behind_z.at[k, g]),
            )[axis]()
            if last:
                rest = pl.ds(8, 8)
                source = send_x.at[k, g, :, :, rest]
                target = behind_x.at[k, g, :, :, rest]
        side = 0 if sign < 0 else 2
        return pltpu.make_async_remote_copy(
            src_ref=source,
            dst_ref=target,
            send_sem=face_sems.at[side, k, g, axis],
            recv_sem=face_sems.at[side + 1, k, g, axis],
            device_id=neighbour(axis, sign),
            device_id_type=MESH,
        )

    def gather_y(k, g, odd, blocks):
        def one(p, c):
            out = fields[k, g, p, c, rows_of(0, odd)]
            out = lane_roll(out, blocks)
            for x in range(1, 4):
                value = lane_roll(fields[k, g, p, c, rows_of(x, odd)], blocks + x)
                out = jnp.where(block == x, value, out)
            return out

        return both(one)

    def strided(k, g, z):
        return both(lambda p, c: fields[k, g, p, c, pl.ds(z, 8, stride=8)])

    def make_high_x(k, g, odds=(0, 1)):
        for odd in odds:
            value = backward(tile_link(0, 3, odd), tile(k, g, 3, odd))
            store(send_x, value, k, g, pl.ds(8 * odd, 8))

    def make_low_y(k, g):
        store(low_y, gather_y(k, g, 0, 0), k, g)

    def make_high_y(k, g):
        store(send_y, backward(face_link(face_y), gather_y(k, g, 1, 1)), k, g)

    def make_low_z(k, g):
        store(low_z, strided(k, g, 0), k, g)

    def make_high_z(k, g):
        store(send_z, backward(face_link(face_z), strided(k, g, 7)), k, g)

    def send_faces(k, g):
        face_copy(-1, 0, k, g).start()
        make_high_x(k, g)
        face_copy(1, 0, k, g).start()
        make_low_y(k, g)
        face_copy(-1, 1, k, g).start()
        make_high_y(k, g)
        face_copy(1, 1, k, g).start()
        make_low_z(k, g)
        face_copy(-1, 2, k, g).start()
        make_high_z(k, g)
        face_copy(1, 2, k, g).start()

    def send_last(g):
        k = FILTER_STEPS
        face_copy(-1, 0, k, g).start()
        make_high_x(k, g, (1,))
        face_copy(1, 0, k, g).start()
        make_low_y(k, g)
        face_copy(-1, 1, k, g).start()
        make_low_z(k, g)
        face_copy(-1, 2, k, g).start()

    def forward_hops(k, g, x, odd, here, acc):
        rolled = both(lambda p, c: pltpu.roll(here[p][c], 7, 0))
        value = forward(tile_link(2, x, odd), rolled)
        acc = value if acc is None else plus(acc, value)
        if x < 3:
            acc = plus(acc, forward(tile_link(0, x, odd), tile(k, g, x + 1, odd)))
        other = tile(k, g, x, 1 - odd)
        if odd:
            other = both(lambda p, c: lane_roll(other_of(k, g, p, c, x), 3))
        return plus(acc, forward(tile_link(1, x, odd), other))

    def other_of(k, g, p, c, x):
        return fields[k, g, p, c, rows_of(x, 0)]

    def local_pass(k, g):
        again = jnp.where(k == 0, 0.0, jnp.where(k == 1, 2.0, 1.0)).astype(f32)
        before = jnp.maximum(k - 1, 0)
        for x in range(4):
            for odd in range(2):
                here = tile(k, g, x, odd)
                old = tile(before, g, x, odd)
                acc = both(lambda p, c: SELF * here[p][c] - again * old[p][c])
                acc = forward_hops(k, g, x, odd, here, acc)
                back = backward(tile_link(2, x, odd), here)
                acc = plus(acc, both(lambda p, c: pltpu.roll(back[p][c], 1, 0)))
                if x > 0:
                    acc = plus(acc, backward(tile_link(0, x - 1, odd), tile(k, g, x - 1, odd)))
                back = backward(tile_link(1, x, 1 - odd), tile(k, g, x, 1 - odd))
                if not odd:
                    back_y = back
                    back = both(lambda p, c: lane_roll(back_y[p][c], 1))
                acc = plus(acc, back)
                store(fields, acc, k + 1, g, rows_of(x, odd))

    def forward_pass(k, g):
        for x in range(4):
            for odd in range(2):
                acc = forward_hops(k, g, x, odd, tile(k, g, x, odd), None)
                for p in range(2):
                    for c in range(3):
                        packed_hops[g, p, c, rows_of(x, odd)] = acc[p][c]

    def from_ahead_x(at, k, g, odds=(0, 1)):
        for odd in odds:
            value = forward(
                tile_link(0, 3, odd),
                both(lambda p, c: ahead_x[k, g, p, c, pl.ds(8 * odd, 8)]),
            )
            for p in range(2):
                for c in range(3):
                    ref, index = at(p, c)
                    rows = (*index, rows_of(3, odd))
                    ref[rows] = ref[rows] + value[p][c]

    def from_behind_x(at, k, g, odds=(0, 1)):
        for odd in odds:
            for p in range(2):
                for c in range(3):
                    ref, index = at(p, c)
                    rows = (*index, rows_of(0, odd))
                    ref[rows] = ref[rows] + behind_x[k, g, p, c, pl.ds(8 * odd, 8)]

    def from_ahead_yz(at, k, g):
        value = forward(face_link(face_y), both(lambda p, c: ahead_y[k, g, p, c]))
        other = forward(face_link(face_z), both(lambda p, c: ahead_z[k, g, p, c]))
        for p in range(2):
            for c in range(3):
                ref, index = at(p, c)
                for x in range(4):
                    rows = (*index, rows_of(x, 1))
                    term = jnp.where(block == 3, lane_roll(value[p][c], 3 - x), zero)
                    ref[rows] = ref[rows] + term
                rows = (*index, pl.ds(7, 8, stride=8))
                ref[rows] = ref[rows] + other[p][c]

    def from_behind_yz(at, k, g):
        for p in range(2):
            for c in range(3):
                ref, index = at(p, c)
                value = behind_y[k, g, p, c]
                for x in range(4):
                    rows = (*index, rows_of(x, 0))
                    term = jnp.where(block == 0, lane_roll(value, 4 - x), zero)
                    ref[rows] = ref[rows] + term
                rows = (*index, pl.ds(0, 8, stride=8))
                ref[rows] = ref[rows] + behind_z[k, g, p, c]

    def finish(k, g):
        at = lambda p, c: (fields, (k + 1, g, p, c))
        for axis in (2, 1):
            face_copy(-1, axis, k, g).wait()
            face_copy(1, axis, k, g).wait()
        from_ahead_yz(at, k, g)
        from_behind_yz(at, k, g)
        face_copy(-1, 0, k, g).wait()
        from_ahead_x(at, k, g)
        face_copy(1, 0, k, g).wait()
        from_behind_x(at, k, g)

    def finish_hops(g):
        k = FILTER_STEPS
        at = lambda p, c: (packed_hops, (g, p, c))
        for axis in (2, 1):
            face_copy(-1, axis, k, g).wait()
        from_ahead_yz(at, k, g)
        face_copy(-1, 0, k, g).wait()
        from_ahead_x(at, k, g, (0,))
        face_copy(1, 0, k, g).wait()
        from_behind_x(at, k, g, (1,))

    def groups(fn, begin=0, end=4):
        def body(g, carry):
            fn(g)
            return carry

        lax.fori_loop(begin, end, body, 0)

    def scatter(j, step):
        device, index = plane_mate(step)
        return pltpu.make_async_remote_copy(
            src_ref=part.at[j, index],
            dst_ref=first.at[j, step],
            send_sem=sum_sems.at[j, 0],
            recv_sem=sum_sems.at[j, 1],
            device_id=device,
            device_id_type=MESH,
        )

    def across(j, step):
        return pltpu.make_async_remote_copy(
            src_ref=second.at[j, line],
            dst_ref=second.at[j, line],
            send_sem=sum_sems.at[j, 2],
            recv_sem=sum_sems.at[j, 3],
            device_id=line_mate(step),
            device_id_type=MESH,
        )

    def gather(j, step):
        device, _ = plane_mate(step)
        return pltpu.make_async_remote_copy(
            src_ref=summed.at[j, mine],
            dst_ref=summed.at[j, mine],
            send_sem=sum_sems.at[j, 4],
            recv_sem=sum_sems.at[j, 5],
            device_id=device,
            device_id_type=MESH,
        )

    def each(fn):
        def body(step, carry):
            fn(step)
            return carry

        lax.fori_loop(0, 15, body, 0)

    def start_all(make, j):
        each(lambda step: make(j, step).start())

    def drain(j, sem):
        pieces = first.at[j, pl.ds(0, 15)]
        pltpu.make_async_copy(pieces, pieces, sum_sems.at[j, sem]).wait()

    def sum_begin(j, value):
        for piece in range(16):
            part[j, piece] = value[8 * piece : 8 * piece + 8]
        start_all(scatter, j)

    def sum_middle(j):
        first[j, 15] = part[j, mine]
        drain(j, 1)
        total = first[j, 0]
        for step in range(1, 16):
            total = total + first[j, step]
        second[j, line] = total
        start_all(across, j)

    def sum_last(j):
        drain(j, 3)
        total = second[j, 0]
        for step in range(1, 16):
            total = total + second[j, step]
        summed[j, mine] = total
        start_all(gather, j)

    def sum_end(j):
        drain(j, 5)

    load_field.wait()
    lax.fori_loop(0, 4, pack, 0)
    load_links.wait()
    lax.fori_loop(0, 14, widen, 0, unroll=True)
    lax.fori_loop(0, 18, edges, 0, unroll=True)
    pl.semaphore_wait(barrier, 36)
    groups(lambda g: send_faces(0, g))
    groups(lambda g: local_pass(0, g))

    def turn_of(index):
        k = index // 4
        g = index % 4
        finish(k, g)
        send_faces(k + 1, g)
        local_pass(k + 1, g)

    groups(turn_of, 0, 4 * (FILTER_STEPS - 1))

    def last_turn(g):
        finish(FILTER_STEPS - 1, g)
        send_last(g)

    groups(last_turn)
    last = FILTER_STEPS
    unpack(lambda g, p, c, rows: fields[last, g, p, c, rows], plain)

    high, low = split(side_by_side(plain))
    gram = mul(high, high, SUBLANES)
    cross = mul(high, low, SUBLANES)
    half = gram.shape[0] // 2
    cross_re = cross[:half, :half] + cross[half:, half:]
    cross_im = cross[:half, half:] - cross[half:, :half]
    sum_begin(
        0,
        packed(
            gram[:half, :half] + gram[half:, half:] + (cross_re + cross_re.T),
            gram[:half, half:] - gram[half:, :half] + (cross_im - cross_im.T),
        ),
    )

    groups(lambda g: forward_pass(last, g))
    groups(finish_hops)
    unpack(lambda g, p, c, rows: packed_hops[g, p, c, rows], hops)
    hop_high, hop_low = split(side_by_side(hops))
    proj = mul(high, hop_high, SUBLANES)
    proj = proj + mul(high, hop_low, SUBLANES)
    proj = proj + mul(low, hop_high, SUBLANES)
    proj_re = proj[:half, :half] + proj[half:, half:]
    proj_im = proj[:half, half:] - proj[half:, :half]
    sum_begin(1, packed(proj_re + proj_re.T, proj_im - proj_im.T))
    sum_middle(0)
    sum_middle(1)
    sum_last(0)
    sum_last(1)
    sum_end(0)
    gram_sum = sum_of(summed, 0) / sites_all

    scale = jnp.sqrt(2.0 * jnp.sum(gram_sum * gram_sum, keepdims=True))
    eye = (
        lax.broadcasted_iota(jnp.int32, (half, 2 * half), 0)
        == lax.broadcasted_iota(jnp.int32, (half, 2 * half), 1)
    ).astype(f32)
    iterate = gram_sum / scale
    factor = 1.5 * eye - 0.5 * iterate
    iterate = product(split(iterate), whole_split(factor))
    result = factor

    def newton(step, carry):
        iterate, result = carry
        result_split = split(result)
        factor = 1.5 * eye - 0.5 * product(result_split, whole_split(iterate))
        right = whole_split(factor)
        return (product(split(iterate), right), product(result_split, right))

    iterate, result = lax.fori_loop(1, NS_STEPS - 1, newton, (iterate, result))
    result_split = split(result)
    factor = 1.5 * eye - 0.5 * product(result_split, whole_split(iterate))
    root_ref[...] = product(result_split, whole_split(factor)) / jnp.sqrt(scale)
    sum_end(1)
    for j in range(2):
        for sem in (0, 2, 4):
            drain(j, sem)


def sum_of(summed, j):
    return unpacked(summed[j].reshape(128, 128))


def rotate_kernel(
    sites_all, plain, root_ref, summed, basis_ref, ritz_ref, turned, ritz_rows, sems
):
    root = root_ref[...]
    half = root.shape[0]
    right = whole_split(root)
    copies = []
    for c in range(3):
        left = jnp.concatenate([plain[p, c].reshape(-1, half) for p in range(2)], 1)
        out = product(split(left), right)
        for p in range(2):
            turned[p, c] = out[:, p * half : (p + 1) * half].reshape(turned.shape[2:])
            copy = pltpu.make_async_copy(turned.at[p, c], basis_ref.at[p, c], sems.at[p, c])
            copy.start()
            copies.append(copy)
    gram_sum = sum_of(summed, 0) / sites_all
    proj_sum = 6.0 * gram_sum + (-1.0 / HOP) * (sum_of(summed, 1) / sites_all)
    ritz = product(split(proj_sum), right)
    ritz = product(split(root), whole_split(ritz))
    for p in range(2):
        ritz_rows[p] = ritz[:, p * half : (p + 1) * half]
    copy = pltpu.make_async_copy(ritz_rows, ritz_ref, sems.at[0, 3])
    copy.start()
    copies.append(copy)
    for copy in copies:
        copy.wait()


def shards(vectors, links):
    brick = vectors.shape
    sites_all = float(
        vectors.shape[2]
        * lax.axis_size("gx")
        * vectors.shape[3]
        * lax.axis_size("gy")
        * vectors.shape[4]
        * lax.axis_size("gz")
    )
    vec = vectors.reshape(2, 3, 4, 64, 128)
    link = links.reshape(54, 4, 8, 8)
    steps = FILTER_STEPS
    face_x = (steps + 1, 4, 2, 3, 16, 128)
    face = (steps + 1, 4, 2, 3, 8, 128)
    vmem = lambda *shape: pltpu.VMEM(shape, f32)
    space = pl.BlockSpec(memory_space=pltpu.VMEM)
    far = pl.BlockSpec(memory_space=pltpu.HBM)
    field, root, sums = pl.pallas_call(
        lambda *refs: whole_kernel(sites_all, *refs),
        out_shape=(
            jax.ShapeDtypeStruct(vec.shape, f32),
            jax.ShapeDtypeStruct((128, 256), f32),
            jax.ShapeDtypeStruct((2, 16, 8, 128), f32),
        ),
        in_specs=[far, far],
        out_specs=(space, space, space),
        scratch_shapes=[
            vmem(*vec.shape),
            vmem(steps + 1, 4, 2, 3, 64, 128),
            vmem(4, 2, 3, 64, 128),
            vmem(54, 64, 128),
            vmem(18, 8, 128),
            vmem(18, 8, 128),
            vmem(*face_x),
            vmem(*face),
            vmem(*face),
            vmem(*face),
            vmem(*face),
            vmem(*face_x),
            vmem(*face),
            vmem(*face),
            vmem(*face_x),
            vmem(*face),
            vmem(*face),
            vmem(2, 16, 8, 128),
            vmem(2, 16, 8, 128),
            vmem(2, 16, 8, 128),
            vmem(*link.shape),
            pltpu.SemaphoreType.DMA((2,)),
            pltpu.SemaphoreType.DMA((4, steps + 1, 4, 3)),
            pltpu.SemaphoreType.DMA((2, 6)),
        ],
        compiler_params=pltpu.CompilerParams(
            collective_id=0, has_side_effects=True, vmem_limit_bytes=48 * 1024 * 1024
        ),
    )(
        pltpu.with_memory_space_constraint(vec, pltpu.HBM),
        pltpu.with_memory_space_constraint(link, pltpu.HBM),
    )
    basis, ritz = pl.pallas_call(
        lambda *refs: rotate_kernel(sites_all, *refs),
        out_shape=(
            jax.ShapeDtypeStruct(vec.shape, f32),
            jax.ShapeDtypeStruct((2, 128, 128), f32),
        ),
        in_specs=[space, space, space],
        out_specs=(far, far),
        scratch_shapes=[
            vmem(*vec.shape),
            vmem(2, 128, 128),
            pltpu.SemaphoreType.DMA((2, 4)),
        ],
        compiler_params=pltpu.CompilerParams(vmem_limit_bytes=8 * 1024 * 1024),
    )(field, root, sums)
    return (basis.reshape(brick), ritz)


def solution(mesh):
    return jax.shard_map(
        shards,
        mesh=mesh,
        in_specs=(
            P(None, None, "gx", "gy", "gz", None),
            P(None, None, None, None, "gx", "gy", "gz"),
        ),
        out_specs=(P(None, None, "gx", "gy", "gz", None), P()),
        check_vma=False,
    )
```

```python
import jax
import jax.numpy as jnp
from jax import lax
from jax.experimental import pallas as pl
from jax.experimental.pallas import tpu as pltpu
from jax.sharding import PartitionSpec as P

NS_STEPS = 10
FILTER_STEPS = 4

filter_low = 1.0
filter_high = 12.0

MESH = pl.DeviceIdType.MESH
HOP = -4.0 / (filter_high - filter_low)
SELF = 2.0 * (12.0 - filter_high - filter_low) / (filter_high - filter_low)
SUBLANES = ((0,), (0,))
f32 = jnp.float32
bf16 = jnp.bfloat16


def places():
    gx = lax.axis_index("gx")
    gy = lax.axis_index("gy")
    gz = lax.axis_index("gz")
    return gx, gy, gz // 2, gz % 2


def plane_mate(step):
    def offset(place):
        return jnp.where(place == 0, 2, jnp.where(place == 1, 1, jnp.where(place == 2, 3, 0)))

    gx, gy, row, core = places()
    other_y = (gy + offset(step // 4)) % 4
    other_row = (row + offset(step % 4)) % 4
    return (gx, other_y, other_row * 2 + core), other_y * 4 + other_row


def line_mate(step):
    gx, gy, row, core = places()
    place = step // 2
    offset = jnp.where(place % 2 == 0, 4 + place // 2, 4 - (place + 1) // 2)
    other_x = (gx + offset) % 8
    other_core = (core + (step + 1) % 2) % 2
    return (other_x, gy, row * 2 + other_core)


def neighbour(axis, sign):
    place = [lax.axis_index("gx"), lax.axis_index("gy"), lax.axis_index("gz")]
    count = (8, 4, 8)[axis]
    place[axis] = (place[axis] + sign + count) % count
    return tuple(place)


def forward(link, field):
    out = [[None] * 3, [None] * 3]
    for r in range(3):
        re = im = None
        for c in range(3):
            ur, ui = link[0][r][c], link[1][r][c]
            vr, vi = field[0][c], field[1][c]
            re_term = ur * vr - ui * vi
            im_term = ur * vi + ui * vr
            re = re_term if re is None else re + re_term
            im = im_term if im is None else im + im_term
        out[0][r], out[1][r] = re, im
    return out


def backward(link, field):
    out = [[None] * 3, [None] * 3]
    for r in range(3):
        re = im = None
        for c in range(3):
            ur, ui = link[0][c][r], link[1][c][r]
            vr, vi = field[0][c], field[1][c]
            re_term = ur * vr + ui * vi
            im_term = ur * vi - ui * vr
            re = re_term if re is None else re + re_term
            im = im_term if im is None else im + im_term
        out[0][r], out[1][r] = re, im
    return out


def both(fn):
    return [[fn(p, c) for c in range(3)] for p in range(2)]


def plus(left, right):
    return both(lambda p, c: left[p][c] + right[p][c])


def split(value):
    high = value.astype(bf16)
    return high, (value - high.astype(f32)).astype(bf16)


def mul(left, right, dims=((1,), (0,))):
    return lax.dot_general(left, right, (dims, ((), ())), preferred_element_type=f32)


def whole(rows):
    half = rows.shape[1] // 2
    return jnp.concatenate(
        [rows, jnp.concatenate([-rows[:, half:], rows[:, :half]], 1)], 0
    )


def whole_split(rows):
    high, low = split(rows)
    return whole(high), whole(low)


def product(left, right):
    rows = left[0].shape[0]
    out = mul(jnp.concatenate(left, 0), right[0])
    return out[:rows] + out[rows:] + mul(left[0], right[1])


def lower_mask(order, strict):
    row = lax.broadcasted_iota(jnp.int32, (order, order), 0)
    column = lax.broadcasted_iota(jnp.int32, (order, order), 1)
    return row > column if strict else row >= column


def packed(re_part, im_part):
    return jnp.where(lower_mask(re_part.shape[0], False), re_part, im_part)


def unpacked(mixed):
    zero = jnp.zeros_like(mixed)
    low = jnp.where(lower_mask(mixed.shape[0], False), mixed, zero)
    strict = jnp.where(lower_mask(mixed.shape[0], True), mixed, zero)
    high = mixed - low
    return jnp.concatenate([low + strict.T, high - high.T], 1)


def side_by_side(ref, *index):
    half = [ref[(*index, p)].reshape(-1, ref.shape[-1]) for p in range(2)]
    return jnp.concatenate(half, 1)


def transposed(tiles):
    block = lax.broadcasted_iota(jnp.int32, (8, 128), 1) // 32
    low = block < 2
    even = block % 2 == 0
    a, b, c, d = tiles
    pairs = [
        jnp.where(low, a, pltpu.roll(c, 64, 1)),
        jnp.where(low, b, pltpu.roll(d, 64, 1)),
        jnp.where(low, pltpu.roll(a, 64, 1), c),
        jnp.where(low, pltpu.roll(b, 64, 1), d),
    ]
    out = []
    for first, second in (pairs[:2], pairs[2:]):
        out.append(jnp.where(even, first, pltpu.roll(second, 32, 1)))
        out.append(jnp.where(even, pltpu.roll(first, 96, 1), second))
    return out


def lane_roll(value, blocks):
    shift = 32 * (blocks % 4)
    return value if shift == 0 else pltpu.roll(value, shift, 1)


def whole_kernel(
    sites_all,
    vec_hbm,
    link_hbm,
    plain,
    root_ref,
    summed,
    hops,
    fields,
    packed_hops,
    wide,
    face_y,
    face_z,
    send_x,
    send_y,
    send_z,
    low_y,
    low_z,
    ahead_x,
    ahead_y,
    ahead_z,
    behind_x,
    behind_y,
    behind_z,
    part,
    first,
    second,
    link_ref,
    load_sems,
    face_sems,
    sent_sems,
    sum_sems,
):
    gx, gy, row, core = places()
    mine = gy * 4 + row
    line = gx * 2 + core

    barrier = pltpu.get_barrier_semaphore()
    load_field = pltpu.make_async_copy(vec_hbm, plain, load_sems.at[0])
    load_links = pltpu.make_async_copy(link_hbm, link_ref, load_sems.at[1])
    load_links.start()
    load_field.start()
    for axis in range(3):
        for sign in (-1, 1):
            pl.semaphore_signal(
                barrier, inc=1, device_id=neighbour(axis, sign), device_id_type=MESH
            )

    def greet(step, carry):
        device, _ = plane_mate(step)
        pl.semaphore_signal(barrier, inc=1, device_id=device, device_id_type=MESH)
        pl.semaphore_signal(barrier, inc=1, device_id=line_mate(step), device_id_type=MESH)
        return carry

    lax.fori_loop(0, 15, greet, 0)

    block = lax.broadcasted_iota(jnp.int32, (8, 128), 1) // 32
    zero = jnp.zeros((8, 128), f32)

    def rows_of(x, odd):
        return pl.ds(16 * x + 8 * odd, 8)

    def widen(batch, carry):
        begin = jnp.minimum(4 * batch, 50)
        tiles = link_ref[pl.ds(begin, 4)].reshape(128, 8)
        turned = tiles.T * HOP
        for entry in range(4):
            for x in range(4):
                for odd in range(2):
                    wide[begin + entry, rows_of(x, odd)] = jnp.take_along_axis(
                        turned,
                        32 * entry + 8 * x + odd + 2 * block,
                        axis=1,
                        mode="promise_in_bounds",
                    )
        return carry

    def edges(entry, carry):
        across_y = zero
        for x in range(4):
            value = wide[18 + entry, rows_of(x, 1)]
            across_y = jnp.where(block == x, lane_roll(value, x + 1), across_y)
            wide[18 + entry, rows_of(x, 1)] = jnp.where(block == 3, zero, value)
        face_y[entry] = across_y
        face_z[entry] = wide[36 + entry, pl.ds(7, 8, stride=8)]
        wide[36 + entry, pl.ds(7, 8, stride=8)] = zero
        return carry

    def pack(x, carry):
        for p in range(2):
            for c in range(3):
                for odd in range(2):
                    tiles = transposed(
                        [plain[p, c, x, pl.ds(8 * y, 8)] * 0.5 for y in range(odd, 8, 2)]
                    )
                    rows = pl.ds(pl.multiple_of(16 * x + 8 * odd, 8), 8)
                    for g in range(4):
                        fields[0, g, p, c, rows] = tiles[g]
        return carry

    def unpack(read, target):
        def body(x, carry):
            for p in range(2):
                for c in range(3):
                    for odd in range(2):
                        rows = pl.ds(pl.multiple_of(16 * x + 8 * odd, 8), 8)
                        tiles = transposed([read(g, p, c, rows) for g in range(4)])
                        for q in range(4):
                            target[p, c, x, pl.ds(8 * (odd + 2 * q), 8)] = tiles[q]
            return carry

        lax.fori_loop(0, 4, body, 0, unroll=True)

    def tile_link(mu, x, odd):
        rows = rows_of(x, odd)
        return [
            [[wide[18 * mu + p * 9 + r * 3 + c, rows] for c in range(3)] for r in range(3)]
            for p in range(2)
        ]

    def face_link(ref):
        return [
            [[ref[p * 9 + r * 3 + c] for c in range(3)] for r in range(3)]
            for p in range(2)
        ]

    def tile(k, g, x, odd):
        return both(lambda p, c: fields[k, g, p, c, rows_of(x, odd)])

    def store(ref, value, *index):
        for p in range(2):
            for c in range(3):
                ref[(*index[:2], p, c, *index[2:])] = value[p][c]

    def await_bytes(ref, sem):
        pltpu.make_async_copy(ref, ref, sem).wait()

    def face_copy(sign, axis, k, g):
        last = isinstance(k, int) and k == FILTER_STEPS
        if sign < 0:
            source, target = (
                lambda: (fields.at[k, g, :, :, pl.ds(0, 16)], ahead_x.at[k, g]),
                lambda: (low_y.at[k, g], ahead_y.at[k, g]),
                lambda: (low_z.at[k, g], ahead_z.at[k, g]),
            )[axis]()
            if last and axis == 0:
                some = pl.ds(0, 8)
                source = fields.at[k, g, :, :, some]
                target = ahead_x.at[k, g, :, :, some]
        else:
            source, target = (
                lambda: (send_x.at[k, g], behind_x.at[k, g]),
                lambda: (send_y.at[k, g], behind_y.at[k, g]),
                lambda: (send_z.at[k, g], behind_z.at[k, g]),
            )[axis]()
            if last:
                rest = pl.ds(8, 8)
                source = send_x.at[k, g, :, :, rest]
                target = behind_x.at[k, g, :, :, rest]
        side = 0 if sign < 0 else 1
        return pltpu.make_async_remote_copy(
            src_ref=source,
            dst_ref=target,
            send_sem=sent_sems.at[6 if last else 2 * axis + side],
            recv_sem=face_sems.at[0 if axis == 0 else 1, k, g],
            device_id=neighbour(axis, sign),
            device_id_type=MESH,
        )

    def gather_y(k, g, odd, blocks):
        def one(p, c):
            out = fields[k, g, p, c, rows_of(0, odd)]
            out = lane_roll(out, blocks)
            for x in range(1, 4):
                value = lane_roll(fields[k, g, p, c, rows_of(x, odd)], blocks + x)
                out = jnp.where(block == x, value, out)
            return out

        return both(one)

    def strided(k, g, z):
        return both(lambda p, c: fields[k, g, p, c, pl.ds(z, 8, stride=8)])

    def make_high_x(k, g, odds=(0, 1)):
        for odd in odds:
            value = backward(tile_link(0, 3, odd), tile(k, g, 3, odd))
            store(send_x, value, k, g, pl.ds(8 * odd, 8))

    def make_low_y(k, g):
        store(low_y, gather_y(k, g, 0, 0), k, g)

    def make_high_y(k, g):
        store(send_y, backward(face_link(face_y), gather_y(k, g, 1, 1)), k, g)

    def make_low_z(k, g):
        store(low_z, strided(k, g, 0), k, g)

    def make_high_z(k, g):
        store(send_z, backward(face_link(face_z), strided(k, g, 7)), k, g)

    def send_faces(k, g):
        face_copy(-1, 0, k, g).start()
        make_high_x(k, g)
        face_copy(1, 0, k, g).start()
        make_low_y(k, g)
        face_copy(-1, 1, k, g).start()
        make_high_y(k, g)
        face_copy(1, 1, k, g).start()
        make_low_z(k, g)
        face_copy(-1, 2, k, g).start()
        make_high_z(k, g)
        face_copy(1, 2, k, g).start()

    def send_last(g):
        k = FILTER_STEPS
        face_copy(-1, 0, k, g).start()
        make_high_x(k, g, (1,))
        face_copy(1, 0, k, g).start()
        make_low_y(k, g)
        face_copy(-1, 1, k, g).start()
        make_low_z(k, g)
        face_copy(-1, 2, k, g).start()

    def forward_hops(k, g, x, odd, here, acc):
        rolled = both(lambda p, c: pltpu.roll(here[p][c], 7, 0))
        value = forward(tile_link(2, x, odd), rolled)
        acc = value if acc is None else plus(acc, value)
        if x < 3:
            acc = plus(acc, forward(tile_link(0, x, odd), tile(k, g, x + 1, odd)))
        other = tile(k, g, x, 1 - odd)
        if odd:
            other = both(lambda p, c: lane_roll(other_of(k, g, p, c, x), 3))
        return plus(acc, forward(tile_link(1, x, odd), other))

    def other_of(k, g, p, c, x):
        return fields[k, g, p, c, rows_of(x, 0)]

    def local_pass(k, g):
        again = jnp.where(k == 0, 0.0, jnp.where(k == 1, 2.0, 1.0)).astype(f32)
        before = jnp.maximum(k - 1, 0)
        for x in range(4):
            for odd in range(2):
                here = tile(k, g, x, odd)
                old = tile(before, g, x, odd)
                acc = both(lambda p, c: SELF * here[p][c] - again * old[p][c])
                acc = forward_hops(k, g, x, odd, here, acc)
                back = backward(tile_link(2, x, odd), here)
                acc = plus(acc, both(lambda p, c: pltpu.roll(back[p][c], 1, 0)))
                if x > 0:
                    acc = plus(acc, backward(tile_link(0, x - 1, odd), tile(k, g, x - 1, odd)))
                back = backward(tile_link(1, x, 1 - odd), tile(k, g, x, 1 - odd))
                if not odd:
                    back_y = back
                    back = both(lambda p, c: lane_roll(back_y[p][c], 1))
                acc = plus(acc, back)
                store(fields, acc, k + 1, g, rows_of(x, odd))

    def forward_pass(k, g):
        for x in range(4):
            for odd in range(2):
                acc = forward_hops(k, g, x, odd, tile(k, g, x, odd), None)
                for p in range(2):
                    for c in range(3):
                        packed_hops[g, p, c, rows_of(x, odd)] = acc[p][c]

    def from_ahead_x(at, k, g, odds=(0, 1)):
        for odd in odds:
            value = forward(
                tile_link(0, 3, odd),
                both(lambda p, c: ahead_x[k, g, p, c, pl.ds(8 * odd, 8)]),
            )
            for p in range(2):
                for c in range(3):
                    ref, index = at(p, c)
                    rows = (*index, rows_of(3, odd))
                    ref[rows] = ref[rows] + value[p][c]

    def from_behind_x(at, k, g, odds=(0, 1)):
        for odd in odds:
            for p in range(2):
                for c in range(3):
                    ref, index = at(p, c)
                    rows = (*index, rows_of(0, odd))
                    ref[rows] = ref[rows] + behind_x[k, g, p, c, pl.ds(8 * odd, 8)]

    def from_ahead_yz(at, k, g):
        value = forward(face_link(face_y), both(lambda p, c: ahead_y[k, g, p, c]))
        other = forward(face_link(face_z), both(lambda p, c: ahead_z[k, g, p, c]))
        for p in range(2):
            for c in range(3):
                ref, index = at(p, c)
                for x in range(4):
                    rows = (*index, rows_of(x, 1))
                    term = jnp.where(block == 3, lane_roll(value[p][c], 3 - x), zero)
                    ref[rows] = ref[rows] + term
                rows = (*index, pl.ds(7, 8, stride=8))
                ref[rows] = ref[rows] + other[p][c]

    def from_behind_yz(at, k, g):
        for p in range(2):
            for c in range(3):
                ref, index = at(p, c)
                value = behind_y[k, g, p, c]
                for x in range(4):
                    rows = (*index, rows_of(x, 0))
                    term = jnp.where(block == 0, lane_roll(value, 4 - x), zero)
                    ref[rows] = ref[rows] + term
                rows = (*index, pl.ds(0, 8, stride=8))
                ref[rows] = ref[rows] + behind_z[k, g, p, c]

    def finish(k, g):
        at = lambda p, c: (fields, (k + 1, g, p, c))
        await_bytes(ahead_y.at[k], face_sems.at[1, k, g])
        from_ahead_yz(at, k, g)
        from_behind_yz(at, k, g)
        await_bytes(ahead_x.at[k, pl.ds(0, 2)], face_sems.at[0, k, g])
        from_behind_x(at, k, g)
        from_ahead_x(at, k, g)

    def finish_hops(g):
        k = FILTER_STEPS
        at = lambda p, c: (packed_hops, (g, p, c))
        await_bytes(ahead_y.at[k, pl.ds(0, 2)], face_sems.at[1, k, g])
        from_ahead_yz(at, k, g)
        await_bytes(ahead_y.at[k, pl.ds(0, 2)], face_sems.at[0, k, g])
        from_ahead_x(at, k, g, (0,))
        from_behind_x(at, k, g, (1,))

    def groups(fn, begin=0, end=4):
        def body(g, carry):
            fn(g)
            return carry

        lax.fori_loop(begin, end, body, 0)

    def scatter(j, step):
        device, index = plane_mate(step)
        return pltpu.make_async_remote_copy(
            src_ref=part.at[j, index],
            dst_ref=first.at[j, step],
            send_sem=sum_sems.at[j, 0],
            recv_sem=sum_sems.at[j, 1],
            device_id=device,
            device_id_type=MESH,
        )

    def across(j, step):
        return pltpu.make_async_remote_copy(
            src_ref=second.at[j, line],
            dst_ref=second.at[j, line],
            send_sem=sum_sems.at[j, 2],
            recv_sem=sum_sems.at[j, 3],
            device_id=line_mate(step),
            device_id_type=MESH,
        )

    def gather(j, step):
        device, _ = plane_mate(step)
        return pltpu.make_async_remote_copy(
            src_ref=summed.at[j, mine],
            dst_ref=summed.at[j, mine],
            send_sem=sum_sems.at[j, 4],
            recv_sem=sum_sems.at[j, 5],
            device_id=device,
            device_id_type=MESH,
        )

    def each(fn):
        def body(step, carry):
            fn(step)
            return carry

        lax.fori_loop(0, 15, body, 0)

    def start_all(make, j):
        each(lambda step: make(j, step).start())

    def drain(j, sem):
        pieces = first.at[j, pl.ds(0, 15)]
        pltpu.make_async_copy(pieces, pieces, sum_sems.at[j, sem]).wait()

    def sum_begin(j, value):
        for piece in range(16):
            part[j, piece] = value[8 * piece : 8 * piece + 8]
        start_all(scatter, j)

    def sum_middle(j):
        first[j, 15] = part[j, mine]
        drain(j, 1)
        total = first[j, 0]
        for step in range(1, 16):
            total = total + first[j, step]
        second[j, line] = total
        start_all(across, j)

    def sum_last(j):
        drain(j, 3)
        total = second[j, 0]
        for step in range(1, 16):
            total = total + second[j, step]
        summed[j, mine] = total
        start_all(gather, j)

    def sum_end(j):
        drain(j, 5)

    load_field.wait()
    lax.fori_loop(0, 4, pack, 0)
    load_links.wait()
    lax.fori_loop(0, 14, widen, 0, unroll=True)
    lax.fori_loop(0, 18, edges, 0, unroll=True)
    pl.semaphore_wait(barrier, 36)
    groups(lambda g: send_faces(0, g))
    groups(lambda g: local_pass(0, g))

    def turn_of(index):
        k = index // 4
        g = index % 4
        finish(k, g)
        send_faces(k + 1, g)
        local_pass(k + 1, g)

    groups(turn_of, 0, 4 * (FILTER_STEPS - 1))

    def last_turn(g):
        finish(FILTER_STEPS - 1, g)
        send_last(g)

    groups(last_turn)
    last = FILTER_STEPS
    unpack(lambda g, p, c, rows: fields[last, g, p, c, rows], plain)

    high, low = split(side_by_side(plain))
    gram = mul(high, high, SUBLANES)
    cross = mul(high, low, SUBLANES)
    half = gram.shape[0] // 2
    cross_re = cross[:half, :half] + cross[half:, half:]
    cross_im = cross[:half, half:] - cross[half:, :half]
    sum_begin(
        0,
        packed(
            gram[:half, :half] + gram[half:, half:] + (cross_re + cross_re.T),
            gram[:half, half:] - gram[half:, :half] + (cross_im - cross_im.T),
        ),
    )

    groups(lambda g: forward_pass(last, g))
    groups(finish_hops)
    unpack(lambda g, p, c, rows: packed_hops[g, p, c, rows], hops)
    hop_high, hop_low = split(side_by_side(hops))
    proj = mul(high, hop_high, SUBLANES)
    proj = proj + mul(high, hop_low, SUBLANES)
    proj = proj + mul(low, hop_high, SUBLANES)
    proj_re = proj[:half, :half] + proj[half:, half:]
    proj_im = proj[:half, half:] - proj[half:, :half]
    sum_begin(1, packed(proj_re + proj_re.T, proj_im - proj_im.T))
    sum_middle(0)
    sum_middle(1)
    sum_last(0)
    sum_last(1)
    sum_end(0)
    gram_sum = sum_of(summed, 0) / sites_all

    scale = jnp.sqrt(2.0 * jnp.sum(gram_sum * gram_sum, keepdims=True))
    eye = (
        lax.broadcasted_iota(jnp.int32, (half, 2 * half), 0)
        == lax.broadcasted_iota(jnp.int32, (half, 2 * half), 1)
    ).astype(f32)
    iterate = gram_sum / scale
    factor = 1.5 * eye - 0.5 * iterate
    iterate = product(split(iterate), whole_split(factor))
    result = factor

    def newton(step, carry):
        iterate, result = carry
        result_split = split(result)
        factor = 1.5 * eye - 0.5 * product(result_split, whole_split(iterate))
        right = whole_split(factor)
        return (product(split(iterate), right), product(result_split, right))

    iterate, result = lax.fori_loop(1, NS_STEPS - 1, newton, (iterate, result))
    result_split = split(result)
    factor = 1.5 * eye - 0.5 * product(result_split, whole_split(iterate))
    root_ref[...] = product(result_split, whole_split(factor)) / jnp.sqrt(scale)
    sum_end(1)
    early = pl.ds(0, FILTER_STEPS)
    for index, ref in enumerate((send_x, send_x, send_y, send_y, send_z, send_z, send_y)):
        await_bytes(ref.at[early], sent_sems.at[index])
    for j in range(2):
        for sem in (0, 2, 4):
            drain(j, sem)


def sum_of(summed, j):
    return unpacked(summed[j].reshape(128, 128))


def rotate_kernel(
    sites_all, plain, root_ref, summed, basis_ref, ritz_ref, turned, ritz_rows, sems
):
    root = root_ref[...]
    half = root.shape[0]
    right = whole_split(root)
    copies = []
    for c in range(3):
        left = jnp.concatenate([plain[p, c].reshape(-1, half) for p in range(2)], 1)
        out = product(split(left), right)
        for p in range(2):
            turned[p, c] = out[:, p * half : (p + 1) * half].reshape(turned.shape[2:])
            copy = pltpu.make_async_copy(turned.at[p, c], basis_ref.at[p, c], sems.at[p, c])
            copy.start()
            copies.append(copy)
    gram_sum = sum_of(summed, 0) / sites_all
    proj_sum = 6.0 * gram_sum + (-1.0 / HOP) * (sum_of(summed, 1) / sites_all)
    ritz = product(split(proj_sum), right)
    ritz = product(split(root), whole_split(ritz))
    for p in range(2):
        ritz_rows[p] = ritz[:, p * half : (p + 1) * half]
    copy = pltpu.make_async_copy(ritz_rows, ritz_ref, sems.at[0, 3])
    copy.start()
    copies.append(copy)
    for copy in copies:
        copy.wait()


def shards(vectors, links):
    brick = vectors.shape
    sites_all = float(
        vectors.shape[2]
        * lax.axis_size("gx")
        * vectors.shape[3]
        * lax.axis_size("gy")
        * vectors.shape[4]
        * lax.axis_size("gz")
    )
    vec = vectors.reshape(2, 3, 4, 64, 128)
    link = links.reshape(54, 4, 8, 8)
    steps = FILTER_STEPS
    face_x = (steps + 1, 4, 2, 3, 16, 128)
    face = (steps + 1, 4, 2, 3, 8, 128)
    vmem = lambda *shape: pltpu.VMEM(shape, f32)
    space = pl.BlockSpec(memory_space=pltpu.VMEM)
    far = pl.BlockSpec(memory_space=pltpu.HBM)
    field, root, sums = pl.pallas_call(
        lambda *refs: whole_kernel(sites_all, *refs),
        out_shape=(
            jax.ShapeDtypeStruct(vec.shape, f32),
            jax.ShapeDtypeStruct((128, 256), f32),
            jax.ShapeDtypeStruct((2, 16, 8, 128), f32),
        ),
        in_specs=[far, far],
        out_specs=(space, space, space),
        scratch_shapes=[
            vmem(*vec.shape),
            vmem(steps + 1, 4, 2, 3, 64, 128),
            vmem(4, 2, 3, 64, 128),
            vmem(54, 64, 128),
            vmem(18, 8, 128),
            vmem(18, 8, 128),
            vmem(*face_x),
            vmem(*face),
            vmem(*face),
            vmem(*face),
            vmem(*face),
            vmem(*face_x),
            vmem(*face),
            vmem(*face),
            vmem(*face_x),
            vmem(*face),
            vmem(*face),
            vmem(2, 16, 8, 128),
            vmem(2, 16, 8, 128),
            vmem(2, 16, 8, 128),
            vmem(*link.shape),
            pltpu.SemaphoreType.DMA((2,)),
            pltpu.SemaphoreType.DMA((2, steps + 1, 4)),
            pltpu.SemaphoreType.DMA((7,)),
            pltpu.SemaphoreType.DMA((2, 6)),
        ],
        compiler_params=pltpu.CompilerParams(
            collective_id=0, has_side_effects=True, vmem_limit_bytes=48 * 1024 * 1024
        ),
    )(
        pltpu.with_memory_space_constraint(vec, pltpu.HBM),
        pltpu.with_memory_space_constraint(link, pltpu.HBM),
    )
    basis, ritz = pl.pallas_call(
        lambda *refs: rotate_kernel(sites_all, *refs),
        out_shape=(
            jax.ShapeDtypeStruct(vec.shape, f32),
            jax.ShapeDtypeStruct((2, 128, 128), f32),
        ),
        in_specs=[space, space, space],
        out_specs=(far, far),
        scratch_shapes=[
            vmem(*vec.shape),
            vmem(2, 128, 128),
            pltpu.SemaphoreType.DMA((2, 4)),
        ],
        compiler_params=pltpu.CompilerParams(vmem_limit_bytes=8 * 1024 * 1024),
    )(field, root, sums)
    return (basis.reshape(brick), ritz)


def solution(mesh):
    return jax.shard_map(
        shards,
        mesh=mesh,
        in_specs=(
            P(None, None, "gx", "gy", "gz", None),
            P(None, None, None, None, "gx", "gy", "gz"),
        ),
        out_specs=(P(None, None, "gx", "gy", "gz", None), P()),
        check_vma=False,
    )
```

```python
import jax
import jax.numpy as jnp
from jax import lax
from jax.experimental import pallas as pl
from jax.experimental.pallas import tpu as pltpu
from jax.sharding import PartitionSpec as P

NS_STEPS = 10
FILTER_STEPS = 4

filter_low = 1.0
filter_high = 12.0

MESH = pl.DeviceIdType.MESH
HOP = -4.0 / (filter_high - filter_low)
SELF = 2.0 * (12.0 - filter_high - filter_low) / (filter_high - filter_low)
SUBLANES = ((0,), (0,))
f32 = jnp.float32
bf16 = jnp.bfloat16


def places():
    gx = lax.axis_index("gx")
    gy = lax.axis_index("gy")
    gz = lax.axis_index("gz")
    return gx, gy, gz // 2, gz % 2


def plane_mate(step):
    def offset(place):
        return jnp.where(place == 0, 2, jnp.where(place == 1, 1, jnp.where(place == 2, 3, 0)))

    gx, gy, row, core = places()
    other_y = (gy + offset(step // 4)) % 4
    other_row = (row + offset(step % 4)) % 4
    return (gx, other_y, other_row * 2 + core), other_y * 4 + other_row


def line_mate(step):
    gx, gy, row, core = places()
    place = step // 2
    offset = jnp.where(place % 2 == 0, 4 + place // 2, 4 - (place + 1) // 2)
    other_x = (gx + offset) % 8
    other_core = (core + (step + 1) % 2) % 2
    return (other_x, gy, row * 2 + other_core)


def neighbour(axis, sign):
    place = [lax.axis_index("gx"), lax.axis_index("gy"), lax.axis_index("gz")]
    count = (8, 4, 8)[axis]
    place[axis] = (place[axis] + sign + count) % count
    return tuple(place)


def forward(link, field):
    out = [[None] * 3, [None] * 3]
    for r in range(3):
        re = im = None
        for c in range(3):
            ur, ui = link[0][r][c], link[1][r][c]
            vr, vi = field[0][c], field[1][c]
            re_term = ur * vr - ui * vi
            im_term = ur * vi + ui * vr
            re = re_term if re is None else re + re_term
            im = im_term if im is None else im + im_term
        out[0][r], out[1][r] = re, im
    return out


def backward(link, field):
    out = [[None] * 3, [None] * 3]
    for r in range(3):
        re = im = None
        for c in range(3):
            ur, ui = link[0][c][r], link[1][c][r]
            vr, vi = field[0][c], field[1][c]
            re_term = ur * vr + ui * vi
            im_term = ur * vi - ui * vr
            re = re_term if re is None else re + re_term
            im = im_term if im is None else im + im_term
        out[0][r], out[1][r] = re, im
    return out


def both(fn):
    return [[fn(p, c) for c in range(3)] for p in range(2)]


def plus(left, right):
    return both(lambda p, c: left[p][c] + right[p][c])


def split(value):
    high = value.astype(bf16)
    return high, (value - high.astype(f32)).astype(bf16)


def mul(left, right, dims=((1,), (0,))):
    return lax.dot_general(left, right, (dims, ((), ())), preferred_element_type=f32)


def whole(rows):
    half = rows.shape[1] // 2
    return jnp.concatenate(
        [rows, jnp.concatenate([-rows[:, half:], rows[:, :half]], 1)], 0
    )


def whole_split(rows):
    high, low = split(rows)
    return whole(high), whole(low)


def product(left, right):
    rows = left[0].shape[0]
    out = mul(jnp.concatenate(left, 0), right[0])
    return out[:rows] + out[rows:] + mul(left[0], right[1])


def lower_mask(order, strict):
    row = lax.broadcasted_iota(jnp.int32, (order, order), 0)
    column = lax.broadcasted_iota(jnp.int32, (order, order), 1)
    return row > column if strict else row >= column


def packed(re_part, im_part):
    return jnp.where(lower_mask(re_part.shape[0], False), re_part, im_part)


def unpacked(mixed):
    zero = jnp.zeros_like(mixed)
    low = jnp.where(lower_mask(mixed.shape[0], False), mixed, zero)
    strict = jnp.where(lower_mask(mixed.shape[0], True), mixed, zero)
    high = mixed - low
    return jnp.concatenate([low + strict.T, high - high.T], 1)


def side_by_side(ref, *index):
    half = [ref[(*index, p)].reshape(-1, ref.shape[-1]) for p in range(2)]
    return jnp.concatenate(half, 1)


def transposed(tiles):
    block = lax.broadcasted_iota(jnp.int32, (8, 128), 1) // 32
    low = block < 2
    even = block % 2 == 0
    a, b, c, d = tiles
    pairs = [
        jnp.where(low, a, pltpu.roll(c, 64, 1)),
        jnp.where(low, b, pltpu.roll(d, 64, 1)),
        jnp.where(low, pltpu.roll(a, 64, 1), c),
        jnp.where(low, pltpu.roll(b, 64, 1), d),
    ]
    out = []
    for first, second in (pairs[:2], pairs[2:]):
        out.append(jnp.where(even, first, pltpu.roll(second, 32, 1)))
        out.append(jnp.where(even, pltpu.roll(first, 96, 1), second))
    return out


def lane_roll(value, blocks):
    shift = 32 * (blocks % 4)
    return value if shift == 0 else pltpu.roll(value, shift, 1)


def whole_kernel(
    sites_all,
    vec_hbm,
    link_hbm,
    plain,
    root_ref,
    summed,
    hops,
    fields,
    packed_hops,
    wide,
    face_y,
    face_z,
    send_x,
    send_y,
    send_z,
    low_y,
    low_z,
    ahead_x,
    ahead_y,
    ahead_z,
    behind_x,
    behind_y,
    behind_z,
    part,
    first,
    second,
    link_ref,
    load_sems,
    face_sems,
    sent_sems,
    sum_sems,
):
    gx, gy, row, core = places()
    mine = gy * 4 + row
    line = gx * 2 + core

    barrier = pltpu.get_barrier_semaphore()
    load_field = pltpu.make_async_copy(vec_hbm, plain, load_sems.at[0])
    load_links = pltpu.make_async_copy(link_hbm, link_ref, load_sems.at[1])
    load_links.start()
    load_field.start()
    for axis in range(3):
        for sign in (-1, 1):
            pl.semaphore_signal(
                barrier, inc=1, device_id=neighbour(axis, sign), device_id_type=MESH
            )

    def greet(step, carry):
        device, _ = plane_mate(step)
        pl.semaphore_signal(barrier, inc=1, device_id=device, device_id_type=MESH)
        pl.semaphore_signal(barrier, inc=1, device_id=line_mate(step), device_id_type=MESH)
        return carry

    lax.fori_loop(0, 15, greet, 0)

    block = lax.broadcasted_iota(jnp.int32, (8, 128), 1) // 32
    zero = jnp.zeros((8, 128), f32)

    def rows_of(x, odd):
        return pl.ds(16 * x + 8 * odd, 8)

    def widen(batch, carry):
        begin = jnp.minimum(4 * batch, 50)
        tiles = link_ref[pl.ds(begin, 4)].reshape(128, 8)
        turned = tiles.T * HOP
        for entry in range(4):
            for x in range(4):
                for odd in range(2):
                    wide[begin + entry, rows_of(x, odd)] = jnp.take_along_axis(
                        turned,
                        32 * entry + 8 * x + odd + 2 * block,
                        axis=1,
                        mode="promise_in_bounds",
                    )
        return carry

    def edges(entry, carry):
        across_y = zero
        for x in range(4):
            value = wide[18 + entry, rows_of(x, 1)]
            across_y = jnp.where(block == x, lane_roll(value, x + 1), across_y)
            wide[18 + entry, rows_of(x, 1)] = jnp.where(block == 3, zero, value)
        face_y[entry] = across_y
        face_z[entry] = wide[36 + entry, pl.ds(7, 8, stride=8)]
        wide[36 + entry, pl.ds(7, 8, stride=8)] = zero
        return carry

    def pack(x, carry):
        for p in range(2):
            for c in range(3):
                for odd in range(2):
                    tiles = transposed(
                        [plain[p, c, x, pl.ds(8 * y, 8)] * 0.5 for y in range(odd, 8, 2)]
                    )
                    rows = pl.ds(pl.multiple_of(16 * x + 8 * odd, 8), 8)
                    for g in range(4):
                        fields[0, g, p, c, rows] = tiles[g]
        return carry

    def unpack(read, target):
        def body(x, carry):
            for p in range(2):
                for c in range(3):
                    for odd in range(2):
                        rows = pl.ds(pl.multiple_of(16 * x + 8 * odd, 8), 8)
                        tiles = transposed([read(g, p, c, rows) for g in range(4)])
                        for q in range(4):
                            target[p, c, x, pl.ds(8 * (odd + 2 * q), 8)] = tiles[q]
            return carry

        lax.fori_loop(0, 4, body, 0, unroll=True)

    def tile_link(mu, x, odd):
        rows = rows_of(x, odd)
        return [
            [[wide[18 * mu + p * 9 + r * 3 + c, rows] for c in range(3)] for r in range(3)]
            for p in range(2)
        ]

    def face_link(ref):
        return [
            [[ref[p * 9 + r * 3 + c] for c in range(3)] for r in range(3)]
            for p in range(2)
        ]

    def tile(k, g, x, odd):
        return both(lambda p, c: fields[k, g, p, c, rows_of(x, odd)])

    def store(ref, value, *index):
        for p in range(2):
            for c in range(3):
                ref[(*index[:2], p, c, *index[2:])] = value[p][c]

    def await_bytes(ref, sem):
        pltpu.make_async_copy(ref, ref, sem).wait()

    def face_copy(sign, axis, k, g):
        last = isinstance(k, int) and k == FILTER_STEPS
        if sign < 0:
            source, target = (
                lambda: (fields.at[k, g, :, :, pl.ds(0, 16)], ahead_x.at[k, g]),
                lambda: (low_y.at[k, g], ahead_y.at[k, g]),
                lambda: (low_z.at[k, g], ahead_z.at[k, g]),
            )[axis]()
            if last and axis == 0:
                some = pl.ds(0, 8)
                source = fields.at[k, g, :, :, some]
                target = ahead_x.at[k, g, :, :, some]
        else:
            source, target = (
                lambda: (send_x.at[k, g], behind_x.at[k, g]),
                lambda: (send_y.at[k, g], behind_y.at[k, g]),
                lambda: (send_z.at[k, g], behind_z.at[k, g]),
            )[axis]()
            if last:
                rest = pl.ds(8, 8)
                source = send_x.at[k, g, :, :, rest]
                target = behind_x.at[k, g, :, :, rest]
        side = 0 if sign < 0 else 1
        return pltpu.make_async_remote_copy(
            src_ref=source,
            dst_ref=target,
            send_sem=sent_sems.at[6 if last else 2 * axis + side],
            recv_sem=face_sems.at[0 if axis == 0 else 1, k, g],
            device_id=neighbour(axis, sign),
            device_id_type=MESH,
        )

    def gather_y(k, g, odd, blocks):
        def one(p, c):
            out = fields[k, g, p, c, rows_of(0, odd)]
            out = lane_roll(out, blocks)
            for x in range(1, 4):
                value = lane_roll(fields[k, g, p, c, rows_of(x, odd)], blocks + x)
                out = jnp.where(block == x, value, out)
            return out

        return both(one)

    def strided(k, g, z):
        return both(lambda p, c: fields[k, g, p, c, pl.ds(z, 8, stride=8)])

    def make_high_x(k, g, odds=(0, 1)):
        for odd in odds:
            value = backward(tile_link(0, 3, odd), tile(k, g, 3, odd))
            store(send_x, value, k, g, pl.ds(8 * odd, 8))

    def make_low_y(k, g):
        store(low_y, gather_y(k, g, 0, 0), k, g)

    def make_high_y(k, g):
        store(send_y, backward(face_link(face_y), gather_y(k, g, 1, 1)), k, g)

    def make_low_z(k, g):
        store(low_z, strided(k, g, 0), k, g)

    def make_high_z(k, g):
        store(send_z, backward(face_link(face_z), strided(k, g, 7)), k, g)

    def send_faces(k, g):
        face_copy(-1, 0, k, g).start()
        make_high_x(k, g)
        face_copy(1, 0, k, g).start()
        make_low_y(k, g)
        face_copy(-1, 1, k, g).start()
        make_high_y(k, g)
        face_copy(1, 1, k, g).start()
        make_low_z(k, g)
        face_copy(-1, 2, k, g).start()
        make_high_z(k, g)
        face_copy(1, 2, k, g).start()

    def send_last(g):
        k = FILTER_STEPS
        face_copy(-1, 0, k, g).start()
        make_high_x(k, g, (1,))
        face_copy(1, 0, k, g).start()
        make_low_y(k, g)
        face_copy(-1, 1, k, g).start()
        make_low_z(k, g)
        face_copy(-1, 2, k, g).start()

    def forward_hops(k, g, x, odd, here, acc):
        rolled = both(lambda p, c: pltpu.roll(here[p][c], 7, 0))
        value = forward(tile_link(2, x, odd), rolled)
        acc = value if acc is None else plus(acc, value)
        if x < 3:
            acc = plus(acc, forward(tile_link(0, x, odd), tile(k, g, x + 1, odd)))
        other = tile(k, g, x, 1 - odd)
        if odd:
            other = both(lambda p, c: lane_roll(other_of(k, g, p, c, x), 3))
        return plus(acc, forward(tile_link(1, x, odd), other))

    def other_of(k, g, p, c, x):
        return fields[k, g, p, c, rows_of(x, 0)]

    def local_pass(k, g):
        again = jnp.where(k == 0, 0.0, jnp.where(k == 1, 2.0, 1.0)).astype(f32)
        before = jnp.maximum(k - 1, 0)
        for x in range(4):
            for odd in range(2):
                here = tile(k, g, x, odd)
                old = tile(before, g, x, odd)
                acc = both(lambda p, c: SELF * here[p][c] - again * old[p][c])
                acc = forward_hops(k, g, x, odd, here, acc)
                back = backward(tile_link(2, x, odd), here)
                acc = plus(acc, both(lambda p, c: pltpu.roll(back[p][c], 1, 0)))
                if x > 0:
                    acc = plus(acc, backward(tile_link(0, x - 1, odd), tile(k, g, x - 1, odd)))
                back = backward(tile_link(1, x, 1 - odd), tile(k, g, x, 1 - odd))
                if not odd:
                    back_y = back
                    back = both(lambda p, c: lane_roll(back_y[p][c], 1))
                acc = plus(acc, back)
                store(fields, acc, k + 1, g, rows_of(x, odd))

    def forward_pass(k, g):
        for x in range(4):
            for odd in range(2):
                acc = forward_hops(k, g, x, odd, tile(k, g, x, odd), None)
                for p in range(2):
                    for c in range(3):
                        packed_hops[g, p, c, rows_of(x, odd)] = acc[p][c]

    def from_ahead_x(at, k, g, odds=(0, 1)):
        for odd in odds:
            value = forward(
                tile_link(0, 3, odd),
                both(lambda p, c: ahead_x[k, g, p, c, pl.ds(8 * odd, 8)]),
            )
            for p in range(2):
                for c in range(3):
                    ref, index = at(p, c)
                    rows = (*index, rows_of(3, odd))
                    ref[rows] = ref[rows] + value[p][c]

    def from_behind_x(at, k, g, odds=(0, 1)):
        for odd in odds:
            for p in range(2):
                for c in range(3):
                    ref, index = at(p, c)
                    rows = (*index, rows_of(0, odd))
                    ref[rows] = ref[rows] + behind_x[k, g, p, c, pl.ds(8 * odd, 8)]

    def from_ahead_yz(at, k, g):
        value = forward(face_link(face_y), both(lambda p, c: ahead_y[k, g, p, c]))
        other = forward(face_link(face_z), both(lambda p, c: ahead_z[k, g, p, c]))
        for p in range(2):
            for c in range(3):
                ref, index = at(p, c)
                for x in range(4):
                    rows = (*index, rows_of(x, 1))
                    term = jnp.where(block == 3, lane_roll(value[p][c], 3 - x), zero)
                    ref[rows] = ref[rows] + term
                rows = (*index, pl.ds(7, 8, stride=8))
                ref[rows] = ref[rows] + other[p][c]

    def from_behind_yz(at, k, g):
        for p in range(2):
            for c in range(3):
                ref, index = at(p, c)
                value = behind_y[k, g, p, c]
                for x in range(4):
                    rows = (*index, rows_of(x, 0))
                    term = jnp.where(block == 0, lane_roll(value, 4 - x), zero)
                    ref[rows] = ref[rows] + term
                rows = (*index, pl.ds(0, 8, stride=8))
                ref[rows] = ref[rows] + behind_z[k, g, p, c]

    def finish(k, g):
        at = lambda p, c: (fields, (k + 1, g, p, c))
        await_bytes(ahead_y.at[k], face_sems.at[1, k, g])
        from_ahead_yz(at, k, g)
        from_behind_yz(at, k, g)
        await_bytes(ahead_x.at[k, pl.ds(0, 2)], face_sems.at[0, k, g])
        from_behind_x(at, k, g)
        from_ahead_x(at, k, g)

    def finish_hops(g):
        k = FILTER_STEPS
        at = lambda p, c: (packed_hops, (g, p, c))
        await_bytes(ahead_y.at[k, pl.ds(0, 2)], face_sems.at[1, k, g])
        from_ahead_yz(at, k, g)
        await_bytes(ahead_y.at[k, pl.ds(0, 2)], face_sems.at[0, k, g])
        from_ahead_x(at, k, g, (0,))
        from_behind_x(at, k, g, (1,))

    def groups(fn, begin=0, end=4):
        def body(g, carry):
            fn(g)
            return carry

        lax.fori_loop(begin, end, body, 0)

    def scatter(j, step):
        device, index = plane_mate(step)
        return pltpu.make_async_remote_copy(
            src_ref=part.at[j, index],
            dst_ref=first.at[j, step],
            send_sem=sum_sems.at[j, 0],
            recv_sem=sum_sems.at[j, 1],
            device_id=device,
            device_id_type=MESH,
        )

    def across(j, step):
        return pltpu.make_async_remote_copy(
            src_ref=second.at[j, line],
            dst_ref=second.at[j, line],
            send_sem=sum_sems.at[j, 2],
            recv_sem=sum_sems.at[j, 3],
            device_id=line_mate(step),
            device_id_type=MESH,
        )

    def gather(j, step):
        device, _ = plane_mate(step)
        return pltpu.make_async_remote_copy(
            src_ref=summed.at[j, mine],
            dst_ref=summed.at[j, mine],
            send_sem=sum_sems.at[j, 4],
            recv_sem=sum_sems.at[j, 5],
            device_id=device,
            device_id_type=MESH,
        )

    def each(fn):
        def body(step, carry):
            fn(step)
            return carry

        lax.fori_loop(0, 15, body, 0, unroll=True)

    def start_all(make, j):
        each(lambda step: make(j, step).start())

    def drain(j, sem):
        pieces = first.at[j, pl.ds(0, 15)]
        pltpu.make_async_copy(pieces, pieces, sum_sems.at[j, sem]).wait()

    def sum_begin(j, value):
        for piece in range(16):
            part[j, piece] = value[8 * piece : 8 * piece + 8]
        start_all(scatter, j)

    def sum_middle(j):
        first[j, 15] = part[j, mine]
        drain(j, 1)
        total = first[j, 0]
        for step in range(1, 16):
            total = total + first[j, step]
        second[j, line] = total
        start_all(across, j)

    def sum_last(j):
        drain(j, 3)
        total = second[j, 0]
        for step in range(1, 16):
            total = total + second[j, step]
        summed[j, mine] = total
        start_all(gather, j)

    def sum_end(j):
        drain(j, 5)

    load_field.wait()
    lax.fori_loop(0, 4, pack, 0)
    load_links.wait()
    lax.fori_loop(0, 14, widen, 0, unroll=True)
    lax.fori_loop(0, 18, edges, 0, unroll=True)
    pl.semaphore_wait(barrier, 36)
    groups(lambda g: send_faces(0, g))
    groups(lambda g: local_pass(0, g))

    def turn_of(index):
        k = index // 4
        g = index % 4
        finish(k, g)
        send_faces(k + 1, g)
        local_pass(k + 1, g)

    groups(turn_of, 0, 4 * (FILTER_STEPS - 1))

    def last_turn(g):
        finish(FILTER_STEPS - 1, g)
        send_last(g)

    groups(last_turn)
    last = FILTER_STEPS
    unpack(lambda g, p, c, rows: fields[last, g, p, c, rows], plain)

    high, low = split(side_by_side(plain))
    gram = mul(high, high, SUBLANES)
    cross = mul(high, low, SUBLANES)
    half = gram.shape[0] // 2
    cross_re = cross[:half, :half] + cross[half:, half:]
    cross_im = cross[:half, half:] - cross[half:, :half]
    sum_begin(
        0,
        packed(
            gram[:half, :half] + gram[half:, half:] + (cross_re + cross_re.T),
            gram[:half, half:] - gram[half:, :half] + (cross_im - cross_im.T),
        ),
    )

    groups(lambda g: forward_pass(last, g))
    groups(finish_hops)
    unpack(lambda g, p, c, rows: packed_hops[g, p, c, rows], hops)
    hop_high, hop_low = split(side_by_side(hops))
    proj = mul(high, hop_high, SUBLANES)
    proj = proj + mul(high, hop_low, SUBLANES)
    proj = proj + mul(low, hop_high, SUBLANES)
    proj_re = proj[:half, :half] + proj[half:, half:]
    proj_im = proj[:half, half:] - proj[half:, :half]
    sum_begin(1, packed(proj_re + proj_re.T, proj_im - proj_im.T))
    sum_middle(0)
    sum_middle(1)
    sum_last(0)
    sum_last(1)
    sum_end(0)
    gram_sum = sum_of(summed, 0) / sites_all

    scale = jnp.sqrt(2.0 * jnp.sum(gram_sum * gram_sum, keepdims=True))
    eye = (
        lax.broadcasted_iota(jnp.int32, (half, 2 * half), 0)
        == lax.broadcasted_iota(jnp.int32, (half, 2 * half), 1)
    ).astype(f32)
    iterate = gram_sum / scale
    factor = 1.5 * eye - 0.5 * iterate
    iterate = product(split(iterate), whole_split(factor))
    result = factor

    def newton(step, carry):
        iterate, result = carry
        result_split = split(result)
        factor = 1.5 * eye - 0.5 * product(result_split, whole_split(iterate))
        right = whole_split(factor)
        return (product(split(iterate), right), product(result_split, right))

    iterate, result = lax.fori_loop(1, NS_STEPS - 1, newton, (iterate, result))
    result_split = split(result)
    factor = 1.5 * eye - 0.5 * product(result_split, whole_split(iterate))
    root_ref[...] = product(result_split, whole_split(factor)) / jnp.sqrt(scale)
    sum_end(1)
    early = pl.ds(0, FILTER_STEPS)
    for index, ref in enumerate((send_x, send_x, send_y, send_y, send_z, send_z, send_y)):
        await_bytes(ref.at[early], sent_sems.at[index])
    for j in range(2):
        for sem in (0, 2, 4):
            drain(j, sem)


def sum_of(summed, j):
    return unpacked(summed[j].reshape(128, 128))


def rotate_kernel(
    sites_all, plain, root_ref, summed, basis_ref, ritz_ref, turned, ritz_rows, sems
):
    root = root_ref[...]
    half = root.shape[0]
    right = whole_split(root)
    copies = []
    for c in range(3):
        left = jnp.concatenate([plain[p, c].reshape(-1, half) for p in range(2)], 1)
        out = product(split(left), right)
        for p in range(2):
            turned[p, c] = out[:, p * half : (p + 1) * half].reshape(turned.shape[2:])
            copy = pltpu.make_async_copy(turned.at[p, c], basis_ref.at[p, c], sems.at[p, c])
            copy.start()
            copies.append(copy)
    gram_sum = sum_of(summed, 0) / sites_all
    proj_sum = 6.0 * gram_sum + (-1.0 / HOP) * (sum_of(summed, 1) / sites_all)
    ritz = product(split(proj_sum), right)
    ritz = product(split(root), whole_split(ritz))
    for p in range(2):
        ritz_rows[p] = ritz[:, p * half : (p + 1) * half]
    copy = pltpu.make_async_copy(ritz_rows, ritz_ref, sems.at[0, 3])
    copy.start()
    copies.append(copy)
    for copy in copies:
        copy.wait()


def shards(vectors, links):
    brick = vectors.shape
    sites_all = float(
        vectors.shape[2]
        * lax.axis_size("gx")
        * vectors.shape[3]
        * lax.axis_size("gy")
        * vectors.shape[4]
        * lax.axis_size("gz")
    )
    vec = vectors.reshape(2, 3, 4, 64, 128)
    link = links.reshape(54, 4, 8, 8)
    steps = FILTER_STEPS
    face_x = (steps + 1, 4, 2, 3, 16, 128)
    face = (steps + 1, 4, 2, 3, 8, 128)
    vmem = lambda *shape: pltpu.VMEM(shape, f32)
    space = pl.BlockSpec(memory_space=pltpu.VMEM)
    far = pl.BlockSpec(memory_space=pltpu.HBM)
    field, root, sums = pl.pallas_call(
        lambda *refs: whole_kernel(sites_all, *refs),
        out_shape=(
            jax.ShapeDtypeStruct(vec.shape, f32),
            jax.ShapeDtypeStruct((128, 256), f32),
            jax.ShapeDtypeStruct((2, 16, 8, 128), f32),
        ),
        in_specs=[far, far],
        out_specs=(space, space, space),
        scratch_shapes=[
            vmem(*vec.shape),
            vmem(steps + 1, 4, 2, 3, 64, 128),
            vmem(4, 2, 3, 64, 128),
            vmem(54, 64, 128),
            vmem(18, 8, 128),
            vmem(18, 8, 128),
            vmem(*face_x),
            vmem(*face),
            vmem(*face),
            vmem(*face),
            vmem(*face),
            vmem(*face_x),
            vmem(*face),
            vmem(*face),
            vmem(*face_x),
            vmem(*face),
            vmem(*face),
            vmem(2, 16, 8, 128),
            vmem(2, 16, 8, 128),
            vmem(2, 16, 8, 128),
            vmem(*link.shape),
            pltpu.SemaphoreType.DMA((2,)),
            pltpu.SemaphoreType.DMA((2, steps + 1, 4)),
            pltpu.SemaphoreType.DMA((7,)),
            pltpu.SemaphoreType.DMA((2, 6)),
        ],
        compiler_params=pltpu.CompilerParams(
            collective_id=0, has_side_effects=True, vmem_limit_bytes=48 * 1024 * 1024
        ),
    )(
        pltpu.with_memory_space_constraint(vec, pltpu.HBM),
        pltpu.with_memory_space_constraint(link, pltpu.HBM),
    )
    basis, ritz = pl.pallas_call(
        lambda *refs: rotate_kernel(sites_all, *refs),
        out_shape=(
            jax.ShapeDtypeStruct(vec.shape, f32),
            jax.ShapeDtypeStruct((2, 128, 128), f32),
        ),
        in_specs=[space, space, space],
        out_specs=(far, far),
        scratch_shapes=[
            vmem(*vec.shape),
            vmem(2, 128, 128),
            pltpu.SemaphoreType.DMA((2, 4)),
        ],
        compiler_params=pltpu.CompilerParams(vmem_limit_bytes=8 * 1024 * 1024),
    )(field, root, sums)
    return (basis.reshape(brick), ritz)


def solution(mesh):
    return jax.shard_map(
        shards,
        mesh=mesh,
        in_specs=(
            P(None, None, "gx", "gy", "gz", None),
            P(None, None, None, None, "gx", "gy", "gz"),
        ),
        out_specs=(P(None, None, "gx", "gy", "gz", None), P()),
        check_vma=False,
    )
```

```python
import jax
import jax.numpy as jnp
from jax import lax
from jax.experimental import pallas as pl
from jax.experimental.pallas import tpu as pltpu
from jax.sharding import PartitionSpec as P

NS_STEPS = 10
FILTER_STEPS = 4

filter_low = 1.0
filter_high = 12.0

MESH = pl.DeviceIdType.MESH
HOP = -4.0 / (filter_high - filter_low)
SELF = 2.0 * (12.0 - filter_high - filter_low) / (filter_high - filter_low)
SUBLANES = ((0,), (0,))
f32 = jnp.float32
bf16 = jnp.bfloat16


def places():
    gx = lax.axis_index("gx")
    gy = lax.axis_index("gy")
    gz = lax.axis_index("gz")
    return gx, gy, gz // 2, gz % 2


def plane_mate(step, here):
    def offset(place):
        return jnp.where(place == 0, 2, jnp.where(place == 1, 1, jnp.where(place == 2, 3, 0)))

    gx, gy, row, core = here
    other_y = (gy + offset(step // 4)) % 4
    other_row = (row + offset(step % 4)) % 4
    return (gx, other_y, other_row * 2 + core), other_y * 4 + other_row


def line_mate(step, here):
    gx, gy, row, core = here
    place = step // 2
    offset = jnp.where(place % 2 == 0, 4 + place // 2, 4 - (place + 1) // 2)
    other_x = (gx + offset) % 8
    other_core = (core + (step + 1) % 2) % 2
    return (other_x, gy, row * 2 + other_core)


def neighbour(axis, sign):
    place = [lax.axis_index("gx"), lax.axis_index("gy"), lax.axis_index("gz")]
    count = (8, 4, 8)[axis]
    place[axis] = (place[axis] + sign + count) % count
    return tuple(place)


def forward(link, field):
    out = [[None] * 3, [None] * 3]
    for r in range(3):
        re = im = None
        for c in range(3):
            ur, ui = link[0][r][c], link[1][r][c]
            vr, vi = field[0][c], field[1][c]
            re_term = ur * vr - ui * vi
            im_term = ur * vi + ui * vr
            re = re_term if re is None else re + re_term
            im = im_term if im is None else im + im_term
        out[0][r], out[1][r] = re, im
    return out


def backward(link, field):
    out = [[None] * 3, [None] * 3]
    for r in range(3):
        re = im = None
        for c in range(3):
            ur, ui = link[0][c][r], link[1][c][r]
            vr, vi = field[0][c], field[1][c]
            re_term = ur * vr + ui * vi
            im_term = ur * vi - ui * vr
            re = re_term if re is None else re + re_term
            im = im_term if im is None else im + im_term
        out[0][r], out[1][r] = re, im
    return out


def both(fn):
    return [[fn(p, c) for c in range(3)] for p in range(2)]


def plus(left, right):
    return both(lambda p, c: left[p][c] + right[p][c])


def split(value):
    high = value.astype(bf16)
    return high, (value - high.astype(f32)).astype(bf16)


def mul(left, right, dims=((1,), (0,))):
    return lax.dot_general(left, right, (dims, ((), ())), preferred_element_type=f32)


def whole(rows):
    half = rows.shape[1] // 2
    return jnp.concatenate(
        [rows, jnp.concatenate([-rows[:, half:], rows[:, :half]], 1)], 0
    )


def whole_split(rows):
    high, low = split(rows)
    return whole(high), whole(low)


def product(left, right):
    rows = left[0].shape[0]
    out = mul(jnp.concatenate(left, 0), right[0])
    return out[:rows] + out[rows:] + mul(left[0], right[1])


def lower_mask(order, strict):
    row = lax.broadcasted_iota(jnp.int32, (order, order), 0)
    column = lax.broadcasted_iota(jnp.int32, (order, order), 1)
    return row > column if strict else row >= column


def packed(re_part, im_part):
    return jnp.where(lower_mask(re_part.shape[0], False), re_part, im_part)


def unpacked(mixed):
    zero = jnp.zeros_like(mixed)
    low = jnp.where(lower_mask(mixed.shape[0], False), mixed, zero)
    strict = jnp.where(lower_mask(mixed.shape[0], True), mixed, zero)
    high = mixed - low
    return jnp.concatenate([low + strict.T, high - high.T], 1)


def side_by_side(ref, *index):
    half = [ref[(*index, p)].reshape(-1, ref.shape[-1]) for p in range(2)]
    return jnp.concatenate(half, 1)


def transposed(tiles):
    block = lax.broadcasted_iota(jnp.int32, (8, 128), 1) // 32
    low = block < 2
    even = block % 2 == 0
    a, b, c, d = tiles
    pairs = [
        jnp.where(low, a, pltpu.roll(c, 64, 1)),
        jnp.where(low, b, pltpu.roll(d, 64, 1)),
        jnp.where(low, pltpu.roll(a, 64, 1), c),
        jnp.where(low, pltpu.roll(b, 64, 1), d),
    ]
    out = []
    for first, second in (pairs[:2], pairs[2:]):
        out.append(jnp.where(even, first, pltpu.roll(second, 32, 1)))
        out.append(jnp.where(even, pltpu.roll(first, 96, 1), second))
    return out


def lane_roll(value, blocks):
    shift = 32 * (blocks % 4)
    return value if shift == 0 else pltpu.roll(value, shift, 1)


def whole_kernel(
    sites_all,
    vec_hbm,
    link_hbm,
    plain,
    root_ref,
    summed,
    hops,
    fields,
    packed_hops,
    wide,
    face_y,
    face_z,
    send_x,
    send_y,
    send_z,
    low_y,
    low_z,
    ahead_x,
    ahead_y,
    ahead_z,
    behind_x,
    behind_y,
    behind_z,
    part,
    first,
    second,
    link_ref,
    load_sems,
    face_sems,
    sent_sems,
    sum_sems,
):
    here = places()
    gx, gy, row, core = here
    near = {(axis, sign): neighbour(axis, sign) for axis in range(3) for sign in (-1, 1)}
    mine = gy * 4 + row
    line = gx * 2 + core

    barrier = pltpu.get_barrier_semaphore()
    load_field = pltpu.make_async_copy(vec_hbm, plain, load_sems.at[0])
    load_links = pltpu.make_async_copy(link_hbm, link_ref, load_sems.at[1])
    load_links.start()
    load_field.start()
    for axis in range(3):
        for sign in (-1, 1):
            pl.semaphore_signal(
                barrier, inc=1, device_id=near[axis, sign], device_id_type=MESH
            )

    def greet(step, carry):
        device, _ = plane_mate(step, here)
        pl.semaphore_signal(barrier, inc=1, device_id=device, device_id_type=MESH)
        pl.semaphore_signal(barrier, inc=1, device_id=line_mate(step, here), device_id_type=MESH)
        return carry

    lax.fori_loop(0, 15, greet, 0)

    block = lax.broadcasted_iota(jnp.int32, (8, 128), 1) // 32
    zero = jnp.zeros((8, 128), f32)

    def rows_of(x, odd):
        return pl.ds(16 * x + 8 * odd, 8)

    def widen(batch, carry):
        begin = jnp.minimum(4 * batch, 50)
        tiles = link_ref[pl.ds(begin, 4)].reshape(128, 8)
        turned = tiles.T * HOP
        for entry in range(4):
            for x in range(4):
                for odd in range(2):
                    wide[begin + entry, rows_of(x, odd)] = jnp.take_along_axis(
                        turned,
                        32 * entry + 8 * x + odd + 2 * block,
                        axis=1,
                        mode="promise_in_bounds",
                    )
        return carry

    def edges(entry, carry):
        across_y = zero
        for x in range(4):
            value = wide[18 + entry, rows_of(x, 1)]
            across_y = jnp.where(block == x, lane_roll(value, x + 1), across_y)
            wide[18 + entry, rows_of(x, 1)] = jnp.where(block == 3, zero, value)
        face_y[entry] = across_y
        face_z[entry] = wide[36 + entry, pl.ds(7, 8, stride=8)]
        wide[36 + entry, pl.ds(7, 8, stride=8)] = zero
        return carry

    def pack(x, carry):
        for p in range(2):
            for c in range(3):
                for odd in range(2):
                    tiles = transposed(
                        [plain[p, c, x, pl.ds(8 * y, 8)] * 0.5 for y in range(odd, 8, 2)]
                    )
                    rows = pl.ds(pl.multiple_of(16 * x + 8 * odd, 8), 8)
                    for g in range(4):
                        fields[0, g, p, c, rows] = tiles[g]
        return carry

    def unpack(read, target):
        def body(x, carry):
            for p in range(2):
                for c in range(3):
                    for odd in range(2):
                        rows = pl.ds(pl.multiple_of(16 * x + 8 * odd, 8), 8)
                        tiles = transposed([read(g, p, c, rows) for g in range(4)])
                        for q in range(4):
                            target[p, c, x, pl.ds(8 * (odd + 2 * q), 8)] = tiles[q]
            return carry

        lax.fori_loop(0, 4, body, 0, unroll=True)

    def tile_link(mu, x, odd):
        rows = rows_of(x, odd)
        return [
            [[wide[18 * mu + p * 9 + r * 3 + c, rows] for c in range(3)] for r in range(3)]
            for p in range(2)
        ]

    def face_link(ref):
        return [
            [[ref[p * 9 + r * 3 + c] for c in range(3)] for r in range(3)]
            for p in range(2)
        ]

    def tile(k, g, x, odd):
        return both(lambda p, c: fields[k, g, p, c, rows_of(x, odd)])

    def store(ref, value, *index):
        for p in range(2):
            for c in range(3):
                ref[(*index[:2], p, c, *index[2:])] = value[p][c]

    def await_bytes(ref, sem):
        pltpu.make_async_copy(ref, ref, sem).wait()

    def face_copy(sign, axis, k, g):
        last = isinstance(k, int) and k == FILTER_STEPS
        if sign < 0:
            source, target = (
                lambda: (fields.at[k, g, :, :, pl.ds(0, 16)], ahead_x.at[k, g]),
                lambda: (low_y.at[k, g], ahead_y.at[k, g]),
                lambda: (low_z.at[k, g], ahead_z.at[k, g]),
            )[axis]()
            if last and axis == 0:
                some = pl.ds(0, 8)
                source = fields.at[k, g, :, :, some]
                target = ahead_x.at[k, g, :, :, some]
        else:
            source, target = (
                lambda: (send_x.at[k, g], behind_x.at[k, g]),
                lambda: (send_y.at[k, g], behind_y.at[k, g]),
                lambda: (send_z.at[k, g], behind_z.at[k, g]),
            )[axis]()
            if last:
                rest = pl.ds(8, 8)
                source = send_x.at[k, g, :, :, rest]
                target = behind_x.at[k, g, :, :, rest]
        side = 0 if sign < 0 else 1
        return pltpu.make_async_remote_copy(
            src_ref=source,
            dst_ref=target,
            send_sem=sent_sems.at[6 if last else 2 * axis + side],
            recv_sem=face_sems.at[0 if axis == 0 else 1, k, g],
            device_id=near[axis, sign],
            device_id_type=MESH,
        )

    def gather_y(k, g, odd, blocks):
        def one(p, c):
            out = fields[k, g, p, c, rows_of(0, odd)]
            out = lane_roll(out, blocks)
            for x in range(1, 4):
                value = lane_roll(fields[k, g, p, c, rows_of(x, odd)], blocks + x)
                out = jnp.where(block == x, value, out)
            return out

        return both(one)

    def strided(k, g, z):
        return both(lambda p, c: fields[k, g, p, c, pl.ds(z, 8, stride=8)])

    def make_high_x(k, g, odds=(0, 1)):
        for odd in odds:
            value = backward(tile_link(0, 3, odd), tile(k, g, 3, odd))
            store(send_x, value, k, g, pl.ds(8 * odd, 8))

    def make_low_y(k, g):
        store(low_y, gather_y(k, g, 0, 0), k, g)

    def make_high_y(k, g):
        store(send_y, backward(face_link(face_y), gather_y(k, g, 1, 1)), k, g)

    def make_low_z(k, g):
        store(low_z, strided(k, g, 0), k, g)

    def make_high_z(k, g):
        store(send_z, backward(face_link(face_z), strided(k, g, 7)), k, g)

    def send_faces(k, g):
        make_high_x(k, g)
        face_copy(1, 0, k, g).start()
        make_low_y(k, g)
        face_copy(-1, 1, k, g).start()
        make_high_y(k, g)
        face_copy(1, 1, k, g).start()
        make_low_z(k, g)
        face_copy(-1, 2, k, g).start()
        make_high_z(k, g)
        face_copy(1, 2, k, g).start()

    def send_last(g):
        k = FILTER_STEPS
        make_high_x(k, g, (1,))
        face_copy(1, 0, k, g).start()
        make_low_y(k, g)
        face_copy(-1, 1, k, g).start()
        make_low_z(k, g)
        face_copy(-1, 2, k, g).start()

    def forward_hops(k, g, x, odd, here, acc):
        rolled = both(lambda p, c: pltpu.roll(here[p][c], 7, 0))
        value = forward(tile_link(2, x, odd), rolled)
        acc = value if acc is None else plus(acc, value)
        if x < 3:
            acc = plus(acc, forward(tile_link(0, x, odd), tile(k, g, x + 1, odd)))
        other = tile(k, g, x, 1 - odd)
        if odd:
            other = both(lambda p, c: lane_roll(other_of(k, g, p, c, x), 3))
        return plus(acc, forward(tile_link(1, x, odd), other))

    def other_of(k, g, p, c, x):
        return fields[k, g, p, c, rows_of(x, 0)]

    def local_pass(k, g):
        again = jnp.where(k == 0, 0.0, jnp.where(k == 1, 2.0, 1.0)).astype(f32)
        before = jnp.maximum(k - 1, 0)
        for x in range(4):
            for odd in range(2):
                here = tile(k, g, x, odd)
                old = tile(before, g, x, odd)
                acc = both(lambda p, c: SELF * here[p][c] - again * old[p][c])
                acc = forward_hops(k, g, x, odd, here, acc)
                back = backward(tile_link(2, x, odd), here)
                acc = plus(acc, both(lambda p, c: pltpu.roll(back[p][c], 1, 0)))
                if x > 0:
                    acc = plus(acc, backward(tile_link(0, x - 1, odd), tile(k, g, x - 1, odd)))
                back = backward(tile_link(1, x, 1 - odd), tile(k, g, x, 1 - odd))
                if not odd:
                    back_y = back
                    back = both(lambda p, c: lane_roll(back_y[p][c], 1))
                acc = plus(acc, back)
                store(fields, acc, k + 1, g, rows_of(x, odd))

    def forward_pass(k, g):
        for x in range(4):
            for odd in range(2):
                acc = forward_hops(k, g, x, odd, tile(k, g, x, odd), None)
                for p in range(2):
                    for c in range(3):
                        packed_hops[g, p, c, rows_of(x, odd)] = acc[p][c]

    def from_ahead_x(at, k, g, odds=(0, 1)):
        for odd in odds:
            value = forward(
                tile_link(0, 3, odd),
                both(lambda p, c: ahead_x[k, g, p, c, pl.ds(8 * odd, 8)]),
            )
            for p in range(2):
                for c in range(3):
                    ref, index = at(p, c)
                    rows = (*index, rows_of(3, odd))
                    ref[rows] = ref[rows] + value[p][c]

    def from_behind_x(at, k, g, odds=(0, 1)):
        for odd in odds:
            for p in range(2):
                for c in range(3):
                    ref, index = at(p, c)
                    rows = (*index, rows_of(0, odd))
                    ref[rows] = ref[rows] + behind_x[k, g, p, c, pl.ds(8 * odd, 8)]

    def from_ahead_yz(at, k, g):
        value = forward(face_link(face_y), both(lambda p, c: ahead_y[k, g, p, c]))
        other = forward(face_link(face_z), both(lambda p, c: ahead_z[k, g, p, c]))
        for p in range(2):
            for c in range(3):
                ref, index = at(p, c)
                for x in range(4):
                    rows = (*index, rows_of(x, 1))
                    term = jnp.where(block == 3, lane_roll(value[p][c], 3 - x), zero)
                    ref[rows] = ref[rows] + term
                rows = (*index, pl.ds(7, 8, stride=8))
                ref[rows] = ref[rows] + other[p][c]

    def from_behind_yz(at, k, g):
        for p in range(2):
            for c in range(3):
                ref, index = at(p, c)
                value = behind_y[k, g, p, c]
                for x in range(4):
                    rows = (*index, rows_of(x, 0))
                    term = jnp.where(block == 0, lane_roll(value, 4 - x), zero)
                    ref[rows] = ref[rows] + term
                rows = (*index, pl.ds(0, 8, stride=8))
                ref[rows] = ref[rows] + behind_z[k, g, p, c]

    def finish(k, g):
        at = lambda p, c: (fields, (k + 1, g, p, c))
        await_bytes(ahead_y.at[k], face_sems.at[1, k, g])
        from_ahead_yz(at, k, g)
        from_behind_yz(at, k, g)
        await_bytes(ahead_x.at[k, pl.ds(0, 2)], face_sems.at[0, k, g])
        from_behind_x(at, k, g)
        face_copy(-1, 0, k + 1, g).start()
        from_ahead_x(at, k, g)

    def finish_hops(g):
        k = FILTER_STEPS
        at = lambda p, c: (packed_hops, (g, p, c))
        await_bytes(ahead_y.at[k, pl.ds(0, 2)], face_sems.at[1, k, g])
        from_ahead_yz(at, k, g)
        await_bytes(ahead_y.at[k, pl.ds(0, 2)], face_sems.at[0, k, g])
        from_ahead_x(at, k, g, (0,))
        from_behind_x(at, k, g, (1,))

    def groups(fn, begin=0, end=4):
        def body(g, carry):
            fn(g)
            return carry

        lax.fori_loop(begin, end, body, 0)

    def scatter(j, step):
        device, index = plane_mate(step, here)
        return pltpu.make_async_remote_copy(
            src_ref=part.at[j, index],
            dst_ref=first.at[j, step],
            send_sem=sum_sems.at[j, 0],
            recv_sem=sum_sems.at[j, 1],
            device_id=device,
            device_id_type=MESH,
        )

    def across(j, step):
        return pltpu.make_async_remote_copy(
            src_ref=second.at[j, line],
            dst_ref=second.at[j, line],
            send_sem=sum_sems.at[j, 2],
            recv_sem=sum_sems.at[j, 3],
            device_id=line_mate(step, here),
            device_id_type=MESH,
        )

    def gather(j, step):
        device, _ = plane_mate(step, here)
        return pltpu.make_async_remote_copy(
            src_ref=summed.at[j, mine],
            dst_ref=summed.at[j, mine],
            send_sem=sum_sems.at[j, 4],
            recv_sem=sum_sems.at[j, 5],
            device_id=device,
            device_id_type=MESH,
        )

    def each(fn):
        def body(step, carry):
            fn(step)
            return carry

        lax.fori_loop(0, 15, body, 0, unroll=True)

    def start_all(make, j):
        each(lambda step: make(j, step).start())

    def drain(j, sem):
        pieces = first.at[j, pl.ds(0, 15)]
        pltpu.make_async_copy(pieces, pieces, sum_sems.at[j, sem]).wait()

    def sum_begin(j, value):
        for piece in range(16):
            part[j, piece] = value[8 * piece : 8 * piece + 8]
        start_all(scatter, j)

    def sum_middle(j):
        first[j, 15] = part[j, mine]
        drain(j, 1)
        total = first[j, 0]
        for step in range(1, 16):
            total = total + first[j, step]
        second[j, line] = total
        start_all(across, j)

    def sum_last(j):
        drain(j, 3)
        total = second[j, 0]
        for step in range(1, 16):
            total = total + second[j, step]
        summed[j, mine] = total
        start_all(gather, j)

    def sum_end(j):
        drain(j, 5)

    load_field.wait()
    lax.fori_loop(0, 4, pack, 0)
    load_links.wait()
    lax.fori_loop(0, 14, widen, 0, unroll=True)
    lax.fori_loop(0, 18, edges, 0, unroll=True)
    pl.semaphore_wait(barrier, 36)
    groups(lambda g: face_copy(-1, 0, 0, g).start())
    groups(lambda g: send_faces(0, g))
    groups(lambda g: local_pass(0, g))

    def turn_of(index):
        k = index // 4
        g = index % 4
        finish(k, g)
        send_faces(k + 1, g)
        local_pass(k + 1, g)

    groups(turn_of, 0, 4 * (FILTER_STEPS - 1))

    def last_turn(g):
        finish(FILTER_STEPS - 1, g)
        send_last(g)

    groups(last_turn)
    last = FILTER_STEPS
    unpack(lambda g, p, c, rows: fields[last, g, p, c, rows], plain)

    high, low = split(side_by_side(plain))
    gram = mul(high, high, SUBLANES)
    cross = mul(high, low, SUBLANES)
    half = gram.shape[0] // 2
    cross_re = cross[:half, :half] + cross[half:, half:]
    cross_im = cross[:half, half:] - cross[half:, :half]
    sum_begin(
        0,
        packed(
            gram[:half, :half] + gram[half:, half:] + (cross_re + cross_re.T),
            gram[:half, half:] - gram[half:, :half] + (cross_im - cross_im.T),
        ),
    )

    groups(lambda g: forward_pass(last, g))
    groups(finish_hops)
    unpack(lambda g, p, c, rows: packed_hops[g, p, c, rows], hops)
    hop_high, hop_low = split(side_by_side(hops))
    proj = mul(high, hop_high, SUBLANES)
    proj = proj + mul(high, hop_low, SUBLANES)
    proj = proj + mul(low, hop_high, SUBLANES)
    proj_re = proj[:half, :half] + proj[half:, half:]
    proj_im = proj[:half, half:] - proj[half:, :half]
    sum_begin(1, packed(proj_re + proj_re.T, proj_im - proj_im.T))
    sum_middle(0)
    sum_middle(1)
    sum_last(0)
    sum_last(1)
    sum_end(0)
    gram_sum = sum_of(summed, 0) / sites_all

    scale = jnp.sqrt(2.0 * jnp.sum(gram_sum * gram_sum, keepdims=True))
    eye = (
        lax.broadcasted_iota(jnp.int32, (half, 2 * half), 0)
        == lax.broadcasted_iota(jnp.int32, (half, 2 * half), 1)
    ).astype(f32)
    iterate = gram_sum / scale
    factor = 1.5 * eye - 0.5 * iterate
    iterate = product(split(iterate), whole_split(factor))
    result = factor

    def newton(step, carry):
        iterate, result = carry
        result_split = split(result)
        factor = 1.5 * eye - 0.5 * product(result_split, whole_split(iterate))
        right = whole_split(factor)
        return (product(split(iterate), right), product(result_split, right))

    iterate, result = lax.fori_loop(1, NS_STEPS - 1, newton, (iterate, result))
    result_split = split(result)
    factor = 1.5 * eye - 0.5 * product(result_split, whole_split(iterate))
    root_ref[...] = product(result_split, whole_split(factor)) / jnp.sqrt(scale)
    sum_end(1)
    early = pl.ds(0, FILTER_STEPS)
    for index, ref in enumerate((send_x, send_x, send_y, send_y, send_z, send_z, send_y)):
        await_bytes(ref.at[early], sent_sems.at[index])
    for j in range(2):
        for sem in (0, 2, 4):
            drain(j, sem)


def sum_of(summed, j):
    return unpacked(summed[j].reshape(128, 128))


def rotate_kernel(
    sites_all, plain, root_ref, summed, basis_ref, ritz_ref, turned, ritz_rows, sems
):
    root = root_ref[...]
    half = root.shape[0]
    right = whole_split(root)
    copies = []
    for c in range(3):
        left = jnp.concatenate([plain[p, c].reshape(-1, half) for p in range(2)], 1)
        out = product(split(left), right)
        for p in range(2):
            turned[p, c] = out[:, p * half : (p + 1) * half].reshape(turned.shape[2:])
            copy = pltpu.make_async_copy(turned.at[p, c], basis_ref.at[p, c], sems.at[p, c])
            copy.start()
            copies.append(copy)
    gram_sum = sum_of(summed, 0) / sites_all
    proj_sum = 6.0 * gram_sum + (-1.0 / HOP) * (sum_of(summed, 1) / sites_all)
    ritz = product(split(proj_sum), right)
    ritz = product(split(root), whole_split(ritz))
    for p in range(2):
        ritz_rows[p] = ritz[:, p * half : (p + 1) * half]
    copy = pltpu.make_async_copy(ritz_rows, ritz_ref, sems.at[0, 3])
    copy.start()
    copies.append(copy)
    for copy in copies:
        copy.wait()


def shards(vectors, links):
    brick = vectors.shape
    sites_all = float(
        vectors.shape[2]
        * lax.axis_size("gx")
        * vectors.shape[3]
        * lax.axis_size("gy")
        * vectors.shape[4]
        * lax.axis_size("gz")
    )
    vec = vectors.reshape(2, 3, 4, 64, 128)
    link = links.reshape(54, 4, 8, 8)
    steps = FILTER_STEPS
    face_x = (steps + 1, 4, 2, 3, 16, 128)
    face = (steps + 1, 4, 2, 3, 8, 128)
    vmem = lambda *shape: pltpu.VMEM(shape, f32)
    space = pl.BlockSpec(memory_space=pltpu.VMEM)
    far = pl.BlockSpec(memory_space=pltpu.HBM)
    field, root, sums = pl.pallas_call(
        lambda *refs: whole_kernel(sites_all, *refs),
        out_shape=(
            jax.ShapeDtypeStruct(vec.shape, f32),
            jax.ShapeDtypeStruct((128, 256), f32),
            jax.ShapeDtypeStruct((2, 16, 8, 128), f32),
        ),
        in_specs=[far, far],
        out_specs=(space, space, space),
        scratch_shapes=[
            vmem(*vec.shape),
            vmem(steps + 1, 4, 2, 3, 64, 128),
            vmem(4, 2, 3, 64, 128),
            vmem(54, 64, 128),
            vmem(18, 8, 128),
            vmem(18, 8, 128),
            vmem(*face_x),
            vmem(*face),
            vmem(*face),
            vmem(*face),
            vmem(*face),
            vmem(*face_x),
            vmem(*face),
            vmem(*face),
            vmem(*face_x),
            vmem(*face),
            vmem(*face),
            vmem(2, 16, 8, 128),
            vmem(2, 16, 8, 128),
            vmem(2, 16, 8, 128),
            vmem(*link.shape),
            pltpu.SemaphoreType.DMA((2,)),
            pltpu.SemaphoreType.DMA((2, steps + 1, 4)),
            pltpu.SemaphoreType.DMA((7,)),
            pltpu.SemaphoreType.DMA((2, 6)),
        ],
        compiler_params=pltpu.CompilerParams(
            collective_id=0, has_side_effects=True, vmem_limit_bytes=48 * 1024 * 1024
        ),
    )(
        pltpu.with_memory_space_constraint(vec, pltpu.HBM),
        pltpu.with_memory_space_constraint(link, pltpu.HBM),
    )
    basis, ritz = pl.pallas_call(
        lambda *refs: rotate_kernel(sites_all, *refs),
        out_shape=(
            jax.ShapeDtypeStruct(vec.shape, f32),
            jax.ShapeDtypeStruct((2, 128, 128), f32),
        ),
        in_specs=[space, space, space],
        out_specs=(far, far),
        scratch_shapes=[
            vmem(*vec.shape),
            vmem(2, 128, 128),
            pltpu.SemaphoreType.DMA((2, 4)),
        ],
        compiler_params=pltpu.CompilerParams(vmem_limit_bytes=8 * 1024 * 1024),
    )(field, root, sums)
    return (basis.reshape(brick), ritz)


def solution(mesh):
    return jax.shard_map(
        shards,
        mesh=mesh,
        in_specs=(
            P(None, None, "gx", "gy", "gz", None),
            P(None, None, None, None, "gx", "gy", "gz"),
        ),
        out_specs=(P(None, None, "gx", "gy", "gz", None), P()),
        check_vma=False,
    )
```
